32 devices in a mesh: ep: 8 (over z, x), tp: 4 (over y, core).
Axes of the slice: x: 2, y: 2, z: 4, core: 2. Of those that a mesh axis runs over, the one named last changes fastest.
Arguments:
- cache_pages: bfloat16 [512, 256, 576], P(('ep', 'tp')), may hold values from -6 to 6
- queries: bfloat16 [512, 128, 576], P(('ep', 'tp')), may hold values from -400 to 400
- lengths: int32 [512], replicated, may hold values from 2 to 256, as said below
- swap_slot: int32 [32], replicated, may hold values from 0 to 15
- swap_mask: int32 [1], replicated, may hold values from 1 to 7
- hidden: bfloat16 [512, 3584], P('ep'), may hold values from -6 to 6
- expert_ids: int32 [512, 8], P('ep'), may hold values from 0 to 23, all different within a row; in each aligned block of 64 rows (0 to 63, 64 to 127, ...) at most 42 rows name the same one
- gate_weights: float32 [512, 8], P('ep'), may hold values from 0.1 to 0.6
- w_gate: bfloat16 [24, 3584, 1024], P('ep', None, 'tp'), may hold values from -0.09375 to 0.09375
- w_up: bfloat16 [24, 3584, 1024], P('ep', None, 'tp'), may hold values from -0.09375 to 0.09375
- w_down: bfloat16 [24, 1024, 3584], P('ep', 'tp'), may hold values from -0.1875 to 0.1875
Outputs:
- attention_out: bfloat16 [512, 128, 512], P(('ep', 'tp'))
- moe_out: bfloat16 [512, 3584], P('ep', 'tp')
The draws below stay inside these ranges and needn't reach their ends.
Inputs may be any that keep to these rules, and one draw needn't show every extreme that they name: `lengths`: each request's cache holds at least 2 tokens; some request holds exactly 256. `expert_ids`: A row's 8 experts are distinct. Among the 64 rows of one ep rank no expert is named by more than 42 rows, a bound that some block reaches.
All inputs are finite; a program needn't handle non-finite values.
Results may differ from the reference program's by a relative error of at most 0.012.
Values may be sent and summed in bfloat16 or wider, within the bound.
No kernel may reach another device: no remote copies, remote signals or barrier semaphores. Data moves between devices by JAX's collectives and lax.ppermute only.
A program may use at most 128 MiB of HBM per device.

```python
import math
import jax
import jax.numpy as jnp
import numpy as np
from jax import lax

D = 3584
FF = 1024
HEADS = 128
LAT = 512
KV = 576
TOPK = 8
EXPERTS = 24
REQ_DEV = 64
REQ_LOCAL = 16
REQS = 512
CTX = 256
CAP = 42
N_EP = 8
N_TP = 4


def trade_slots(key):
    return jax.random.randint(jax.random.fold_in(key, 11), (REQS // REQ_LOCAL,), 0, REQ_LOCAL).astype(jnp.int32)


def full_cache(key):
    full_shape = (REQS, CTX, KV)
    return jax.random.truncated_normal(jax.random.fold_in(key, 21), -5.0, 5.0, full_shape, jnp.float32)


def draw_cache_pages(key, part):
    return full_cache(key).astype(jnp.bfloat16)


def draw_queries(key, part):
    full_shape = (REQS, HEADS, KV)
    base_vals = 2.0 * jax.random.truncated_normal(jax.random.fold_in(key, 31), -5.0, 5.0, full_shape, jnp.float32)
    return base_vals.astype(jnp.bfloat16)


def draw_lengths(key, part):
    group_count = REQS // REQ_LOCAL
    base_vals = jax.random.randint(jax.random.fold_in(key, 41), (REQS,), 0, CTX - 1)
    factor = jax.random.randint(jax.random.fold_in(key, 42), (group_count,), 1, 5)
    spread = jnp.repeat(factor, REQ_LOCAL)
    size_vals = 2 + base_vals * spread // 4
    longest = jax.random.randint(jax.random.fold_in(key, 43), (), 0, REQS)
    return jnp.where(jnp.arange(REQS) == longest, CTX, size_vals).astype(jnp.int32)


def draw_swap_slot(key, part):
    return trade_slots(key)


def block_levels(own_key, shape, split, low, largest):
    def one(axis_at, parts):
        steps = jax.random.uniform(jax.random.fold_in(jax.random.fold_in(own_key, 6), axis_at), (parts,), jnp.float32, low / len(split), largest / len(split))
        return jnp.repeat(jnp.exp(steps), shape[axis_at] // parts).reshape((-1,) + (1,) * (len(shape) - axis_at - 1))

    factor_of = one(*split[0])
    for cut in split[1:]:
        factor_of = factor_of * one(*cut)
    return factor_of


def routed_block(own_key, own, number, rows, count, top, reach, skew):
    order = jax.random.permutation(own_key, count)
    heavy_load, ordinary = shares(count, rows * top, reach, skew, True), shares(count, rows * top, reach, skew, False)
    places = jnp.arange(count)

    def named(tallies, rotation):
        used = int((tallies > 0).sum())
        fixed = max(1, used // 4)
        passed = fixed + (places - fixed + rotation * (used - fixed)) % max(1, count - fixed)
        return jnp.zeros((count,), jnp.int32).at[order[jnp.where(places < fixed, places, passed)]].set(jnp.asarray(tallies, jnp.int32))

    tallies = jnp.where(number % 4 == 0, named(heavy_load, number // 4), named(ordinary, number - number // 4 - 1))
    mixed = jax.random.permutation(jax.random.fold_in(own, 3), count)
    donor, taker = mixed[0:count // 2 * 2:2], mixed[1:count // 2 * 2:2]
    room = jnp.minimum(tallies[donor] - 1, reach - tallies[taker]) // 2
    room = jnp.where((donor == order[0]) | (taker == order[0]) | (tallies[taker] == 0), 0, jnp.maximum(room, 0))
    passed = jax.random.randint(jax.random.fold_in(own, 4), (count // 2,), 0, 1 << 20) % (room + 1)
    tallies = tallies.at[donor].add(-passed).at[taker].add(passed)
    members = jnp.searchsorted(jnp.cumsum(tallies), jnp.arange(rows * top), side="right").astype(jnp.int32)
    table = members.reshape(top, rows).T
    table = table[jax.random.permutation(jax.random.fold_in(own, 1), rows)]
    rotation = jax.random.randint(jax.random.fold_in(own, 2), (rows, 1), 0, top)
    return jnp.take_along_axis(table, (jnp.arange(top)[None, :] + rotation) % top, axis=1)


def shares(count, total, most, lean, full):
    weights = [(1 << 20) // math.isqrt(rank ** lean) + 1 for rank in range(1, count + 1)]
    largest = most if full else min(most, max(-(-total // count), total * weights[0] // sum(weights)))
    least = 1 if total - largest >= count - 1 else 0
    counts, rest = [largest] + [least] * (count - 1), total - largest - least * (count - 1)
    while rest > 0:
        candidates = [i for i in range(1, count) if counts[i] < largest] or [i for i in range(1, count) if counts[i] < most]
        whole, remaining = sum([weights[i] for i in candidates]), rest
        for i in candidates:
            extra = min(most - counts[i], max(1, remaining * weights[i] // whole), rest)
            counts[i] = counts[i] + extra
            rest = rest - extra
    return np.array(counts)


def gaussian(stream_key, shape, scale, bound, pieces=(), kind=jnp.bfloat16):
    drawn = scale * jax.random.normal(stream_key, shape, jnp.float32)
    if pieces:
        drawn = drawn * block_levels(stream_key, shape, pieces, -0.22, 0.18)
    return jnp.clip(drawn, -bound, bound).astype(kind)


def setup_inputs(seed: int = 0) -> dict:
    streams_of = jax.random.split(jax.random.key(seed), 12)
    cache_pages = draw_cache_pages(jax.random.fold_in(streams_of[11], 71), 0)
    queries = draw_queries(jax.random.fold_in(streams_of[11], 71), 0)
    lengths = draw_lengths(jax.random.fold_in(streams_of[11], 71), 0)
    swap_slot = draw_swap_slot(jax.random.fold_in(streams_of[11], 71), 0)
    swap_mask = jax.random.randint(streams_of[4], (1,), 1, N_EP).astype(jnp.int32)
    hidden = gaussian(streams_of[5], (REQS, D), 1.0, 6.0, ((0, 8),))
    expert_ids_keys = jax.random.split(jax.random.fold_in(streams_of[6], 1), REQS // REQ_DEV)
    expert_ids_turns = jax.random.permutation(jax.random.fold_in(streams_of[6], 3), REQS // REQ_DEV)
    expert_ids = jax.vmap(lambda own, number: routed_block(jax.random.fold_in(streams_of[6], 2), own, number, REQ_DEV, EXPERTS, TOPK, CAP, 2))(expert_ids_keys, expert_ids_turns).reshape((REQS, TOPK))
    gate_weights = jnp.clip(0.1 + 0.5 * jax.random.uniform(streams_of[7], (REQS, TOPK), jnp.float32) ** block_levels(streams_of[7], (REQS, TOPK), ((0, 8),), -0.2, 0.2), 0.1, 0.6)
    w_gate = gaussian(streams_of[8], (EXPERTS, D, FF), D ** -0.5, 0.09375, ((0, 8), (2, 4)))
    w_up = gaussian(streams_of[9], (EXPERTS, D, FF), D ** -0.5, 0.09375, ((0, 8), (2, 4)))
    w_down = gaussian(streams_of[10], (EXPERTS, FF, D), FF ** -0.5, 0.1875, ((0, 8), (1, 4)))
    return dict(cache_pages=cache_pages, queries=queries, lengths=lengths, swap_slot=swap_slot, swap_mask=swap_mask, hidden=hidden, expert_ids=expert_ids, gate_weights=gate_weights, w_gate=w_gate, w_up=w_up, w_down=w_down)


SCORE_SCALE = 192.0 ** -0.5
MASK_FLOOR = -1.0e30


def attend(query_row, page_rows, length):
    scores = jnp.dot(query_row, page_rows.T, preferred_element_type=jnp.float32) * SCORE_SCALE
    live_mask = jnp.arange(page_rows.shape[0], dtype=jnp.int32) < length
    scores = jnp.where(live_mask[None, :], scores, MASK_FLOOR)
    top_score = jnp.max(scores, axis=1, keepdims=True)
    weight = jnp.where(live_mask[None, :], jnp.exp(scores - top_score), 0.0)
    totals = jnp.sum(weight, axis=1, keepdims=True)
    weight_low = weight.astype(jnp.bfloat16)
    blended = jnp.dot(weight_low, page_rows[:, :LAT], preferred_element_type=jnp.float32)
    return (blended / totals).astype(jnp.bfloat16)


def reference(cache_pages, queries, lengths, swap_slot, swap_mask, hidden, expert_ids, gate_weights, w_gate, w_up, w_down):
    req_index = jnp.arange(REQS, dtype=jnp.int32)
    device = req_index // REQ_LOCAL
    slot_pos = req_index % REQ_LOCAL
    partner = (jnp.bitwise_xor(device // N_TP, swap_mask[0]) * N_TP + device % N_TP).astype(jnp.int32)
    is_moved = slot_pos == swap_slot[device]
    source = jnp.where(is_moved, partner * REQ_LOCAL + swap_slot[partner], req_index).astype(jnp.int32)

    def single(request):
        anchor = source[request]
        return attend(queries[request], cache_pages[anchor], lengths[anchor])

    attention_out = lax.map(single, req_index)

    pair_count = REQ_DEV * TOPK
    flat_ids = expert_ids.reshape(N_EP, pair_count).astype(jnp.int32)
    onehot = (flat_ids[:, :, None] == jnp.arange(EXPERTS, dtype=jnp.int32)[None, None, :]).astype(jnp.int32)
    pair_rank = jnp.sum(jnp.cumsum(onehot, axis=1) * onehot, axis=2) - 1
    slot_id = (jnp.arange(N_EP, dtype=jnp.int32)[:, None] * CAP + pair_rank).astype(jnp.int32)
    token_ids = (jnp.arange(N_EP, dtype=jnp.int32)[:, None] * REQ_DEV + jnp.arange(pair_count, dtype=jnp.int32)[None, :] // TOPK).astype(jnp.int32)
    slot_table = jnp.full((EXPERTS, N_EP * CAP), -1, jnp.int32).at[flat_ids.reshape(-1), slot_id.reshape(-1)].set(token_ids.reshape(-1))
    share_width = FF // N_TP

    def expert_block(expert):
        row_ids = slot_table[expert]
        inputs = jnp.where((row_ids >= 0)[:, None], hidden[jnp.maximum(row_ids, 0)], jnp.zeros((), jnp.bfloat16))
        gate_act = jnp.dot(inputs, w_gate[expert], preferred_element_type=jnp.float32)
        up_act = jnp.dot(inputs, w_up[expert], preferred_element_type=jnp.float32)
        inner_act = (jax.nn.silu(gate_act) * up_act).astype(jnp.bfloat16)
        down_rows = w_down[expert]
        totals = jnp.zeros((row_ids.shape[0], D), jnp.float32)
        for share_index in range(N_TP):
            lower = share_index * share_width
            share_out = jnp.dot(inner_act[:, lower:lower + share_width], down_rows[lower:lower + share_width], preferred_element_type=jnp.float32).astype(jnp.bfloat16)
            share_out = lax.optimization_barrier(share_out)
            totals = totals + share_out.astype(jnp.float32)
        return totals.astype(jnp.bfloat16)

    expert_out = lax.map(expert_block, jnp.arange(EXPERTS, dtype=jnp.int32))
    picked = expert_out[flat_ids, slot_id]
    weights = gate_weights.reshape(N_EP, pair_count).astype(jnp.float32)
    moe_rows = (picked.astype(jnp.float32) * weights[:, :, None]).reshape(N_EP, REQ_DEV, TOPK, D).sum(axis=2)
    return attention_out, moe_rows.reshape(REQS, D).astype(jnp.bfloat16)
```

```python
import functools

import jax
import jax.numpy as jnp
from jax import lax
from jax.experimental import pallas as pl
from jax.experimental.pallas import tpu as pltpu
from jax.sharding import PartitionSpec as P

LAT = 512
SCORE_SCALE = 192.0 ** (-0.5)
MASK_FLOOR = -1e30
ROWS = 256
MIB = 1 << 20


def flip(block, axis, apart):
    count = lax.axis_size(axis)
    return lax.ppermute(block, axis, [(i, i ^ apart) for i in range(count)])


def attend_body(query, page, length):
    scores = (
        lax.dot_general(query, page, (((1,), (1,)), ((), ())), preferred_element_type=jnp.float32)
        * SCORE_SCALE
    )
    live = lax.broadcasted_iota(jnp.int32, scores.shape, 1) < length
    scores = jnp.where(live, scores, MASK_FLOOR)
    top = jnp.max(scores, axis=1, keepdims=True)
    weight = jnp.where(live, jnp.exp(scores - top), 0.0)
    total = jnp.sum(weight, axis=1, keepdims=True)
    blended = jnp.dot(
        weight.astype(jnp.bfloat16), page[:, :LAT], preferred_element_type=jnp.float32
    )
    return (blended / total).astype(jnp.bfloat16)


def attend_kernel(lengths_ref, place_ref, query_ref, page_ref, out_ref):
    length = lengths_ref[place_ref[0] + pl.program_id(0)]
    out_ref[0] = attend_body(query_ref[0], page_ref[0], length)


def attend_all(lengths, place, queries, pages):
    count, heads, width = queries.shape
    slots = pages.shape[1]
    return pl.pallas_call(
        attend_kernel,
        out_shape=jax.ShapeDtypeStruct((count, heads, LAT), jnp.bfloat16),
        grid_spec=pltpu.PrefetchScalarGridSpec(
            num_scalar_prefetch=2,
            grid=(count,),
            in_specs=[
                pl.BlockSpec((1, heads, width), lambda i, *_: (i, 0, 0)),
                pl.BlockSpec((1, slots, width), lambda i, *_: (i, 0, 0)),
            ],
            out_specs=pl.BlockSpec((1, heads, LAT), lambda i, *_: (i, 0, 0)),
        ),
        compiler_params=pltpu.CompilerParams(vmem_limit_bytes=16 * MIB),
        cost_estimate=pl.CostEstimate(
            flops=2 * count * heads * slots * (width + LAT),
            bytes_accessed=2 * count * (heads * (width + LAT) + slots * width),
            transcendentals=count * heads * slots,
        ),
        name="attend_local",
    )(lengths, place, queries, pages)


def attend_traded_kernel(place_ref, query_ref, page_ref, old_ref, out_ref):
    out_ref[0] = attend_body(query_ref[0], page_ref[...], place_ref[1])


def attend_traded(place, queries, page, attended):
    _, heads, width = queries.shape
    slots = page.shape[0]
    return pl.pallas_call(
        attend_traded_kernel,
        out_shape=jax.ShapeDtypeStruct(attended.shape, attended.dtype),
        grid_spec=pltpu.PrefetchScalarGridSpec(
            num_scalar_prefetch=1,
            grid=(1,),
            in_specs=[
                pl.BlockSpec((1, heads, width), lambda i, s: (s[0], 0, 0)),
                pl.BlockSpec((slots, width), lambda i, s: (0, 0)),
                pl.BlockSpec(memory_space=pl.ANY),
            ],
            out_specs=pl.BlockSpec((1, heads, LAT), lambda i, s: (s[0], 0, 0)),
        ),
        input_output_aliases={3: 0},
        compiler_params=pltpu.CompilerParams(vmem_limit_bytes=16 * MIB),
        cost_estimate=pl.CostEstimate(
            flops=2 * heads * slots * (width + LAT),
            bytes_accessed=2 * (heads * (width + LAT) + slots * width),
            transcendentals=heads * slots,
        ),
        name="attend_traded",
    )(place, queries, page, attended)


def experts_kernel(
    ranks_ref,
    gates_ref,
    hidden_ref,
    pieces,
    w_gate_ref,
    w_up_ref,
    inner_ref,
    rows_ref,
    gate_buf,
    up_buf,
    row_sems,
    gate_sems,
    up_sems,
):
    blocks = len(pieces) + 1
    experts, _, units = w_gate_ref.shape
    block_rows = hidden_ref.shape[0]
    quarter = pieces[0][0].shape[1]
    ep_rank, tp_rank = ranks_ref[0], ranks_ref[1]
    copies = [pltpu.make_async_copy(hidden_ref, rows_ref.at[pl.ds(0, block_rows), :], row_sems.at[0, 0])]
    for block in range(1, blocks):
        for part, piece in enumerate(pieces[block - 1]):
            column = pl.multiple_of((tp_rank ^ part) * quarter, 128)
            copies.append(
                pltpu.make_async_copy(
                    piece,
                    rows_ref.at[pl.ds(block * block_rows, block_rows), pl.ds(column, quarter)],
                    row_sems.at[block, part],
                )
            )
    weight_copies = []
    for e in range(experts):
        weight_copies.append(
            (
                pltpu.make_async_copy(w_gate_ref.at[e], gate_buf.at[e], gate_sems.at[e]),
                pltpu.make_async_copy(w_up_ref.at[e], up_buf.at[e], up_sems.at[e]),
            )
        )
    for one in weight_copies[0]:
        one.start()
    for one in copies:
        one.start()
    for pair in weight_copies[1:]:
        for one in pair:
            one.start()
    for one in copies:
        one.wait()
    per = ROWS // block_rows
    for e in range(experts):
        for one in weight_copies[e]:
            one.wait()
        column = ep_rank * experts + e

        @pl.loop(0, blocks * block_rows // ROWS)
        def _(step):
            start = pl.multiple_of(step * ROWS, ROWS)
            rows = rows_ref[pl.ds(start, ROWS), :]
            gate = jnp.dot(rows, gate_buf[e], preferred_element_type=jnp.float32)
            up = jnp.dot(rows, up_buf[e], preferred_element_type=jnp.float32)
            table = jnp.concatenate(
                [gates_ref[ep_rank ^ (step * per + i)] for i in range(per)], axis=0
            )
            lane = lax.broadcasted_iota(jnp.int32, table.shape, 1)
            scale = jnp.sum(jnp.where(lane == column, table, 0.0), axis=1, keepdims=True)
            act = gate / (1.0 + jnp.exp(-gate)) * up * scale
            inner_ref[pl.ds(start, ROWS), e * units : (e + 1) * units] = act.astype(jnp.bfloat16)


def run_experts(ranks, gates, hidden, pieces, w_gate, w_up):
    blocks = len(pieces) + 1
    rows = blocks * hidden.shape[0]
    experts, width, units = w_gate.shape
    anywhere = pl.BlockSpec(memory_space=pl.ANY)
    return pl.pallas_call(
        experts_kernel,
        out_shape=jax.ShapeDtypeStruct((rows, experts * units), jnp.bfloat16),
        in_specs=[
            pl.BlockSpec(memory_space=pltpu.SMEM),
            pl.BlockSpec(memory_space=pltpu.VMEM),
            anywhere,
            jax.tree.map(lambda _: anywhere, pieces),
            anywhere,
            anywhere,
        ],
        out_specs=pl.BlockSpec(memory_space=pltpu.VMEM),
        scratch_shapes=[
            pltpu.VMEM((rows, width), jnp.bfloat16),
            pltpu.VMEM((experts, width, units), jnp.bfloat16),
            pltpu.VMEM((experts, width, units), jnp.bfloat16),
            pltpu.SemaphoreType.DMA((blocks, 4)),
            pltpu.SemaphoreType.DMA((experts,)),
            pltpu.SemaphoreType.DMA((experts,)),
        ],
        compiler_params=pltpu.CompilerParams(vmem_limit_bytes=48 * MIB),
        cost_estimate=pl.CostEstimate(
            flops=4 * rows * width * units * experts,
            bytes_accessed=4 * experts * width * units + 2 * rows * width,
            transcendentals=rows * units * experts,
        ),
        name="experts_inner",
    )(ranks, gates, hidden, pieces, w_gate, w_up)


def down_kernel(blocks, ranks_ref, inner_ref, w_ref, *refs):
    out_refs = refs[-blocks:] if blocks else refs[-1:]
    experts, units, _ = w_ref.shape
    total_rows = inner_ref.shape[0]
    count = len(out_refs)
    each = total_rows // count
    stride = ROWS if each < ROWS else each
    stride = min(stride, ROWS)
    for start in range(0, total_rows, stride):
        value = None
        for e in range(experts):
            term = jnp.dot(
                inner_ref[start : start + stride, e * units : (e + 1) * units],
                w_ref[e],
                preferred_element_type=jnp.float32,
            )
            value = term if value is None else value + term
        if len(refs) > count:
            value = value + refs[0][start : start + stride, :].astype(jnp.float32)
        value = value.astype(jnp.bfloat16)
        if count == 1:
            out_refs[0][start : start + stride, :] = value
        else:
            for i in range(stride // each):
                out_refs[start // each + i][...] = value[i * each : (i + 1) * each]


def run_down(ranks, inner, w_down, part, columns, add=None, blocks=0):
    rows, depth = inner.shape
    experts, units, _ = w_down.shape
    whole = lambda shape: pl.BlockSpec(shape, lambda i, s: (0, 0))
    extra = [] if add is None else [add]
    if blocks:
        out_shape = [jax.ShapeDtypeStruct((rows // blocks, columns), jnp.bfloat16)] * blocks
        out_specs = [whole((rows // blocks, columns))] * blocks
    else:
        out_shape = jax.ShapeDtypeStruct((rows, columns), jnp.bfloat16)
        out_specs = whole((rows, columns))
    return pl.pallas_call(
        functools.partial(down_kernel, blocks),
        out_shape=out_shape,
        grid_spec=pltpu.PrefetchScalarGridSpec(
            num_scalar_prefetch=1,
            grid=(1,),
            in_specs=[
                whole((rows, depth)),
                pl.BlockSpec((experts, units, columns), lambda i, s: (0, 0, s[1] ^ part)),
            ]
            + [whole((rows, columns)) for _ in extra],
            out_specs=out_specs,
        ),
        compiler_params=pltpu.CompilerParams(vmem_limit_bytes=48 * MIB),
        cost_estimate=pl.CostEstimate(
            flops=2 * rows * depth * columns,
            bytes_accessed=2 * (rows * depth + depth * columns + rows * columns * (1 + len(extra))),
            transcendentals=0,
        ),
        name="experts_down",
    )(ranks, inner, w_down, *extra)


def total_of(*terms):
    value = terms[0].astype(jnp.float32)
    for term in terms[1:]:
        value = value + term.astype(jnp.float32)
    return value.astype(jnp.bfloat16)


def local(
    cache_pages,
    queries,
    lengths,
    swap_slot,
    swap_mask,
    hidden,
    expert_ids,
    gate_weights,
    w_gate,
    w_up,
    w_down,
):
    local_count = cache_pages.shape[0]
    groups = lax.axis_size("tp")
    ep_size = lax.axis_size("ep")
    ep_rank = lax.axis_index("ep")
    tp_rank = lax.axis_index("tp")
    device = ep_rank * groups + tp_rank
    mask_value = swap_mask[0]
    partner = jnp.bitwise_xor(ep_rank, mask_value) * groups + tp_rank
    my_slot = swap_slot[device]
    far_length = lengths[partner * local_count + swap_slot[partner]]
    ranks = jnp.stack([ep_rank, tp_rank]).astype(jnp.int32)
    model_width = hidden.shape[1]
    columns = model_width // groups
    expert_local = w_gate.shape[0]
    experts_all = ep_size * expert_local

    chosen = expert_ids[:, :, None] == jnp.arange(experts_all, dtype=jnp.int32)[None, None, :]
    gates = jnp.sum(jnp.where(chosen, gate_weights[:, :, None], 0.0), axis=1)
    gates = lax.all_gather(gates, "ep", axis=0)

    def quarter(part):
        start = jnp.bitwise_xor(tp_rank, part) * columns
        return lax.dynamic_slice_in_dim(hidden, start, columns, 1)

    near = {0: quarter(0)}
    far = {0: quarter(2)}
    pairs = ep_size // 2
    for m in range(1, pairs):
        near[2 * m] = flip(near[0], "ep", 2 * m)
    near[1] = flip(near[0], "ep", 1)
    far[1] = flip(far[0], "ep", 1)
    for m in range(1, pairs):
        far[2 * m] = flip(near[2 * m], "tp", 2)
        near[2 * m + 1] = flip(near[2 * m], "ep", 1)
        if m < pairs - 1:
            far[2 * m + 1] = flip(near[2 * m + 1], "tp", 2)
        else:
            far[2 * m + 1] = flip(far[2 * m], "ep", 1)
    pieces = []
    for k in range(1, ep_size):
        pieces.append((near[k], flip(near[k], "tp", 1), far[k], flip(far[k], "tp", 1)))

    place = jnp.stack([device * local_count]).astype(jnp.int32)
    attended = attend_all(lengths, place, queries, cache_pages)
    page = lax.dynamic_index_in_dim(cache_pages, my_slot, 0, keepdims=False)
    page, _ = lax.optimization_barrier((page, near[2 * pairs - 2]))
    for level in reversed(range(ep_size.bit_length() - 1)):
        swapped = flip(page, "ep", 1 << level)
        bit = jnp.bitwise_and(jnp.right_shift(mask_value, level), 1) == 1
        page = jnp.where(bit, swapped, page)
    traded = jnp.stack([my_slot, far_length]).astype(jnp.int32)
    attended = attend_traded(traded, queries, page, attended)

    inner = run_experts(ranks, gates, hidden, pieces, w_gate, w_up)
    down = functools.partial(run_down, ranks, inner, w_down, columns=columns)
    cross = flip(down(part=3), "tp", 1)
    side = flip(down(part=1), "tp", 1)
    sent = down(part=2, add=cross, blocks=ep_size)
    kept = down(part=0, add=side, blocks=ep_size)

    whole = {}
    for m in [*range(1, pairs), 0]:
        even, odd = 2 * m, 2 * m + 1
        if m == 2:
            here = flip(kept[odd], "ep", 1)
            there = total_of(sent[even], flip(sent[odd], "ep", 1))
            whole[m] = total_of(kept[even], here, flip(there, "tp", 2))
        else:
            over = total_of(kept[odd], flip(sent[odd], "tp", 2))
            whole[m] = total_of(kept[even], flip(sent[even], "tp", 2), flip(over, "ep", 1))
    moe_out = total_of(whole[0], *[flip(whole[m], "ep", 2 * m) for m in range(1, pairs)])
    return attended, moe_out


def solution(mesh):
    in_specs = (
        P(("ep", "tp"), None, None),
        P(("ep", "tp"), None, None),
        P(),
        P(),
        P(),
        P("ep", None),
        P("ep", None),
        P("ep", None),
        P("ep", None, "tp"),
        P("ep", None, "tp"),
        P("ep", "tp", None),
    )
    out_specs = (P(("ep", "tp"), None, None), P("ep", "tp"))
    return jax.shard_map(local, mesh=mesh, in_specs=in_specs, out_specs=out_specs, check_vma=False)
```

```python
import functools
import math

import jax
import jax.numpy as jnp
from jax import lax
from jax.experimental import pallas as pl
from jax.experimental.pallas import tpu as pltpu
from jax.sharding import PartitionSpec as P

LAT = 512
SCORE_SCALE = 192.0 ** (-0.5)
MASK_FLOOR = -1e30
ROWS = 256
MIB = 1 << 20


def flip(block, axis, apart):
    count = lax.axis_size(axis)
    return lax.ppermute(block, axis, [(i, i ^ apart) for i in range(count)])


def attend_body(query, page, length):
    scores = (
        lax.dot_general(query, page, (((0,), (0,)), ((), ())), preferred_element_type=jnp.float32)
        * SCORE_SCALE
    )
    live = lax.broadcasted_iota(jnp.int32, scores.shape, 1) < length
    scores = jnp.where(live, scores, MASK_FLOOR)
    top = jnp.max(scores, axis=1, keepdims=True)
    weight = jnp.where(live, jnp.exp(scores - top), 0.0)
    total = jnp.sum(weight, axis=1, keepdims=True)
    blended = lax.dot_general(
        weight.astype(jnp.bfloat16),
        page[:LAT],
        (((1,), (1,)), ((), ())),
        preferred_element_type=jnp.float32,
    )
    return (blended / total).astype(jnp.bfloat16)


def attend_kernel(each, lengths_ref, place_ref, query_ref, page_ref, out_ref):
    first = place_ref[0] + pl.program_id(0) * each
    for i in range(each):
        out_ref[i] = attend_body(query_ref[i], page_ref[i], lengths_ref[first + i])


def attend_all(lengths, place, queries, pages):
    count, width, heads = queries.shape
    slots = pages.shape[2]
    each = math.gcd(count, 4)
    return pl.pallas_call(
        functools.partial(attend_kernel, each),
        out_shape=jax.ShapeDtypeStruct((count, heads, LAT), jnp.bfloat16),
        grid_spec=pltpu.PrefetchScalarGridSpec(
            num_scalar_prefetch=2,
            grid=(count // each,),
            in_specs=[
                pl.BlockSpec((each, width, heads), lambda i, *_: (i, 0, 0)),
                pl.BlockSpec((each, width, slots), lambda i, *_: (i, 0, 0)),
            ],
            out_specs=pl.BlockSpec((each, heads, LAT), lambda i, *_: (i, 0, 0)),
        ),
        compiler_params=pltpu.CompilerParams(vmem_limit_bytes=16 * MIB),
        cost_estimate=pl.CostEstimate(
            flops=2 * count * heads * slots * (width + LAT),
            bytes_accessed=2 * count * (heads * (width + LAT) + slots * width),
            transcendentals=count * heads * slots,
        ),
        name="attend_local",
    )(lengths, place, queries, pages)


def attend_traded_kernel(place_ref, query_ref, page_ref, old_ref, out_ref):
    out_ref[0] = attend_body(query_ref[0], page_ref[...], place_ref[1])


def attend_traded(place, queries, page, attended):
    _, width, heads = queries.shape
    slots = page.shape[1]
    return pl.pallas_call(
        attend_traded_kernel,
        out_shape=jax.ShapeDtypeStruct(attended.shape, attended.dtype),
        grid_spec=pltpu.PrefetchScalarGridSpec(
            num_scalar_prefetch=1,
            grid=(1,),
            in_specs=[
                pl.BlockSpec((1, width, heads), lambda i, s: (s[0], 0, 0)),
                pl.BlockSpec((width, slots), lambda i, s: (0, 0)),
                pl.BlockSpec(memory_space=pl.ANY),
            ],
            out_specs=pl.BlockSpec((1, heads, LAT), lambda i, s: (s[0], 0, 0)),
        ),
        input_output_aliases={3: 0},
        compiler_params=pltpu.CompilerParams(vmem_limit_bytes=16 * MIB),
        cost_estimate=pl.CostEstimate(
            flops=2 * heads * slots * (width + LAT),
            bytes_accessed=2 * (heads * (width + LAT) + slots * width),
            transcendentals=heads * slots,
        ),
        name="attend_traded",
    )(place, queries, page, attended)


def experts_kernel(
    ranks_ref,
    gates,
    hidden_ref,
    pieces,
    w_gate_ref,
    w_up_ref,
    w_down_ref,
    cross_ref,
    side_ref,
    sent,
    kept,
    rows_ref,
    gate_buf,
    up_buf,
    down_buf,
    inner_ref,
    table_ref,
    row_sems,
    weight_sems,
):
    blocks = len(pieces) + 1
    experts, _, units = w_gate_ref.shape
    block_rows = hidden_ref.shape[0]
    quarter = pieces[0][0].shape[1]
    total_rows = blocks * block_rows
    ep_rank, tp_rank = ranks_ref[0], ranks_ref[1]
    copies = [pltpu.make_async_copy(hidden_ref, rows_ref.at[pl.ds(0, block_rows), :], row_sems.at[0, 0])]
    for block in range(1, blocks):
        for part, piece in enumerate(pieces[block - 1]):
            column = pl.multiple_of((tp_rank ^ part) * quarter, 128)
            copies.append(
                pltpu.make_async_copy(
                    piece,
                    rows_ref.at[pl.ds(block * block_rows, block_rows), pl.ds(column, quarter)],
                    row_sems.at[block, part],
                )
            )
    ups, downs = [], []
    for e in range(experts):
        ups.append(
            (
                pltpu.make_async_copy(w_gate_ref.at[e], gate_buf.at[e], weight_sems.at[e, 0]),
                pltpu.make_async_copy(w_up_ref.at[e], up_buf.at[e], weight_sems.at[e, 1]),
            )
        )
        downs.append(
            pltpu.make_async_copy(
                w_down_ref.at[e], down_buf.at[pl.ds(e * units, units), :], weight_sems.at[e, 2]
            )
        )
    for one in ups[0]:
        one.start()
    for one in copies:
        one.start()
    for pair in ups[1:]:
        for one in pair:
            one.start()
    for one in downs:
        one.start()
    lane = lax.broadcasted_iota(jnp.int32, (block_rows, gates[0].shape[2]), 1)
    for pair, gate_ref in enumerate(gates):
        for i in range(2):
            start = (2 * pair + i) * block_rows
            for e in range(experts):
                mine = jnp.where(lane == ep_rank * experts + e, gate_ref[i], 0.0)
                table_ref[start : start + block_rows, e : e + 1] = jnp.sum(
                    mine, axis=1, keepdims=True
                )
    for one in copies:
        one.wait()
    for e in range(experts):
        for one in ups[e]:
            one.wait()

        @pl.loop(0, total_rows // ROWS)
        def _(step):
            start = pl.multiple_of(step * ROWS, ROWS)
            rows = rows_ref[pl.ds(start, ROWS), :]
            gate = jnp.dot(rows, gate_buf[e], preferred_element_type=jnp.float32)
            up = jnp.dot(rows, up_buf[e], preferred_element_type=jnp.float32)
            scale = table_ref[pl.ds(start, ROWS), e : e + 1]
            act = gate / (1.0 + jnp.exp(-gate)) * up * scale
            inner_ref[pl.ds(start, ROWS), e * units : (e + 1) * units] = act.astype(jnp.bfloat16)

    for one in downs:
        one.wait()
    for part, out in ((3, cross_ref), (1, side_ref), (2, sent), (0, kept)):
        column = pl.multiple_of((tp_rank ^ part) * quarter, 128)
        for start in range(0, total_rows, ROWS):
            value = jnp.dot(
                inner_ref[start : start + ROWS, :],
                down_buf[:, pl.ds(column, quarter)],
                preferred_element_type=jnp.float32,
            ).astype(jnp.bfloat16)
            if isinstance(out, (list, tuple)):
                for i in range(ROWS // block_rows):
                    out[start // block_rows + i][...] = value[i * block_rows : (i + 1) * block_rows]
            else:
                out[start : start + ROWS, :] = value


def run_experts(ranks, gates, hidden, pieces, w_gate, w_up, w_down):
    blocks = len(pieces) + 1
    block_rows, width = hidden.shape
    rows = blocks * block_rows
    experts, _, units = w_gate.shape
    quarter = pieces[0][0].shape[1]
    anywhere = pl.BlockSpec(memory_space=pl.ANY)
    vmem = pl.BlockSpec(memory_space=pltpu.VMEM)
    whole = jax.ShapeDtypeStruct((rows, quarter), jnp.bfloat16)
    block = [jax.ShapeDtypeStruct((block_rows, quarter), jnp.bfloat16)] * blocks
    need = 2 * (rows * width + 3 * experts * width * units + 5 * rows * quarter) + rows * 512
    return pl.pallas_call(
        experts_kernel,
        out_shape=(whole, whole, block, block),
        in_specs=[
            pl.BlockSpec(memory_space=pltpu.SMEM),
            jax.tree.map(lambda _: vmem, gates),
            anywhere,
            jax.tree.map(lambda _: anywhere, pieces),
            anywhere,
            anywhere,
            anywhere,
        ],
        out_specs=(vmem, vmem, [vmem] * blocks, [vmem] * blocks),
        scratch_shapes=[
            pltpu.VMEM((rows, width), jnp.bfloat16),
            pltpu.VMEM((experts, width, units), jnp.bfloat16),
            pltpu.VMEM((experts, width, units), jnp.bfloat16),
            pltpu.VMEM((experts * units, width), jnp.bfloat16),
            pltpu.VMEM((rows, experts * units), jnp.bfloat16),
            pltpu.VMEM((rows, 128), jnp.float32),
            pltpu.SemaphoreType.DMA((blocks, 4)),
            pltpu.SemaphoreType.DMA((experts, 3)),
        ],
        compiler_params=pltpu.CompilerParams(vmem_limit_bytes=need + 8 * MIB),
        cost_estimate=pl.CostEstimate(
            flops=6 * rows * width * units * experts,
            bytes_accessed=6 * experts * width * units + 4 * rows * width,
            transcendentals=rows * units * experts,
        ),
        name="experts",
    )(ranks, gates, hidden, pieces, w_gate, w_up, w_down)


def total_of(*terms):
    value = terms[0].astype(jnp.float32)
    for term in terms[1:]:
        value = value + term.astype(jnp.float32)
    return value.astype(jnp.bfloat16)


def local(
    cache_pages,
    queries,
    lengths,
    swap_slot,
    swap_mask,
    hidden,
    expert_ids,
    gate_weights,
    w_gate,
    w_up,
    w_down,
):
    local_count = cache_pages.shape[0]
    groups = lax.axis_size("tp")
    ep_size = lax.axis_size("ep")
    ep_rank = lax.axis_index("ep")
    tp_rank = lax.axis_index("tp")
    device = ep_rank * groups + tp_rank
    mask_value = swap_mask[0]
    partner = jnp.bitwise_xor(ep_rank, mask_value) * groups + tp_rank
    my_slot = swap_slot[device]
    far_length = lengths[partner * local_count + swap_slot[partner]]
    ranks = jnp.stack([ep_rank, tp_rank]).astype(jnp.int32)
    model_width = hidden.shape[1]
    columns = model_width // groups
    expert_local = w_gate.shape[0]
    experts_all = ep_size * expert_local

    chosen = expert_ids[:, :, None] == jnp.arange(experts_all, dtype=jnp.int32)[None, None, :]
    gates = jnp.sum(jnp.where(chosen, gate_weights[:, :, None], 0.0), axis=1)
    gates = jnp.stack([gates, flip(gates, "ep", 1)])
    gates = [gates] + [flip(gates, "ep", 2 * m) for m in range(1, ep_size // 2)]

    def quarter(part):
        start = jnp.bitwise_xor(tp_rank, part) * columns
        return lax.dynamic_slice_in_dim(hidden, start, columns, 1)

    near = {0: quarter(0)}
    far = {0: quarter(2)}
    pairs = ep_size // 2
    for m in range(1, pairs):
        near[2 * m] = flip(near[0], "ep", 2 * m)
    near[1] = flip(near[0], "ep", 1)
    far[1] = flip(far[0], "ep", 1)
    for m in range(1, pairs):
        far[2 * m] = flip(near[2 * m], "tp", 2)
        near[2 * m + 1] = flip(near[2 * m], "ep", 1)
        if m < pairs - 1:
            far[2 * m + 1] = flip(near[2 * m + 1], "tp", 2)
        else:
            far[2 * m + 1] = flip(far[2 * m], "ep", 1)
    pieces = []
    for k in range(1, ep_size):
        pieces.append((near[k], flip(near[k], "tp", 1), far[k], flip(far[k], "tp", 1)))

    cache_pages = jnp.swapaxes(cache_pages, 1, 2)
    queries = jnp.swapaxes(queries, 1, 2)
    place = jnp.stack([device * local_count]).astype(jnp.int32)
    attended = attend_all(lengths, place, queries, cache_pages)
    levels = ep_size.bit_length() - 1

    def page_hop(page, level):
        swapped = flip(page, "ep", 1 << level)
        bit = jnp.bitwise_and(jnp.right_shift(mask_value, level), 1) == 1
        return jnp.where(bit, swapped, page)

    page = lax.dynamic_index_in_dim(cache_pages, my_slot, 0, keepdims=False)
    page = page_hop(page, 0)
    page, near[ep_size - 2] = lax.optimization_barrier((page, near[ep_size - 2]))
    for level in range(levels - 1, 1, -1):
        page = page_hop(page, level)
    ranks, attended, page = lax.optimization_barrier((ranks, attended, page))
    if levels > 1:
        page = page_hop(page, 1)
    traded = jnp.stack([my_slot, far_length]).astype(jnp.int32)
    attended = attend_traded(traded, queries, page, attended)

    cross, side, sent, kept = run_experts(ranks, gates, hidden, pieces, w_gate, w_up, w_down)
    cross = flip(cross, "tp", 1)
    side = flip(side, "tp", 1)
    cross, attended = lax.optimization_barrier((cross, attended))
    rows = hidden.shape[0]

    def block_of(array, k):
        return lax.slice_in_dim(array, k * rows, (k + 1) * rows, axis=0)

    sent = [total_of(one, block_of(cross, k)) for k, one in enumerate(sent)]
    kept = [total_of(one, block_of(side, k)) for k, one in enumerate(kept)]

    whole = {}
    for m in [*range(1, pairs), 0]:
        even, odd = 2 * m, 2 * m + 1
        if m == 2:
            here = flip(kept[odd], "ep", 1)
            there = total_of(sent[even], flip(sent[odd], "ep", 1))
            whole[m] = total_of(kept[even], here, flip(there, "tp", 2))
        else:
            over = total_of(kept[odd], flip(sent[odd], "tp", 2))
            whole[m] = total_of(kept[even], flip(sent[even], "tp", 2), flip(over, "ep", 1))
    moe_out = total_of(whole[0], *[flip(whole[m], "ep", 2 * m) for m in range(1, pairs)])
    return attended, moe_out


def solution(mesh):
    in_specs = (
        P(("ep", "tp"), None, None),
        P(("ep", "tp"), None, None),
        P(),
        P(),
        P(),
        P("ep", None),
        P("ep", None),
        P("ep", None),
        P("ep", None, "tp"),
        P("ep", None, "tp"),
        P("ep", "tp", None),
    )
    out_specs = (P(("ep", "tp"), None, None), P("ep", "tp"))
    return jax.shard_map(local, mesh=mesh, in_specs=in_specs, out_specs=out_specs, check_vma=False)
```

```python
import functools
import math

import jax
import jax.numpy as jnp
from jax import lax
from jax.experimental import pallas as pl
from jax.experimental.pallas import tpu as pltpu
from jax.sharding import PartitionSpec as P

LAT = 512
SCORE_SCALE = 192.0 ** (-0.5)
MASK_FLOOR = -1e30
ROWS = 256
MIB = 1 << 20


def flip(block, axis, apart):
    count = lax.axis_size(axis)
    return lax.ppermute(block, axis, [(i, i ^ apart) for i in range(count)])


def attend_body(query, page, length):
    scores = (
        lax.dot_general(query, page, (((0,), (0,)), ((), ())), preferred_element_type=jnp.float32)
        * SCORE_SCALE
    )
    live = lax.broadcasted_iota(jnp.int32, scores.shape, 1) < length
    scores = jnp.where(live, scores, MASK_FLOOR)
    top = jnp.max(scores, axis=1, keepdims=True)
    weight = jnp.where(live, jnp.exp(scores - top), 0.0)
    total = jnp.sum(weight, axis=1, keepdims=True)
    blended = lax.dot_general(
        weight.astype(jnp.bfloat16),
        page[:LAT],
        (((1,), (1,)), ((), ())),
        preferred_element_type=jnp.float32,
    )
    return (blended / total).astype(jnp.bfloat16)


def attend_kernel(each, lengths_ref, place_ref, query_ref, page_ref, out_ref):
    first = place_ref[0] + pl.program_id(0) * each
    for i in range(each):
        out_ref[i] = attend_body(query_ref[i], page_ref[i], lengths_ref[first + i])


def attend_all(lengths, place, queries, pages):
    count, width, heads = queries.shape
    slots = pages.shape[2]
    each = math.gcd(count, 4)
    return pl.pallas_call(
        functools.partial(attend_kernel, each),
        out_shape=jax.ShapeDtypeStruct((count, heads, LAT), jnp.bfloat16),
        grid_spec=pltpu.PrefetchScalarGridSpec(
            num_scalar_prefetch=2,
            grid=(count // each,),
            in_specs=[
                pl.BlockSpec((each, width, heads), lambda i, *_: (i, 0, 0)),
                pl.BlockSpec((each, width, slots), lambda i, *_: (i, 0, 0)),
            ],
            out_specs=pl.BlockSpec((each, heads, LAT), lambda i, *_: (i, 0, 0)),
        ),
        compiler_params=pltpu.CompilerParams(vmem_limit_bytes=16 * MIB),
        cost_estimate=pl.CostEstimate(
            flops=2 * count * heads * slots * (width + LAT),
            bytes_accessed=2 * count * (heads * (width + LAT) + slots * width),
            transcendentals=count * heads * slots,
        ),
        name="attend_local",
    )(lengths, place, queries, pages)


def attend_traded_kernel(place_ref, query_ref, page_ref, old_ref, out_ref):
    out_ref[0] = attend_body(query_ref[0], page_ref[...], place_ref[1])


def attend_traded(place, queries, page, attended):
    _, width, heads = queries.shape
    slots = page.shape[1]
    return pl.pallas_call(
        attend_traded_kernel,
        out_shape=jax.ShapeDtypeStruct(attended.shape, attended.dtype),
        grid_spec=pltpu.PrefetchScalarGridSpec(
            num_scalar_prefetch=1,
            grid=(1,),
            in_specs=[
                pl.BlockSpec((1, width, heads), lambda i, s: (s[0], 0, 0)),
                pl.BlockSpec((width, slots), lambda i, s: (0, 0)),
                pl.BlockSpec(memory_space=pl.ANY),
            ],
            out_specs=pl.BlockSpec((1, heads, LAT), lambda i, s: (s[0], 0, 0)),
        ),
        input_output_aliases={3: 0},
        compiler_params=pltpu.CompilerParams(vmem_limit_bytes=16 * MIB),
        cost_estimate=pl.CostEstimate(
            flops=2 * heads * slots * (width + LAT),
            bytes_accessed=2 * (heads * (width + LAT) + slots * width),
            transcendentals=heads * slots,
        ),
        name="attend_traded",
    )(place, queries, page, attended)


def experts_kernel(
    order,
    ranks_ref,
    gates,
    hidden_ref,
    pieces,
    w_gate_ref,
    w_up_ref,
    w_down_ref,
    cross_ref,
    side_ref,
    sent_ref,
    kept_ref,
    rows_ref,
    gate_buf,
    up_buf,
    down_buf,
    inner_ref,
    table_ref,
    row_sems,
    up_sems,
    down_sems,
):
    experts, _, units = w_gate_ref.shape
    block_rows, width = hidden_ref.shape
    total_rows = rows_ref.shape[0]
    quarter = kept_ref.shape[1]
    ep_rank, tp_rank = ranks_ref[0], ranks_ref[1]

    def columns_of(part):
        return pl.ds(pl.multiple_of((tp_rank ^ part) * quarter, 128), quarter)

    copies = [(hidden_ref, rows_ref.at[pl.ds(0, block_rows), :])]
    for start, parts, piece in pieces:
        rows = pl.ds(start * block_rows, piece.shape[0])
        for i, part in enumerate(parts):
            copies.append(
                (piece.at[:, pl.ds(i * quarter, quarter)], rows_ref.at[rows, columns_of(part)])
            )
    copies = [
        pltpu.make_async_copy(source, target, row_sems.at[i])
        for i, (source, target) in enumerate(copies)
    ]

    def up_copies(e):
        slot = e % 2
        return (
            pltpu.make_async_copy(w_gate_ref.at[e], gate_buf.at[slot], up_sems.at[slot, 0]),
            pltpu.make_async_copy(w_up_ref.at[e], up_buf.at[slot], up_sems.at[slot, 1]),
        )

    parts = (3, 1, 2, 0)
    downs = [
        pltpu.make_async_copy(
            w_down_ref.at[e, :, columns_of(part)],
            down_buf.at[i, pl.ds(e * units, units), :],
            down_sems.at[i, e],
        )
        for i, part in enumerate(parts)
        for e in range(experts)
    ]
    for one in up_copies(0):
        one.start()
    for one in copies:
        one.start()
    for e in range(1, min(2, experts)):
        for one in up_copies(e):
            one.start()
    for one in downs:
        one.start()
    lane = lax.broadcasted_iota(jnp.int32, (block_rows, gates[0].shape[2]), 1)
    for position, block in enumerate(order):
        start = position * block_rows
        for e in range(experts):
            mine = jnp.where(lane == ep_rank * experts + e, gates[block // 2][block % 2], 0.0)
            table_ref[start : start + block_rows, e : e + 1] = jnp.sum(mine, axis=1, keepdims=True)
    for one in copies:
        one.wait()
    for e in range(experts):
        slot = e % 2
        for one in up_copies(e):
            one.wait()

        @pl.loop(0, total_rows // ROWS)
        def _(step):
            start = pl.multiple_of(step * ROWS, ROWS)
            rows = rows_ref[pl.ds(start, ROWS), :]
            gate = jnp.dot(rows, gate_buf[slot], preferred_element_type=jnp.float32)
            up = jnp.dot(rows, up_buf[slot], preferred_element_type=jnp.float32)
            scale = table_ref[pl.ds(start, ROWS), e : e + 1]
            act = gate / (1.0 + jnp.exp(-gate)) * up * scale
            inner_ref[pl.ds(start, ROWS), e * units : (e + 1) * units] = act.astype(jnp.bfloat16)

        if e + 2 < experts:
            for one in up_copies(e + 2):
                one.start()

    for one in downs:
        one.wait()
    for i, out_ref in enumerate((cross_ref, side_ref, sent_ref, kept_ref)):

        @pl.loop(0, total_rows // ROWS)
        def _(step):
            rows = pl.ds(pl.multiple_of(step * ROWS, ROWS), ROWS)
            out_ref[rows, :] = jnp.dot(
                inner_ref[rows, :], down_buf[i], preferred_element_type=jnp.float32
            ).astype(jnp.bfloat16)


def run_experts(order, ranks, gates, hidden, pieces, w_gate, w_up, w_down, columns):
    block_rows, width = hidden.shape
    rows = len(order) * block_rows
    experts, _, units = w_gate.shape
    anywhere = pl.BlockSpec(memory_space=pl.ANY)
    vmem = pl.BlockSpec(memory_space=pltpu.VMEM)
    arrays = [piece for _, _, piece in pieces]
    count = 1 + sum(len(parts) for _, parts, _ in pieces)

    def kernel(ranks_ref, gates, hidden_ref, array_refs, *refs):
        named = [(start, parts, ref) for (start, parts, _), ref in zip(pieces, array_refs)]
        experts_kernel(order, ranks_ref, gates, hidden_ref, named, *refs)

    need = 2 * (rows * width + 4 * width * units + experts * units * (width + rows))
    need += 8 * rows * columns + 512 * rows
    return pl.pallas_call(
        kernel,
        out_shape=[jax.ShapeDtypeStruct((rows, columns), jnp.bfloat16)] * 4,
        in_specs=[
            pl.BlockSpec(memory_space=pltpu.SMEM),
            [vmem] * len(gates),
            anywhere,
            [anywhere] * len(arrays),
            anywhere,
            anywhere,
            anywhere,
        ],
        out_specs=[vmem] * 4,
        scratch_shapes=[
            pltpu.VMEM((rows, width), jnp.bfloat16),
            pltpu.VMEM((2, width, units), jnp.bfloat16),
            pltpu.VMEM((2, width, units), jnp.bfloat16),
            pltpu.VMEM((4, experts * units, columns), jnp.bfloat16),
            pltpu.VMEM((rows, experts * units), jnp.bfloat16),
            pltpu.VMEM((rows, 128), jnp.float32),
            pltpu.SemaphoreType.DMA((count,)),
            pltpu.SemaphoreType.DMA((2, 2)),
            pltpu.SemaphoreType.DMA((4, experts)),
        ],
        compiler_params=pltpu.CompilerParams(vmem_limit_bytes=need + 3 * MIB),
        cost_estimate=pl.CostEstimate(
            flops=6 * rows * width * units * experts,
            bytes_accessed=6 * experts * width * units + 4 * rows * width,
            transcendentals=rows * units * experts,
        ),
        name="experts",
    )(ranks, gates, hidden, arrays, w_gate, w_up, w_down)


def total_of(*terms):
    value = terms[0].astype(jnp.float32)
    for term in terms[1:]:
        value = value + term.astype(jnp.float32)
    return value.astype(jnp.bfloat16)


def local(
    cache_pages,
    queries,
    lengths,
    swap_slot,
    swap_mask,
    hidden,
    expert_ids,
    gate_weights,
    w_gate,
    w_up,
    w_down,
):
    local_count = cache_pages.shape[0]
    groups = lax.axis_size("tp")
    ep_size = lax.axis_size("ep")
    ep_rank = lax.axis_index("ep")
    tp_rank = lax.axis_index("tp")
    device = ep_rank * groups + tp_rank
    mask_value = swap_mask[0]
    partner = jnp.bitwise_xor(ep_rank, mask_value) * groups + tp_rank
    my_slot = swap_slot[device]
    far_length = lengths[partner * local_count + swap_slot[partner]]
    ranks = jnp.stack([ep_rank, tp_rank]).astype(jnp.int32)
    model_width = hidden.shape[1]
    columns = model_width // groups
    expert_local = w_gate.shape[0]
    experts_all = ep_size * expert_local

    rows = hidden.shape[0]
    pairs = ep_size // 2
    late = list(range(2, pairs))
    half = len(late) // 2
    order = [0, 1, 2, 3] + [2 * m for m in late] + [2 * m + 1 for m in late]
    evens, odds = 4, 4 + len(late)

    def quarter(part):
        start = jnp.bitwise_xor(tp_rank, part) * columns
        return lax.dynamic_slice_in_dim(hidden, start, columns, 1)

    def cut(array, start, count):
        return lax.slice_in_dim(array, start * rows, (start + count) * rows, axis=0)

    own = quarter(0)
    near_late = jnp.concatenate([flip(own, "ep", 2 * m) for m in late], axis=0)
    near_2 = flip(own, "ep", 2)
    both_1 = flip(jnp.concatenate([own, quarter(2)], axis=1), "ep", 1)

    expert_ids, gate_weights, both_1 = lax.optimization_barrier((expert_ids, gate_weights, both_1))
    chosen = expert_ids[:, :, None] == jnp.arange(experts_all, dtype=jnp.int32)[None, None, :]
    gates = jnp.sum(jnp.where(chosen, gate_weights[:, :, None], 0.0), axis=1)
    gates = jnp.stack([gates, flip(gates, "ep", 1)])
    gates = [gates] + [flip(gates, "ep", 2 * m) for m in range(1, pairs)]

    far_2 = flip(near_2, "tp", 2)
    near_3 = flip(near_2, "ep", 1)
    far_3 = flip(near_3, "tp", 2)

    cache_pages = jnp.swapaxes(cache_pages, 1, 2)
    queries = jnp.swapaxes(queries, 1, 2)
    place = jnp.stack([device * local_count]).astype(jnp.int32)
    attended = attend_all(lengths, place, queries, cache_pages)
    near_late, attended = lax.optimization_barrier((near_late, attended))

    far_late = flip(near_late, "tp", 2)
    near_odds = flip(near_late, "ep", 1)
    far_odds_y = flip(cut(near_odds, 0, half), "tp", 2)
    far_odds_x = flip(cut(far_late, half, len(late) - half), "ep", 1)
    pieces = [(1, (0, 2), both_1), (1, (1, 3), flip(both_1, "tp", 1))]
    for start, part, array in (
        (2, 0, near_2),
        (2, 2, far_2),
        (3, 0, near_3),
        (3, 2, far_3),
        (evens, 0, near_late),
        (evens, 2, far_late),
        (odds, 0, near_odds),
        (odds, 2, far_odds_y),
        (odds + half, 2, far_odds_x),
    ):
        pieces += [(start, (part,), array), (start, (part ^ 1,), flip(array, "tp", 1))]

    levels = ep_size.bit_length() - 1

    def page_hop(page, level):
        swapped = flip(page, "ep", 1 << level)
        bit = jnp.bitwise_and(jnp.right_shift(mask_value, level), 1) == 1
        return jnp.where(bit, swapped, page)

    page = lax.dynamic_index_in_dim(cache_pages, my_slot, 0, keepdims=False)
    page, _ = lax.optimization_barrier((page, near_late))
    for level in range(levels - 1, 1, -1):
        page = page_hop(page, level)
    ranks, page = lax.optimization_barrier((ranks, page))
    for level in range(min(levels, 2)):
        page = page_hop(page, level)
    traded = jnp.stack([my_slot, far_length]).astype(jnp.int32)
    attended = attend_traded(traded, queries, page, attended)

    cross, side, sent, kept = run_experts(
        order, ranks, gates, hidden, pieces, w_gate, w_up, w_down, columns
    )
    cross = flip(cross, "tp", 1)
    side = flip(side, "tp", 1)

    def sent_of(start, count):
        return total_of(cut(sent, start, count), cut(cross, start, count))

    def kept_of(start, count):
        return total_of(cut(kept, start, count), cut(side, start, count))

    rest = len(late) - half
    over_y = flip(sent_of(odds, half), "tp", 2)
    over_x = flip(sent_of(odds + half, rest), "ep", 1)
    over_3 = flip(sent_of(3, 1), "tp", 2)
    over_2 = flip(sent_of(2, 1), "tp", 2)
    over_1 = flip(jnp.concatenate([kept_of(1, 1), sent_of(1, 1)], axis=1), "ep", 1)
    odd = total_of(kept_of(odds, len(late)), jnp.pad(over_y, ((0, rest * rows), (0, 0))))
    odd = flip(odd, "ep", 1)
    even = total_of(sent_of(evens, len(late)), jnp.pad(over_x, ((half * rows, 0), (0, 0))))
    even = flip(even, "tp", 2)
    near_3 = flip(total_of(kept_of(3, 1), over_3), "ep", 1)
    zero = flip(total_of(sent_of(0, 1), over_1[:, columns:]), "tp", 2)
    even = total_of(kept_of(evens, len(late)), even, odd)
    back = [flip(cut(even, i, 1), "ep", 2 * m) for i, m in enumerate(late)]
    back.append(flip(total_of(kept_of(2, 1), over_2, near_3), "ep", 2))
    moe_out = total_of(kept_of(0, 1), over_1[:, :columns], zero, *back)
    return attended, moe_out


def solution(mesh):
    in_specs = (
        P(("ep", "tp"), None, None),
        P(("ep", "tp"), None, None),
        P(),
        P(),
        P(),
        P("ep", None),
        P("ep", None),
        P("ep", None),
        P("ep", None, "tp"),
        P("ep", None, "tp"),
        P("ep", "tp", None),
    )
    out_specs = (P(("ep", "tp"), None, None), P("ep", "tp"))
    return jax.shard_map(local, mesh=mesh, in_specs=in_specs, out_specs=out_specs, check_vma=False)
```

```python
import functools
import math

import jax
import jax.numpy as jnp
from jax import lax
from jax.experimental import pallas as pl
from jax.experimental.pallas import tpu as pltpu
from jax.sharding import PartitionSpec as P

LAT = 512
SCORE_SCALE = 192.0 ** (-0.5)
MASK_FLOOR = -1e30
ROWS = 512
MIB = 1 << 20


def flip(block, axis, apart):
    count = lax.axis_size(axis)
    return lax.ppermute(block, axis, [(i, i ^ apart) for i in range(count)])


def attend_body(query, page, length):
    scores = (
        lax.dot_general(query, page, (((0,), (0,)), ((), ())), preferred_element_type=jnp.float32)
        * SCORE_SCALE
    )
    live = lax.broadcasted_iota(jnp.int32, scores.shape, 1) < length
    scores = jnp.where(live, scores, MASK_FLOOR)
    top = jnp.max(scores, axis=1, keepdims=True)
    weight = jnp.where(live, jnp.exp(scores - top), 0.0)
    total = jnp.sum(weight, axis=1, keepdims=True)
    blended = lax.dot_general(
        weight.astype(jnp.bfloat16),
        page[:LAT],
        (((1,), (1,)), ((), ())),
        preferred_element_type=jnp.float32,
    )
    return (blended / total).astype(jnp.bfloat16)


def in_hbm(array):
    return pltpu.with_memory_space_constraint(array, pltpu.HBM)


def in_vmem(array):
    return pltpu.with_memory_space_constraint(array, pltpu.VMEM)


ANYWHERE = pl.BlockSpec(memory_space=pl.ANY)
IN_VMEM = pl.BlockSpec(memory_space=pltpu.VMEM)
IN_SMEM = pl.BlockSpec(memory_space=pltpu.SMEM)


def device_of(ranks_ref, groups, mask=0):
    return (ranks_ref[0] ^ mask) * groups + ranks_ref[1]


def pick_kernel(groups, ranks_ref, slots_ref, ids_ref, gates_ref, hidden_ref, pages_ref, near_ref, both_ref, page_ref, sems):
    rows = hidden_ref.shape[0]
    columns = hidden_ref.shape[1] // groups

    def quarter(part):
        start = pl.multiple_of((ranks_ref[1] ^ part) * columns, 128)
        return hidden_ref.at[:, pl.ds(start, columns)]

    copies = [
        (quarter(0), near_ref.at[:, pl.ds(0, columns)]),
        (quarter(0), both_ref.at[:, pl.ds(0, columns)]),
        (quarter(2), both_ref.at[:, pl.ds(columns, columns)]),
        (pages_ref.at[slots_ref[device_of(ranks_ref, groups)]], page_ref),
    ]
    copies = [pltpu.make_async_copy(*pair, sems.at[i]) for i, pair in enumerate(copies)]
    for one in copies:
        one.start()
    gates = gates_ref[...]
    high = gates.astype(jnp.bfloat16).astype(jnp.float32)
    middle = (gates - high).astype(jnp.bfloat16).astype(jnp.float32)
    low = gates - high - middle
    top = gates.shape[0]
    table = jnp.concatenate(
        [ids_ref[...].astype(jnp.float32), high, middle, low, jnp.zeros((128 - 4 * top, rows), jnp.float32)],
        axis=0,
    )
    table = jnp.concatenate([table, jnp.zeros((128, 128 - rows), jnp.float32)], axis=1)
    table = table.T[:rows].astype(jnp.bfloat16)
    near_ref[:, columns:] = table
    both_ref[:, 2 * columns :] = table
    for one in copies:
        one.wait()


def pick(ranks, swap_slot, expert_ids, gate_weights, hidden, pages, groups):
    rows, width = hidden.shape
    columns = width // groups
    return pl.pallas_call(
        functools.partial(pick_kernel, groups),
        out_shape=(
            pltpu.VMEM((rows, columns + 128), jnp.bfloat16),
            pltpu.VMEM((rows, 2 * columns + 128), jnp.bfloat16),
            pltpu.VMEM(pages.shape[1:], jnp.bfloat16),
        ),
        in_specs=[IN_SMEM, IN_SMEM, IN_VMEM, IN_VMEM, ANYWHERE, ANYWHERE],
        out_specs=(IN_VMEM, IN_VMEM, IN_VMEM),
        scratch_shapes=[pltpu.SemaphoreType.DMA((4,))],
        compiler_params=pltpu.CompilerParams(vmem_limit_bytes=2 * MIB),
        name="pick",
    )(ranks, swap_slot, expert_ids.T, gate_weights.T, in_hbm(hidden), in_hbm(pages))


def attend_kernel(
    each,
    groups,
    ranks_ref,
    lengths_ref,
    query_ref,
    page_ref,
    w_gate_ref,
    w_up_ref,
    w_down_ref,
    out_ref,
    gate_ref,
    up_ref,
    down_ref,
    sems,
):
    step, steps = pl.program_id(0), pl.num_programs(0)
    copies = [
        pltpu.make_async_copy(source, target, sems.at[i])
        for i, (source, target) in enumerate(
            ((w_gate_ref, gate_ref), (w_up_ref, up_ref), (w_down_ref, down_ref))
        )
    ]

    @pl.when(step == 0)
    def _():
        for one in copies:
            one.start()

    first = device_of(ranks_ref, groups) * each * steps + step * each
    for i in range(each):
        out_ref[i] = attend_body(query_ref[i], page_ref[i], lengths_ref[first + i])

    @pl.when(step == steps - 1)
    def _():
        for one in copies:
            one.wait()


def attend_all(ranks, lengths, queries, pages, groups, *weights):
    count, width, heads = queries.shape
    slots = pages.shape[2]
    each = math.gcd(count, 4)
    moved = sum(2 * math.prod(w.shape) for w in weights)
    return pl.pallas_call(
        functools.partial(attend_kernel, each, groups),
        out_shape=[jax.ShapeDtypeStruct((count, heads, LAT), jnp.bfloat16)]
        + [pltpu.VMEM(w.shape, w.dtype) for w in weights],
        grid_spec=pltpu.PrefetchScalarGridSpec(
            num_scalar_prefetch=2,
            grid=(count // each,),
            in_specs=[
                pl.BlockSpec((each, width, heads), lambda i, *_: (i, 0, 0)),
                pl.BlockSpec((each, width, slots), lambda i, *_: (i, 0, 0)),
            ]
            + [ANYWHERE] * len(weights),
            out_specs=[pl.BlockSpec((each, heads, LAT), lambda i, *_: (i, 0, 0))]
            + [ANYWHERE] * len(weights),
            scratch_shapes=[pltpu.SemaphoreType.DMA((len(weights),))],
        ),
        compiler_params=pltpu.CompilerParams(vmem_limit_bytes=12 * MIB),
        cost_estimate=pl.CostEstimate(
            flops=2 * count * heads * slots * (width + LAT),
            bytes_accessed=2 * count * (heads * (width + LAT) + slots * width) + moved,
            transcendentals=count * heads * slots,
        ),
        name="attend_local",
    )(ranks, lengths, in_hbm(queries), in_hbm(pages), *[in_hbm(w) for w in weights])


def attend_traded_kernel(
    groups, ranks_ref, lengths_ref, slots_ref, mask_ref, query_ref, page_ref, old_ref, out_ref
):
    partner = device_of(ranks_ref, groups, mask_ref[0])
    length = lengths_ref[partner * old_ref.shape[0] + slots_ref[partner]]
    out_ref[0] = attend_body(query_ref[0], page_ref[...], length)


def attend_traded(ranks, lengths, swap_slot, swap_mask, queries, page, attended, groups):
    _, width, heads = queries.shape
    slots = page.shape[1]

    def mine(i, ranks_ref, lengths_ref, slots_ref, mask_ref):
        return slots_ref[device_of(ranks_ref, groups)], 0, 0

    return pl.pallas_call(
        functools.partial(attend_traded_kernel, groups),
        out_shape=jax.ShapeDtypeStruct(attended.shape, attended.dtype),
        grid_spec=pltpu.PrefetchScalarGridSpec(
            num_scalar_prefetch=4,
            grid=(1,),
            in_specs=[
                pl.BlockSpec((1, width, heads), mine),
                pl.BlockSpec((width, slots), lambda i, *_: (0, 0)),
                ANYWHERE,
            ],
            out_specs=pl.BlockSpec((1, heads, LAT), mine),
        ),
        input_output_aliases={6: 0},
        compiler_params=pltpu.CompilerParams(vmem_limit_bytes=4 * MIB),
        cost_estimate=pl.CostEstimate(
            flops=2 * heads * slots * (width + LAT),
            bytes_accessed=2 * (heads * (width + LAT) + slots * width),
            transcendentals=heads * slots,
        ),
        name="attend_traded",
    )(ranks, lengths, swap_slot, swap_mask, in_hbm(queries), page, attended)


def experts_kernel(
    top,
    ranks_ref,
    hidden_ref,
    pieces,
    gate_ref,
    up_ref,
    down_ref,
    cross_ref,
    side_ref,
    sent_ref,
    kept_ref,
    rows_ref,
    meta_ref,
    inner_ref,
    table_ref,
    sems,
):
    experts, _, units = gate_ref.shape
    block_rows = hidden_ref.shape[0]
    total_rows = rows_ref.shape[0]
    quarter = kept_ref.shape[1]
    ep_rank, tp_rank = ranks_ref[0], ranks_ref[1]

    def columns_of(part):
        return pl.ds(pl.multiple_of((tp_rank ^ part) * quarter, 128), quarter)

    copies = [(hidden_ref, rows_ref.at[pl.ds(0, block_rows), :])]
    for start, parts, has_meta, piece in pieces:
        rows = pl.ds(start * block_rows, piece.shape[0])
        for i, part in enumerate(parts):
            copies.append(
                (piece.at[:, pl.ds(i * quarter, quarter)], rows_ref.at[rows, columns_of(part)])
            )
        if has_meta:
            copies.append((piece.at[:, pl.ds(piece.shape[1] - 128, 128)], meta_ref.at[rows, :]))
    copies = [
        pltpu.make_async_copy(source, target, sems.at[i])
        for i, (source, target) in enumerate(copies)
    ]
    for one in copies:
        one.start()
    for one in copies:
        one.wait()
    meta = meta_ref[...].astype(jnp.float32)
    gates = sum(pltpu.roll(meta, 128 - i * top, 1) for i in range(1, 4))
    lane = lax.broadcasted_iota(jnp.int32, meta.shape, 1)
    for e in range(experts):
        name = (ep_rank * experts + e).astype(jnp.float32)
        mine = jnp.where((lane < top) & (meta == name), gates, 0.0)
        table_ref[:, e : e + 1] = jnp.sum(mine, axis=1, keepdims=True)
    stride = math.gcd(total_rows, ROWS)
    for e in range(experts):

        @pl.loop(0, total_rows // stride)
        def _(step):
            at = pl.ds(pl.multiple_of(step * stride, stride), stride)
            rows = rows_ref[at, :]
            gate = jnp.dot(rows, gate_ref[e], preferred_element_type=jnp.float32)
            up = jnp.dot(rows, up_ref[e], preferred_element_type=jnp.float32)
            act = gate / (1.0 + jnp.exp(-gate)) * up * table_ref[at, e : e + 1]
            inner_ref[at, e * units : (e + 1) * units] = act.astype(jnp.bfloat16)

    for part, out_ref in ((3, cross_ref), (1, side_ref), (2, sent_ref), (0, kept_ref)):

        @pl.loop(0, total_rows // stride)
        def _(step):
            at = pl.ds(pl.multiple_of(step * stride, stride), stride)
            weight = down_ref[:, :, columns_of(part)].reshape(experts * units, quarter)
            out_ref[at, :] = jnp.dot(
                inner_ref[at, :], weight, preferred_element_type=jnp.float32
            ).astype(jnp.bfloat16)


def run_experts(ranks, hidden, pieces, weights, rows, columns, top):
    width = hidden.shape[1]
    experts, _, units = weights[0].shape
    arrays = [piece for *_, piece in pieces]
    count = 1 + sum(len(parts) + has_meta for _, parts, has_meta, _ in pieces)

    def kernel(ranks_ref, hidden_ref, refs, *others):
        named = [(*about[:3], ref) for about, ref in zip(pieces, refs)]
        experts_kernel(top, ranks_ref, hidden_ref, named, *others)

    need = 2 * rows * (width + 128 + experts * units) + 512 * rows
    return pl.pallas_call(
        kernel,
        out_shape=[pltpu.VMEM((rows, columns), jnp.bfloat16)] * 4,
        in_specs=[IN_SMEM, ANYWHERE, [ANYWHERE] * len(arrays), IN_VMEM, IN_VMEM, IN_VMEM],
        out_specs=[IN_VMEM] * 4,
        scratch_shapes=[
            pltpu.VMEM((rows, width), jnp.bfloat16),
            pltpu.VMEM((rows, 128), jnp.bfloat16),
            pltpu.VMEM((rows, experts * units), jnp.bfloat16),
            pltpu.VMEM((rows, 128), jnp.float32),
            pltpu.SemaphoreType.DMA((count,)),
        ],
        compiler_params=pltpu.CompilerParams(vmem_limit_bytes=need + 6 * MIB),
        cost_estimate=pl.CostEstimate(
            flops=6 * rows * width * units * experts,
            bytes_accessed=4 * rows * width,
            transcendentals=rows * units * experts,
        ),
        name="experts",
    )(ranks, in_hbm(hidden), arrays, *[in_vmem(w) for w in weights])


def total_of(*terms):
    value = terms[0].astype(jnp.float32)
    for term in terms[1:]:
        value = value + term.astype(jnp.float32)
    return value.astype(jnp.bfloat16)


def local(
    cache_pages,
    queries,
    lengths,
    swap_slot,
    swap_mask,
    hidden,
    expert_ids,
    gate_weights,
    w_gate,
    w_up,
    w_down,
):
    groups = lax.axis_size("tp")
    ep_size = lax.axis_size("ep")
    ranks = jnp.stack([lax.axis_index("ep"), lax.axis_index("tp")]).astype(jnp.int32)
    mask_value = swap_mask[0]
    columns = hidden.shape[1] // groups
    top = expert_ids.shape[1]
    cache_pages = jnp.swapaxes(cache_pages, 1, 2)
    queries = jnp.swapaxes(queries, 1, 2)

    rows = hidden.shape[0]
    pairs = ep_size // 2
    late = list(range(2, pairs))
    half = len(late) // 2
    evens, odds = 4, 4 + len(late)

    def cut(array, start, count):
        return lax.slice_in_dim(array, start * rows, (start + count) * rows, axis=0)

    def bare(array):
        return array[:, :columns]

    own, both, page = pick(
        ranks, swap_slot, expert_ids, gate_weights, hidden, cache_pages, groups
    )
    late_pieces = [flip(own, "ep", 2 * m) for m in late]
    near_2 = flip(own, "ep", 2)
    both_1 = flip(both, "ep", 1)
    far_2 = flip(bare(near_2), "tp", 2)
    near_3 = flip(near_2, "ep", 1)
    far_3 = flip(bare(near_3), "tp", 2)

    levels = ep_size.bit_length() - 1

    def page_hop(page, level):
        swapped = flip(page, "ep", 1 << level)
        bit = jnp.bitwise_and(jnp.right_shift(mask_value, level), 1) == 1
        return jnp.where(bit, swapped, page)

    attended, *weights = attend_all(
        ranks, lengths, queries, cache_pages, groups, w_gate, w_up, w_down
    )
    page = page_hop(page, 0)
    near_late = jnp.concatenate(late_pieces, axis=0)
    near_late, attended, page = lax.optimization_barrier((near_late, attended, page))

    far_late = flip(bare(near_late), "tp", 2)
    near_odds = flip(near_late, "ep", 1)
    far_odds_y = flip(bare(cut(near_odds, 0, half)), "tp", 2)
    far_odds_x = flip(cut(far_late, half, len(late) - half), "ep", 1)
    pieces = [
        (0, (), True, own),
        (1, (0, 2), True, both_1),
        (1, (1, 3), False, flip(both_1, "tp", 1)),
    ]
    for start, part, array in (
        (2, 0, near_2),
        (2, 2, far_2),
        (3, 0, near_3),
        (3, 2, far_3),
        (evens, 0, near_late),
        (evens, 2, far_late),
        (odds, 0, near_odds),
        (odds, 2, far_odds_y),
        (odds + half, 2, far_odds_x),
    ):
        pieces += [
            (start, (part,), part == 0, array),
            (start, (part ^ 1,), False, flip(array, "tp", 1)),
        ]

    for level in range(levels - 1, 1, -1):
        page = page_hop(page, level)
    ranks, page = lax.optimization_barrier((ranks, page))
    if levels > 1:
        page = page_hop(page, 1)
    attended = attend_traded(
        ranks, lengths, swap_slot, swap_mask, queries, page, attended, groups
    )

    cross, side, sent, kept = run_experts(
        ranks, hidden, pieces, weights, ep_size * rows, columns, top
    )
    cross = flip(cross, "tp", 1)
    side = flip(side, "tp", 1)

    def sent_of(start, count):
        return total_of(cut(sent, start, count), cut(cross, start, count))

    def kept_of(start, count):
        return total_of(cut(kept, start, count), cut(side, start, count))

    rest = len(late) - half
    over_y = flip(sent_of(odds, half), "tp", 2)
    over_x = flip(sent_of(odds + half, rest), "ep", 1)
    over_3 = flip(sent_of(3, 1), "tp", 2)
    over_2 = flip(sent_of(2, 1), "tp", 2)
    over_1 = flip(jnp.concatenate([kept_of(1, 1), sent_of(1, 1)], axis=1), "ep", 1)
    odd = total_of(kept_of(odds, len(late)), jnp.pad(over_y, ((0, rest * rows), (0, 0))))
    odd = flip(odd, "ep", 1)
    even = total_of(sent_of(evens, len(late)), jnp.pad(over_x, ((half * rows, 0), (0, 0))))
    even = flip(even, "tp", 2)
    near_3 = flip(total_of(kept_of(3, 1), over_3), "ep", 1)
    zero = flip(total_of(sent_of(0, 1), over_1[:, columns:]), "tp", 2)
    even = total_of(kept_of(evens, len(late)), even, odd)
    back = [flip(cut(even, i, 1), "ep", 2 * m) for i, m in enumerate(late)]
    back.append(flip(total_of(kept_of(2, 1), over_2, near_3), "ep", 2))
    moe_out = total_of(kept_of(0, 1), over_1[:, :columns], zero, *back)
    return attended, moe_out


def solution(mesh):
    in_specs = (
        P(("ep", "tp"), None, None),
        P(("ep", "tp"), None, None),
        P(),
        P(),
        P(),
        P("ep", None),
        P("ep", None),
        P("ep", None),
        P("ep", None, "tp"),
        P("ep", None, "tp"),
        P("ep", "tp", None),
    )
    out_specs = (P(("ep", "tp"), None, None), P("ep", "tp"))
    return jax.shard_map(local, mesh=mesh, in_specs=in_specs, out_specs=out_specs, check_vma=False)
```

```python
import functools
import math

import jax
import jax.numpy as jnp
from jax import lax
from jax.experimental import pallas as pl
from jax.experimental.pallas import tpu as pltpu
from jax.sharding import PartitionSpec as P

LAT = 512
SCORE_SCALE = 192.0 ** (-0.5)
MASK_FLOOR = -1e30
ROWS = 512
MIB = 1 << 20


def flip(block, axis, apart):
    count = lax.axis_size(axis)
    return lax.ppermute(block, axis, [(i, i ^ apart) for i in range(count)])


def attend_body(query, page, length):
    scores = (
        lax.dot_general(query, page, (((0,), (0,)), ((), ())), preferred_element_type=jnp.float32)
        * SCORE_SCALE
    )
    live = lax.broadcasted_iota(jnp.int32, scores.shape, 1) < length
    scores = jnp.where(live, scores, MASK_FLOOR)
    top = jnp.max(scores, axis=1, keepdims=True)
    weight = jnp.where(live, jnp.exp(scores - top), 0.0)
    total = jnp.sum(weight, axis=1, keepdims=True)
    blended = lax.dot_general(
        weight.astype(jnp.bfloat16),
        page[:LAT],
        (((1,), (1,)), ((), ())),
        preferred_element_type=jnp.float32,
    )
    return (blended / total).astype(jnp.bfloat16)


def in_hbm(array):
    return pltpu.with_memory_space_constraint(array, pltpu.HBM)


def in_vmem(array):
    return pltpu.with_memory_space_constraint(array, pltpu.VMEM)


ANYWHERE = pl.BlockSpec(memory_space=pl.ANY)
IN_VMEM = pl.BlockSpec(memory_space=pltpu.VMEM)
IN_SMEM = pl.BlockSpec(memory_space=pltpu.SMEM)


def device_of(ranks_ref, groups, mask=0):
    return (ranks_ref[0] ^ mask) * groups + ranks_ref[1]


def pick_kernel(groups, ranks_ref, slots_ref, ids_ref, gates_ref, hidden_ref, pages_ref, near_ref, both_ref, page_ref, sems):
    rows = hidden_ref.shape[0]
    columns = hidden_ref.shape[1] // groups

    def quarter(part):
        start = pl.multiple_of((ranks_ref[1] ^ part) * columns, 128)
        return hidden_ref.at[:, pl.ds(start, columns)]

    copies = [
        (quarter(0), near_ref.at[:, pl.ds(0, columns)]),
        (quarter(0), both_ref.at[:, pl.ds(0, columns)]),
        (quarter(2), both_ref.at[:, pl.ds(columns, columns)]),
        (pages_ref.at[slots_ref[device_of(ranks_ref, groups)]], page_ref),
    ]
    copies = [pltpu.make_async_copy(*pair, sems.at[i]) for i, pair in enumerate(copies)]
    for one in copies:
        one.start()
    gates = gates_ref[...]
    high = gates.astype(jnp.bfloat16).astype(jnp.float32)
    middle = (gates - high).astype(jnp.bfloat16).astype(jnp.float32)
    low = gates - high - middle
    top = gates.shape[0]
    table = jnp.concatenate(
        [ids_ref[...].astype(jnp.float32), high, middle, low, jnp.zeros((128 - 4 * top, rows), jnp.float32)],
        axis=0,
    )
    table = jnp.concatenate([table, jnp.zeros((128, 128 - rows), jnp.float32)], axis=1)
    table = table.T[:rows].astype(jnp.bfloat16)
    near_ref[:, columns:] = table
    both_ref[:, 2 * columns :] = table
    for one in copies:
        one.wait()


def pick(ranks, swap_slot, expert_ids, gate_weights, hidden, pages, groups):
    rows, width = hidden.shape
    columns = width // groups
    return pl.pallas_call(
        functools.partial(pick_kernel, groups),
        out_shape=(
            pltpu.VMEM((rows, columns + 128), jnp.bfloat16),
            pltpu.VMEM((rows, 2 * columns + 128), jnp.bfloat16),
            pltpu.VMEM(pages.shape[1:], jnp.bfloat16),
        ),
        in_specs=[IN_SMEM, IN_SMEM, IN_VMEM, IN_VMEM, ANYWHERE, ANYWHERE],
        out_specs=(IN_VMEM, IN_VMEM, IN_VMEM),
        scratch_shapes=[pltpu.SemaphoreType.DMA((4,))],
        compiler_params=pltpu.CompilerParams(vmem_limit_bytes=2 * MIB),
        name="pick",
    )(
        ranks,
        in_hbm(swap_slot),
        in_hbm(expert_ids.T),
        in_hbm(gate_weights.T),
        in_hbm(hidden),
        in_hbm(pages),
    )


def attend_kernel(each, groups, ranks_ref, lengths_ref, query_ref, page_ref, out_ref):
    step, steps = pl.program_id(0), pl.num_programs(0)
    first = device_of(ranks_ref, groups) * each * steps + step * each
    for i in range(each):
        out_ref[i] = attend_body(query_ref[i], page_ref[i], lengths_ref[first + i])


def attend_all(ranks, lengths, queries, pages, groups):
    count, width, heads = queries.shape
    slots = pages.shape[2]
    each = math.gcd(count, 4)
    return pl.pallas_call(
        functools.partial(attend_kernel, each, groups),
        out_shape=jax.ShapeDtypeStruct((count, heads, LAT), jnp.bfloat16),
        grid_spec=pltpu.PrefetchScalarGridSpec(
            num_scalar_prefetch=2,
            grid=(count // each,),
            in_specs=[
                pl.BlockSpec((each, width, heads), lambda i, *_: (i, 0, 0)),
                pl.BlockSpec((each, width, slots), lambda i, *_: (i, 0, 0)),
            ],
            out_specs=pl.BlockSpec((each, heads, LAT), lambda i, *_: (i, 0, 0)),
        ),
        compiler_params=pltpu.CompilerParams(vmem_limit_bytes=12 * MIB),
        cost_estimate=pl.CostEstimate(
            flops=2 * count * heads * slots * (width + LAT),
            bytes_accessed=2 * count * (heads * (width + LAT) + slots * width),
            transcendentals=count * heads * slots,
        ),
        name="attend_local",
    )(ranks, lengths, in_hbm(queries), in_hbm(pages))


def load_kernel(*refs):
    count = len(refs) // 2
    copies = [
        pltpu.make_async_copy(refs[i], refs[count + i], refs[-1].at[i]) for i in range(count)
    ]
    for one in copies:
        one.start()
    for one in copies:
        one.wait()


def load(*arrays):
    return pl.pallas_call(
        load_kernel,
        out_shape=[pltpu.VMEM(w.shape, w.dtype) for w in arrays],
        in_specs=[ANYWHERE] * len(arrays),
        out_specs=[ANYWHERE] * len(arrays),
        scratch_shapes=[pltpu.SemaphoreType.DMA((len(arrays),))],
        compiler_params=pltpu.CompilerParams(vmem_limit_bytes=MIB),
        cost_estimate=pl.CostEstimate(
            flops=0, bytes_accessed=sum(2 * math.prod(w.shape) for w in arrays), transcendentals=0
        ),
        name="load",
    )(*[in_hbm(w) for w in arrays])


def attend_traded_kernel(
    groups, ranks_ref, lengths_ref, slots_ref, mask_ref, query_ref, page_ref, old_ref, out_ref
):
    partner = device_of(ranks_ref, groups, mask_ref[0])
    length = lengths_ref[partner * old_ref.shape[0] + slots_ref[partner]]
    out_ref[0] = attend_body(query_ref[0], page_ref[...], length)


def attend_traded(ranks, lengths, swap_slot, swap_mask, queries, page, attended, groups):
    _, width, heads = queries.shape
    slots = page.shape[1]

    def mine(i, ranks_ref, lengths_ref, slots_ref, mask_ref):
        return slots_ref[device_of(ranks_ref, groups)], 0, 0

    return pl.pallas_call(
        functools.partial(attend_traded_kernel, groups),
        out_shape=jax.ShapeDtypeStruct(attended.shape, attended.dtype),
        grid_spec=pltpu.PrefetchScalarGridSpec(
            num_scalar_prefetch=4,
            grid=(1,),
            in_specs=[
                pl.BlockSpec((1, width, heads), mine),
                pl.BlockSpec((width, slots), lambda i, *_: (0, 0)),
                ANYWHERE,
            ],
            out_specs=pl.BlockSpec((1, heads, LAT), mine),
        ),
        input_output_aliases={6: 0},
        compiler_params=pltpu.CompilerParams(vmem_limit_bytes=4 * MIB),
        cost_estimate=pl.CostEstimate(
            flops=2 * heads * slots * (width + LAT),
            bytes_accessed=2 * (heads * (width + LAT) + slots * width),
            transcendentals=heads * slots,
        ),
        name="attend_traded",
    )(ranks, lengths, swap_slot, swap_mask, in_hbm(queries), page, attended)


def experts_kernel(
    top,
    fetch,
    ranks_ref,
    pieces,
    gate_ref,
    up_ref,
    source_ref,
    cross_ref,
    side_ref,
    sent_ref,
    kept_ref,
    *refs,
):
    if fetch:
        down_ref, *refs = refs
    else:
        down_ref = source_ref
    rows_ref, meta_ref, inner_ref, table_ref, sems, down_sem = refs
    experts, _, units = gate_ref.shape
    total_rows = rows_ref.shape[0]
    quarter = kept_ref.shape[1]
    ep_rank, tp_rank = ranks_ref[0], ranks_ref[1]

    def columns_of(part):
        return pl.ds(pl.multiple_of((tp_rank ^ part) * quarter, 128), quarter)

    copies = []
    for start, parts, has_meta, piece in pieces:
        rows = pl.ds(start, piece.shape[0])
        if parts is None:
            copies.append((piece, rows_ref.at[rows, :]))
            continue
        for i, part in enumerate(parts):
            copies.append(
                (piece.at[:, pl.ds(i * quarter, quarter)], rows_ref.at[rows, columns_of(part)])
            )
        if has_meta:
            copies.append((piece.at[:, pl.ds(piece.shape[1] - 128, 128)], meta_ref.at[rows, :]))
    copies = [
        pltpu.make_async_copy(source, target, sems.at[i])
        for i, (source, target) in enumerate(copies)
    ]
    for one in copies:
        one.start()
    if fetch:
        down_copy = pltpu.make_async_copy(source_ref, down_ref, down_sem)
        down_copy.start()
    for one in copies:
        one.wait()
    meta = meta_ref[...].astype(jnp.float32)
    gates = sum(pltpu.roll(meta, 128 - i * top, 1) for i in range(1, 4))
    lane = lax.broadcasted_iota(jnp.int32, meta.shape, 1)
    for e in range(experts):
        name = (ep_rank * experts + e).astype(jnp.float32)
        mine = jnp.where((lane < top) & (meta == name), gates, 0.0)
        table_ref[:, e : e + 1] = jnp.sum(mine, axis=1, keepdims=True)
    stride = math.gcd(total_rows, ROWS)
    for e in range(experts):

        @pl.loop(0, total_rows // stride)
        def _(step):
            at = pl.ds(pl.multiple_of(step * stride, stride), stride)
            rows = rows_ref[at, :]
            gate = jnp.dot(rows, gate_ref[e], preferred_element_type=jnp.float32)
            up = jnp.dot(rows, up_ref[e], preferred_element_type=jnp.float32)
            act = gate / (1.0 + jnp.exp(-gate)) * up * table_ref[at, e : e + 1]
            inner_ref[at, e * units : (e + 1) * units] = act.astype(jnp.bfloat16)

    if fetch:
        down_copy.wait()
    for part, out_ref in ((3, cross_ref), (1, side_ref), (2, sent_ref), (0, kept_ref)):

        @pl.loop(0, total_rows // stride)
        def _(step):
            at = pl.ds(pl.multiple_of(step * stride, stride), stride)
            weight = down_ref[:, :, columns_of(part)].reshape(experts * units, quarter)
            out_ref[at, :] = jnp.dot(
                inner_ref[at, :], weight, preferred_element_type=jnp.float32
            ).astype(jnp.bfloat16)


def run_experts(ranks, pieces, w_gate, w_up, w_down, rows, columns, top, fetch):
    experts, width, units = w_gate.shape
    arrays = [piece for *_, piece in pieces]
    count = sum(1 if parts is None else len(parts) + has_meta for _, parts, has_meta, _ in pieces)

    def kernel(ranks_ref, refs, *others):
        named = [(*about[:3], ref) for about, ref in zip(pieces, refs)]
        experts_kernel(top, fetch, ranks_ref, named, *others)

    need = 2 * rows * (width + 128 + experts * units) + 512 * rows
    down_shape = [pltpu.VMEM(w_down.shape, w_down.dtype)] if fetch else []
    return pl.pallas_call(
        kernel,
        out_shape=[pltpu.VMEM((rows, columns), jnp.bfloat16)] * 4 + down_shape,
        in_specs=[
            IN_SMEM,
            [ANYWHERE] * len(arrays),
            IN_VMEM,
            IN_VMEM,
            ANYWHERE if fetch else IN_VMEM,
        ],
        out_specs=[IN_VMEM] * (4 + len(down_shape)),
        scratch_shapes=[
            pltpu.VMEM((rows, width), jnp.bfloat16),
            pltpu.VMEM((rows, 128), jnp.bfloat16),
            pltpu.VMEM((rows, experts * units), jnp.bfloat16),
            pltpu.VMEM((rows, 128), jnp.float32),
            pltpu.SemaphoreType.DMA((count,)),
            pltpu.SemaphoreType.DMA,
        ],
        compiler_params=pltpu.CompilerParams(vmem_limit_bytes=need + 6 * MIB),
        cost_estimate=pl.CostEstimate(
            flops=6 * rows * width * units * experts,
            bytes_accessed=4 * rows * width,
            transcendentals=rows * units * experts,
        ),
        name="experts",
    )(
        ranks,
        arrays,
        in_vmem(w_gate),
        in_vmem(w_up),
        in_hbm(w_down) if fetch else in_vmem(w_down),
    )


def total_of(*terms):
    value = terms[0].astype(jnp.float32)
    for term in terms[1:]:
        value = value + term.astype(jnp.float32)
    return value.astype(jnp.bfloat16)


def local(
    cache_pages,
    queries,
    lengths,
    swap_slot,
    swap_mask,
    hidden,
    expert_ids,
    gate_weights,
    w_gate,
    w_up,
    w_down,
):
    groups = lax.axis_size("tp")
    ep_size = lax.axis_size("ep")
    ranks = jnp.stack([lax.axis_index("ep"), lax.axis_index("tp")]).astype(jnp.int32)
    mask_value = swap_mask[0]
    columns = hidden.shape[1] // groups
    top = expert_ids.shape[1]
    cache_pages = jnp.swapaxes(cache_pages, 1, 2)
    queries = jnp.swapaxes(queries, 1, 2)

    rows = hidden.shape[0]
    pairs = ep_size // 2
    late = list(range(2, pairs))
    half = len(late) // 2
    rest = len(late) - half
    levels = ep_size.bit_length() - 1
    tie = lax.optimization_barrier

    def cut(array, start, count):
        return lax.slice_in_dim(array, start * rows, (start + count) * rows, axis=0)

    def bare(array):
        return array[:, :columns]

    def page_hop(page, level):
        swapped = flip(page, "ep", 1 << level)
        bit = jnp.bitwise_and(jnp.right_shift(mask_value, level), 1) == 1
        return jnp.where(bit, swapped, page)

    own, both, page = pick(
        ranks, swap_slot, expert_ids, gate_weights, hidden, cache_pages, groups
    )
    late_pieces = [flip(own, "ep", 2 * m) for m in late]
    near_2 = flip(own, "ep", 2)
    both_1 = flip(both, "ep", 1)

    near_2, w_gate, w_up = tie((near_2, w_gate, w_up))
    far_2 = flip(bare(near_2), "tp", 2)
    near_3 = flip(near_2, "ep", 1)
    w_gate, w_up = load(w_gate, w_up)
    far_2, near_3, w_gate, w_up, page, both_1, *late_pieces = tie(
        (far_2, near_3, w_gate, w_up, page, both_1, *late_pieces)
    )
    for level in range(levels - 1, 1, -1):
        page = page_hop(page, level)
    far_3 = flip(bare(near_3), "tp", 2)

    near_late = jnp.concatenate(late_pieces, axis=0)
    far_2, queries = tie((far_2, queries))
    far_late = flip(bare(near_late), "tp", 2)
    near_odds = flip(near_late, "ep", 1)
    attended = attend_all(ranks, lengths, queries, cache_pages, groups)
    early = [flip(array, "tp", 1) for array in (both_1, near_2, far_2, near_3)]
    far_late, near_odds, far_3, attended, page, early = tie(
        (far_late, near_odds, far_3, attended, page, early)
    )
    page = page_hop(page, 0)
    far_odds_y = flip(bare(cut(near_odds, 0, half)), "tp", 2)
    far_odds_x = flip(cut(far_late, half, rest), "ep", 1)

    def with_core(start, part, array, other):
        start = start * rows
        return [(start, (part,), part == 0, array), (start, (part ^ 1,), False, other)]

    pieces = [(0, None, False, hidden), (0, (), True, own)]
    pieces += [(rows, (0, 2), True, both_1), (rows, (1, 3), False, early[0])]
    pieces += with_core(2, 0, near_2, early[1]) + with_core(2, 2, far_2, early[2])
    pieces += with_core(3, 0, near_3, early[3])
    pieces += with_core(3, 2, far_3, flip(far_3, "tp", 1))
    *first, w_down = run_experts(
        ranks, pieces, w_gate, w_up, w_down, 4 * rows, columns, top, True
    )
    early = [flip(array, "tp", 1) for array in (near_late, far_late, near_odds)]
    first, far_odds_y, far_odds_x, early = tie((first, far_odds_y, far_odds_x, early))

    def add_core(cross, side, sent, kept):
        return total_of(sent, flip(cross, "tp", 1)), total_of(kept, flip(side, "tp", 1))

    sent, kept = add_core(*first)
    last = [flip(array, "tp", 1) for array in (far_odds_y, far_odds_x)]
    sent, kept, last, page = tie((sent, kept, last, page))
    over_23 = flip(cut(sent, 2, 2), "tp", 2)
    over_1 = flip(jnp.concatenate([cut(kept, 1, 1), cut(sent, 1, 1)], axis=1), "ep", 1)
    if levels > 1:
        page = page_hop(page, 1)
    pieces = with_core(0, 0, near_late, early[0]) + with_core(0, 2, far_late, early[1])
    pieces += with_core(len(late), 0, near_odds, early[2])
    pieces += with_core(len(late), 2, far_odds_y, last[0])
    pieces += with_core(len(late) + half, 2, far_odds_x, last[1])
    second = [
        *run_experts(
            ranks, pieces, w_gate, w_up, w_down, 2 * len(late) * rows, columns, top, False
        )
    ]
    second, over_23, over_1 = tie((second, over_23, over_1))
    late_sent, late_kept = add_core(*second)

    over_y = flip(cut(late_sent, len(late), half), "tp", 2)
    over_x = flip(cut(late_sent, len(late) + half, rest), "ep", 1)
    over_3 = flip(total_of(cut(kept, 3, 1), cut(over_23, 1, 1)), "ep", 1)
    zero = flip(total_of(cut(sent, 0, 1), over_1[:, columns:]), "tp", 2)
    attended = attend_traded(
        ranks, lengths, swap_slot, swap_mask, queries, page, attended, groups
    )
    over_y, over_x, over_3, zero, attended = tie((over_y, over_x, over_3, zero, attended))
    odd = total_of(
        cut(late_kept, len(late), len(late)), jnp.pad(over_y, ((0, rest * rows), (0, 0)))
    )
    odd = flip(odd, "ep", 1)
    even = total_of(cut(late_sent, 0, len(late)), jnp.pad(over_x, ((half * rows, 0), (0, 0))))
    even = flip(even, "tp", 2)
    back = [flip(total_of(cut(kept, 2, 1), cut(over_23, 0, 1), over_3), "ep", 2)]
    even = total_of(cut(late_kept, 0, len(late)), even, odd)
    back += [flip(cut(even, i, 1), "ep", 2 * m) for i, m in enumerate(late)]
    moe_out = total_of(cut(kept, 0, 1), over_1[:, :columns], zero, *back)
    return attended, moe_out


def solution(mesh):
    in_specs = (
        P(("ep", "tp"), None, None),
        P(("ep", "tp"), None, None),
        P(),
        P(),
        P(),
        P("ep", None),
        P("ep", None),
        P("ep", None),
        P("ep", None, "tp"),
        P("ep", None, "tp"),
        P("ep", "tp", None),
    )
    out_specs = (P(("ep", "tp"), None, None), P("ep", "tp"))
    return jax.shard_map(local, mesh=mesh, in_specs=in_specs, out_specs=out_specs, check_vma=False)
```

```python
import functools
import math

import jax
import jax.numpy as jnp
from jax import lax
from jax.experimental import pallas as pl
from jax.experimental.pallas import tpu as pltpu
from jax.sharding import PartitionSpec as P

LAT = 512
SCORE_SCALE = 192.0 ** (-0.5)
MASK_FLOOR = -1e30
ROWS = 512
MIB = 1 << 20


def flip(block, axis, apart):
    count = lax.axis_size(axis)
    return lax.ppermute(block, axis, [(i, i ^ apart) for i in range(count)])


def attend_body(query, page, length):
    scores = (
        lax.dot_general(query, page, (((0,), (0,)), ((), ())), preferred_element_type=jnp.float32)
        * SCORE_SCALE
    )
    live = lax.broadcasted_iota(jnp.int32, scores.shape, 1) < length
    scores = jnp.where(live, scores, MASK_FLOOR)
    top = jnp.max(scores, axis=1, keepdims=True)
    weight = jnp.where(live, jnp.exp(scores - top), 0.0)
    total = jnp.sum(weight, axis=1, keepdims=True)
    blended = lax.dot_general(
        weight.astype(jnp.bfloat16),
        page[:LAT],
        (((1,), (1,)), ((), ())),
        preferred_element_type=jnp.float32,
    )
    return (blended / total).astype(jnp.bfloat16)


def in_hbm(array):
    return pltpu.with_memory_space_constraint(array, pltpu.HBM)


def in_vmem(array):
    return pltpu.with_memory_space_constraint(array, pltpu.VMEM)


ANYWHERE = pl.BlockSpec(memory_space=pl.ANY)
IN_VMEM = pl.BlockSpec(memory_space=pltpu.VMEM)
IN_SMEM = pl.BlockSpec(memory_space=pltpu.SMEM)


def device_of(ranks_ref, groups, mask=0):
    return (ranks_ref[0] ^ mask) * groups + ranks_ref[1]


def pick_kernel(groups, ranks_ref, slots_ref, ids_ref, gates_ref, hidden_ref, pages_ref, near_ref, both_ref, page_ref, sems):
    rows = hidden_ref.shape[0]
    columns = hidden_ref.shape[1] // groups

    def quarter(part):
        start = pl.multiple_of((ranks_ref[1] ^ part) * columns, 128)
        return hidden_ref.at[:, pl.ds(start, columns)]

    copies = [
        (quarter(0), near_ref.at[:, pl.ds(0, columns)]),
        (quarter(0), both_ref.at[:, pl.ds(0, columns)]),
        (quarter(2), both_ref.at[:, pl.ds(columns, columns)]),
        (pages_ref.at[slots_ref[device_of(ranks_ref, groups)]], page_ref),
    ]
    copies = [pltpu.make_async_copy(*pair, sems.at[i]) for i, pair in enumerate(copies)]
    for one in copies:
        one.start()
    gates = gates_ref[...]
    high = gates.astype(jnp.bfloat16).astype(jnp.float32)
    middle = (gates - high).astype(jnp.bfloat16).astype(jnp.float32)
    low = gates - high - middle
    top = gates.shape[0]
    table = jnp.concatenate(
        [ids_ref[...].astype(jnp.float32), high, middle, low, jnp.zeros((128 - 4 * top, rows), jnp.float32)],
        axis=0,
    )
    table = jnp.concatenate([table, jnp.zeros((128, 128 - rows), jnp.float32)], axis=1)
    table = table.T[:rows].astype(jnp.bfloat16)
    near_ref[:, columns:] = table
    both_ref[:, 2 * columns :] = table
    for one in copies:
        one.wait()


def pick(ranks, swap_slot, expert_ids, gate_weights, hidden, pages, groups):
    rows, width = hidden.shape
    columns = width // groups
    return pl.pallas_call(
        functools.partial(pick_kernel, groups),
        out_shape=(
            pltpu.VMEM((rows, columns + 128), jnp.bfloat16),
            pltpu.VMEM((rows, 2 * columns + 128), jnp.bfloat16),
            pltpu.VMEM(pages.shape[1:], jnp.bfloat16),
        ),
        in_specs=[IN_SMEM, IN_SMEM, IN_VMEM, IN_VMEM, ANYWHERE, ANYWHERE],
        out_specs=(IN_VMEM, IN_VMEM, IN_VMEM),
        scratch_shapes=[pltpu.SemaphoreType.DMA((4,))],
        compiler_params=pltpu.CompilerParams(vmem_limit_bytes=2 * MIB),
        name="pick",
    )(
        ranks,
        in_hbm(swap_slot),
        in_hbm(expert_ids.T),
        in_hbm(gate_weights.T),
        in_hbm(hidden),
        in_hbm(pages),
    )


def attend_part(ranks, lengths, queries, pages, groups, first, some, before=None):
    count, width, heads = queries.shape
    slots = pages.shape[2]
    each = math.gcd(some, 2)
    skip = first // each

    def kernel(ranks_ref, lengths_ref, query_ref, page_ref, *refs):
        start = device_of(ranks_ref, groups) * count + first + pl.program_id(0) * each
        for i in range(each):
            refs[-1][i] = attend_body(query_ref[i], page_ref[i], lengths_ref[start + i])

    earlier = [] if before is None else [before]
    return pl.pallas_call(
        kernel,
        out_shape=jax.ShapeDtypeStruct((count, heads, LAT), jnp.bfloat16),
        grid_spec=pltpu.PrefetchScalarGridSpec(
            num_scalar_prefetch=2,
            grid=(some // each,),
            in_specs=[
                pl.BlockSpec((each, width, heads), lambda i, *_: (skip + i, 0, 0)),
                pl.BlockSpec((each, width, slots), lambda i, *_: (skip + i, 0, 0)),
            ]
            + [ANYWHERE] * len(earlier),
            out_specs=pl.BlockSpec((each, heads, LAT), lambda i, *_: (skip + i, 0, 0)),
        ),
        input_output_aliases={4: 0} if earlier else {},
        compiler_params=pltpu.CompilerParams(vmem_limit_bytes=8 * MIB),
        cost_estimate=pl.CostEstimate(
            flops=2 * some * heads * slots * (width + LAT),
            bytes_accessed=2 * some * (heads * (width + LAT) + slots * width),
            transcendentals=some * heads * slots,
        ),
        name="attend_local",
    )(ranks, lengths, in_hbm(queries), in_hbm(pages), *earlier)


def load_kernel(*refs):
    count = len(refs) // 2
    copies = [
        pltpu.make_async_copy(refs[i], refs[count + i], refs[-1].at[i]) for i in range(count)
    ]
    for one in copies:
        one.start()
    for one in copies:
        one.wait()


def load(*arrays):
    return pl.pallas_call(
        load_kernel,
        out_shape=[pltpu.VMEM(w.shape, w.dtype) for w in arrays],
        in_specs=[ANYWHERE] * len(arrays),
        out_specs=[ANYWHERE] * len(arrays),
        scratch_shapes=[pltpu.SemaphoreType.DMA((len(arrays),))],
        compiler_params=pltpu.CompilerParams(vmem_limit_bytes=MIB),
        cost_estimate=pl.CostEstimate(
            flops=0, bytes_accessed=sum(2 * math.prod(w.shape) for w in arrays), transcendentals=0
        ),
        name="load",
    )(*[in_hbm(w) for w in arrays])


def attend_traded_kernel(
    groups, ranks_ref, lengths_ref, slots_ref, mask_ref, query_ref, page_ref, old_ref, out_ref
):
    partner = device_of(ranks_ref, groups, mask_ref[0])
    length = lengths_ref[partner * old_ref.shape[0] + slots_ref[partner]]
    out_ref[0] = attend_body(query_ref[0], page_ref[...], length)


def attend_traded(ranks, lengths, swap_slot, swap_mask, queries, page, attended, groups):
    _, width, heads = queries.shape
    slots = page.shape[1]

    def mine(i, ranks_ref, lengths_ref, slots_ref, mask_ref):
        return slots_ref[device_of(ranks_ref, groups)], 0, 0

    return pl.pallas_call(
        functools.partial(attend_traded_kernel, groups),
        out_shape=jax.ShapeDtypeStruct(attended.shape, attended.dtype),
        grid_spec=pltpu.PrefetchScalarGridSpec(
            num_scalar_prefetch=4,
            grid=(1,),
            in_specs=[
                pl.BlockSpec((1, width, heads), mine),
                pl.BlockSpec((width, slots), lambda i, *_: (0, 0)),
                ANYWHERE,
            ],
            out_specs=pl.BlockSpec((1, heads, LAT), mine),
        ),
        input_output_aliases={6: 0},
        compiler_params=pltpu.CompilerParams(vmem_limit_bytes=4 * MIB),
        cost_estimate=pl.CostEstimate(
            flops=2 * heads * slots * (width + LAT),
            bytes_accessed=2 * (heads * (width + LAT) + slots * width),
            transcendentals=heads * slots,
        ),
        name="attend_traded",
    )(ranks, lengths, swap_slot, swap_mask, in_hbm(queries), page, attended)


def experts_kernel(
    top,
    fetch,
    ranks_ref,
    pieces,
    gate_ref,
    up_ref,
    source_ref,
    given_ref,
    kept_ref,
    *refs,
):
    if fetch:
        down_ref, *refs = refs
    else:
        down_ref = source_ref
    rows_ref, meta_ref, inner_ref, table_ref, sems, down_sem = refs
    experts, _, units = gate_ref.shape
    total_rows = rows_ref.shape[0]
    quarter = kept_ref.shape[1]
    ep_rank, tp_rank = ranks_ref[0], ranks_ref[1]

    def columns_of(part):
        return pl.ds(pl.multiple_of((tp_rank ^ part) * quarter, 128), quarter)

    copies = []
    for start, parts, has_meta, piece in pieces:
        rows = pl.ds(start, piece.shape[0])
        if parts is None:
            copies.append((piece, rows_ref.at[rows, :]))
            continue
        for i, part in enumerate(parts):
            copies.append(
                (piece.at[:, pl.ds(i * quarter, quarter)], rows_ref.at[rows, columns_of(part)])
            )
        if has_meta:
            copies.append((piece.at[:, pl.ds(piece.shape[1] - 128, 128)], meta_ref.at[rows, :]))
    copies = [
        pltpu.make_async_copy(source, target, sems.at[i])
        for i, (source, target) in enumerate(copies)
    ]
    for one in copies:
        one.start()
    if fetch:
        down_copy = pltpu.make_async_copy(source_ref, down_ref, down_sem)
        down_copy.start()
    for one in copies:
        one.wait()
    meta = meta_ref[...].astype(jnp.float32)
    gates = sum(pltpu.roll(meta, 128 - i * top, 1) for i in range(1, 4))
    lane = lax.broadcasted_iota(jnp.int32, meta.shape, 1)
    for e in range(experts):
        name = (ep_rank * experts + e).astype(jnp.float32)
        mine = jnp.where((lane < top) & (meta == name), gates, 0.0)
        table_ref[:, e : e + 1] = jnp.sum(mine, axis=1, keepdims=True)
    stride = math.gcd(total_rows, ROWS)
    for e in range(experts):

        @pl.loop(0, total_rows // stride)
        def _(step):
            at = pl.ds(pl.multiple_of(step * stride, stride), stride)
            rows = rows_ref[at, :]
            gate = jnp.dot(rows, gate_ref[e], preferred_element_type=jnp.float32)
            up = jnp.dot(rows, up_ref[e], preferred_element_type=jnp.float32)
            act = gate / (1.0 + jnp.exp(-gate)) * up * table_ref[at, e : e + 1]
            inner_ref[at, e * units : (e + 1) * units] = act.astype(jnp.bfloat16)

    if fetch:
        down_copy.wait()
    for part, out_ref, half in ((3, given_ref, 0), (1, given_ref, 1), (2, kept_ref, 0), (0, kept_ref, 1)):

        @pl.loop(0, total_rows // stride)
        def _(step):
            at = pl.ds(pl.multiple_of(step * stride, stride), stride)
            to = pl.ds(pl.multiple_of(half * total_rows + step * stride, stride), stride)
            weight = down_ref[:, :, columns_of(part)].reshape(experts * units, quarter)
            out_ref[to, :] = jnp.dot(
                inner_ref[at, :], weight, preferred_element_type=jnp.float32
            ).astype(jnp.bfloat16)


def run_experts(ranks, pieces, w_gate, w_up, w_down, rows, columns, top, fetch):
    experts, width, units = w_gate.shape
    arrays = [piece for *_, piece in pieces]
    count = sum(1 if parts is None else len(parts) + has_meta for _, parts, has_meta, _ in pieces)

    def kernel(ranks_ref, refs, *others):
        named = [(*about[:3], ref) for about, ref in zip(pieces, refs)]
        experts_kernel(top, fetch, ranks_ref, named, *others)

    need = 2 * rows * (width + 128 + experts * units) + 512 * rows
    down_shape = [pltpu.VMEM(w_down.shape, w_down.dtype)] if fetch else []
    return pl.pallas_call(
        kernel,
        out_shape=[pltpu.VMEM((2 * rows, columns), jnp.bfloat16)] * 2 + down_shape,
        in_specs=[
            IN_SMEM,
            [ANYWHERE] * len(arrays),
            IN_VMEM,
            IN_VMEM,
            ANYWHERE if fetch else IN_VMEM,
        ],
        out_specs=[IN_VMEM] * (2 + len(down_shape)),
        scratch_shapes=[
            pltpu.VMEM((rows, width), jnp.bfloat16),
            pltpu.VMEM((rows, 128), jnp.bfloat16),
            pltpu.VMEM((rows, experts * units), jnp.bfloat16),
            pltpu.VMEM((rows, 128), jnp.float32),
            pltpu.SemaphoreType.DMA((count,)),
            pltpu.SemaphoreType.DMA,
        ],
        compiler_params=pltpu.CompilerParams(vmem_limit_bytes=need + 6 * MIB),
        cost_estimate=pl.CostEstimate(
            flops=6 * rows * width * units * experts,
            bytes_accessed=4 * rows * width,
            transcendentals=rows * units * experts,
        ),
        name="experts",
    )(
        ranks,
        arrays,
        in_vmem(w_gate),
        in_vmem(w_up),
        in_hbm(w_down) if fetch else in_vmem(w_down),
    )


def total_of(*terms):
    value = terms[0].astype(jnp.float32)
    for term in terms[1:]:
        value = value + term.astype(jnp.float32)
    return value.astype(jnp.bfloat16)


def local(
    cache_pages,
    queries,
    lengths,
    swap_slot,
    swap_mask,
    hidden,
    expert_ids,
    gate_weights,
    w_gate,
    w_up,
    w_down,
):
    groups = lax.axis_size("tp")
    ep_size = lax.axis_size("ep")
    ranks = jnp.stack([lax.axis_index("ep"), lax.axis_index("tp")]).astype(jnp.int32)
    mask_value = swap_mask[0]
    columns = hidden.shape[1] // groups
    top = expert_ids.shape[1]
    cache_pages = jnp.swapaxes(cache_pages, 1, 2)
    queries = jnp.swapaxes(queries, 1, 2)

    rows = hidden.shape[0]
    pairs = ep_size // 2
    late = list(range(2, pairs))
    half = len(late) // 2
    rest = len(late) - half
    levels = ep_size.bit_length() - 1
    tie = lax.optimization_barrier

    def cut(array, start, count):
        return lax.slice_in_dim(array, start * rows, (start + count) * rows, axis=0)

    def bare(array):
        return array[:, :columns]

    def page_take(page, swapped, level):
        bit = jnp.bitwise_and(jnp.right_shift(mask_value, level), 1) == 1
        return jnp.where(bit, swapped, page)

    def page_hop(page, level):
        return page_take(page, flip(page, "ep", 1 << level), level)

    def page_far(page):
        for level in range(levels - 1, 2, -1):
            page = page_hop(page, level)
        return flip(page, "ep", 4) if levels > 2 else page, page

    own, both, page = pick(
        ranks, swap_slot, expert_ids, gate_weights, hidden, cache_pages, groups
    )
    late_pieces = [flip(own, "ep", 2 * m) for m in late]
    near_2 = flip(own, "ep", 2)
    both_1 = flip(both, "ep", 1)

    near_2, w_gate, w_up = tie((near_2, w_gate, w_up))
    far_2 = flip(bare(near_2), "tp", 2)
    near_3 = flip(near_2, "ep", 1)
    w_gate, w_up = load(w_gate, w_up)
    far_2, near_3, w_gate, w_up, page, both_1, *late_pieces = tie(
        (far_2, near_3, w_gate, w_up, page, both_1, *late_pieces)
    )
    upper, lower = jnp.split(page, 2, axis=0)
    upper_far, upper = page_far(upper)
    far_3 = flip(bare(near_3), "tp", 2)

    near_late = jnp.concatenate(late_pieces, axis=0)
    far_late = flip(bare(near_late), "tp", 2)
    near_odds = flip(near_late, "ep", 1)
    early = [flip(array, "tp", 1) for array in (both_1, near_2, far_2, near_3)]

    def with_core(start, part, array, other):
        start = start * rows
        return [(start, (part,), part == 0, array), (start, (part ^ 1,), False, other)]

    pieces = [(0, None, False, hidden), (0, (), True, own)]
    pieces += [(rows, (0, 2), True, both_1), (rows, (1, 3), False, early[0])]
    pieces += with_core(2, 0, near_2, early[1]) + with_core(2, 2, far_2, early[2])
    pieces += with_core(3, 0, near_3, early[3])
    pieces += with_core(3, 2, far_3, flip(far_3, "tp", 1))
    *first, w_down = run_experts(
        ranks, pieces, w_gate, w_up, w_down, 4 * rows, columns, top, True
    )
    first, far_late, near_odds, upper_far = tie((first, far_late, near_odds, upper_far))

    def add_core(given, own):
        total = total_of(own, flip(given, "tp", 1))
        return jnp.split(total, 2, axis=0)

    far_odds_y = flip(bare(cut(near_odds, 0, half)), "tp", 2)
    far_odds_x = flip(cut(far_late, half, rest), "ep", 1)
    sent, kept = add_core(*first)
    far_odds_y, far_odds_x, sent, kept, lower, near_late, far_late, near_odds = tie(
        (far_odds_y, far_odds_x, sent, kept, lower, near_late, far_late, near_odds)
    )
    early = [flip(array, "tp", 1) for array in (near_late, far_late, near_odds)]
    last = [flip(array, "tp", 1) for array in (far_odds_y, far_odds_x)]
    over_23 = flip(cut(sent, 2, 2), "tp", 2)
    over_1 = flip(jnp.concatenate([cut(kept, 1, 1), cut(sent, 1, 1)], axis=1), "ep", 1)
    lower_far, lower = page_far(lower)

    pieces = with_core(0, 0, near_late, early[0]) + with_core(0, 2, far_late, early[1])
    pieces += with_core(len(late), 0, near_odds, early[2])
    pieces += with_core(len(late), 2, far_odds_y, last[0])
    pieces += with_core(len(late) + half, 2, far_odds_x, last[1])
    second = [
        *run_experts(
            ranks, pieces, w_gate, w_up, w_down, 2 * len(late) * rows, columns, top, False
        )
    ]
    second, over_23, over_1, lower_far = tie((second, over_23, over_1, lower_far))
    page = jnp.concatenate([upper, lower], axis=0)
    page = page_take(page, jnp.concatenate([upper_far, lower_far], axis=0), 2)
    late_sent, late_kept = add_core(*second)
    over_3 = flip(total_of(cut(kept, 3, 1), cut(over_23, 1, 1)), "ep", 1)
    zero = flip(total_of(cut(sent, 0, 1), over_1[:, columns:]), "tp", 2)
    late_sent, late_kept, queries, page = tie((late_sent, late_kept, queries, page))

    over_y = flip(cut(late_sent, len(late), half), "tp", 2)
    over_x = flip(cut(late_sent, len(late) + half, rest), "ep", 1)
    if levels > 1:
        page = page_hop(page, 1)
    some = queries.shape[0] // 2
    attended = attend_part(ranks, lengths, queries, cache_pages, groups, 0, some)
    over_y, over_x, attended = tie((over_y, over_x, attended))
    odd = total_of(
        cut(late_kept, len(late), len(late)), jnp.pad(over_y, ((0, rest * rows), (0, 0)))
    )
    odd = flip(odd, "ep", 1)
    even = total_of(cut(late_sent, 0, len(late)), jnp.pad(over_x, ((half * rows, 0), (0, 0))))
    even = flip(even, "tp", 2)
    attended = attend_part(
        ranks, lengths, queries, cache_pages, groups, some, queries.shape[0] - some, attended
    )
    odd, even, over_3, attended, page = tie((odd, even, over_3, attended, page))
    even = total_of(cut(late_kept, 0, len(late)), even, odd)
    back = [flip(cut(even, i, 1), "ep", 2 * m) for i, m in enumerate(late)]
    back.append(flip(total_of(cut(kept, 2, 1), cut(over_23, 0, 1), over_3), "ep", 2))
    page = page_hop(page, 0)
    attended = attend_traded(
        ranks, lengths, swap_slot, swap_mask, queries, page, attended, groups
    )
    *back, attended = tie((*back, attended))
    moe_out = total_of(cut(kept, 0, 1), over_1[:, :columns], zero, *back)
    return attended, moe_out


def solution(mesh):
    in_specs = (
        P(("ep", "tp"), None, None),
        P(("ep", "tp"), None, None),
        P(),
        P(),
        P(),
        P("ep", None),
        P("ep", None),
        P("ep", None),
        P("ep", None, "tp"),
        P("ep", None, "tp"),
        P("ep", "tp", None),
    )
    out_specs = (P(("ep", "tp"), None, None), P("ep", "tp"))
    return jax.shard_map(local, mesh=mesh, in_specs=in_specs, out_specs=out_specs, check_vma=False)
```

```python
import functools
import math

import jax
import jax.numpy as jnp
from jax import lax
from jax.experimental import pallas as pl
from jax.experimental.pallas import tpu as pltpu
from jax.sharding import PartitionSpec as P

LAT = 512
SCORE_SCALE = 192.0 ** (-0.5)
MASK_FLOOR = -1e30
ROWS = 512
MIB = 1 << 20


def flip(block, axis, apart):
    count = lax.axis_size(axis)
    return lax.ppermute(block, axis, [(i, i ^ apart) for i in range(count)])


def attend_body(query, page, length):
    scores = (
        lax.dot_general(query, page, (((0,), (0,)), ((), ())), preferred_element_type=jnp.float32)
        * SCORE_SCALE
    )
    live = lax.broadcasted_iota(jnp.int32, scores.shape, 1) < length
    scores = jnp.where(live, scores, MASK_FLOOR)
    top = jnp.max(scores, axis=1, keepdims=True)
    weight = jnp.where(live, jnp.exp(scores - top), 0.0)
    total = jnp.sum(weight, axis=1, keepdims=True)
    blended = lax.dot_general(
        weight.astype(jnp.bfloat16),
        page[:LAT],
        (((1,), (1,)), ((), ())),
        preferred_element_type=jnp.float32,
    )
    return (blended / total).astype(jnp.bfloat16)


def in_hbm(array):
    return pltpu.with_memory_space_constraint(array, pltpu.HBM)


def in_vmem(array):
    return pltpu.with_memory_space_constraint(array, pltpu.VMEM)


ANYWHERE = pl.BlockSpec(memory_space=pl.ANY)
IN_VMEM = pl.BlockSpec(memory_space=pltpu.VMEM)
IN_SMEM = pl.BlockSpec(memory_space=pltpu.SMEM)


def device_of(ranks_ref, groups, mask=0):
    return (ranks_ref[0] ^ mask) * groups + ranks_ref[1]


def pick_kernel(groups, ranks_ref, slots_ref, ids_ref, gates_ref, hidden_ref, pages_ref, near_ref, both_ref, page_ref, sems):
    rows = hidden_ref.shape[0]
    columns = hidden_ref.shape[1] // groups

    def quarter(part):
        start = pl.multiple_of((ranks_ref[1] ^ part) * columns, 128)
        return hidden_ref.at[:, pl.ds(start, columns)]

    copies = [
        (quarter(0), near_ref.at[:, pl.ds(0, columns)]),
        (quarter(0), both_ref.at[:, pl.ds(0, columns)]),
        (quarter(2), both_ref.at[:, pl.ds(columns, columns)]),
        (pages_ref.at[slots_ref[device_of(ranks_ref, groups)]], page_ref),
    ]
    copies = [pltpu.make_async_copy(*pair, sems.at[i]) for i, pair in enumerate(copies)]
    for one in copies:
        one.start()
    gates = gates_ref[...]
    high = gates.astype(jnp.bfloat16).astype(jnp.float32)
    middle = (gates - high).astype(jnp.bfloat16).astype(jnp.float32)
    low = gates - high - middle
    top = gates.shape[0]
    table = jnp.concatenate(
        [ids_ref[...].astype(jnp.float32), high, middle, low, jnp.zeros((128 - 4 * top, rows), jnp.float32)],
        axis=0,
    )
    table = jnp.concatenate([table, jnp.zeros((128, 128 - rows), jnp.float32)], axis=1)
    table = table.T[:rows].astype(jnp.bfloat16)
    near_ref[:, columns:] = table
    both_ref[:, 2 * columns :] = table
    for one in copies:
        one.wait()


def pick(ranks, swap_slot, expert_ids, gate_weights, hidden, pages, groups):
    rows, width = hidden.shape
    columns = width // groups
    return pl.pallas_call(
        functools.partial(pick_kernel, groups),
        out_shape=(
            pltpu.VMEM((rows, columns + 128), jnp.bfloat16),
            pltpu.VMEM((rows, 2 * columns + 128), jnp.bfloat16),
            pltpu.VMEM(pages.shape[1:], jnp.bfloat16),
        ),
        in_specs=[IN_SMEM, IN_SMEM, IN_VMEM, IN_VMEM, ANYWHERE, ANYWHERE],
        out_specs=(IN_VMEM, IN_VMEM, IN_VMEM),
        scratch_shapes=[pltpu.SemaphoreType.DMA((4,))],
        compiler_params=pltpu.CompilerParams(vmem_limit_bytes=2 * MIB),
        name="pick",
    )(
        ranks,
        in_hbm(swap_slot),
        in_hbm(expert_ids.T),
        in_hbm(gate_weights.T),
        in_hbm(hidden),
        in_hbm(pages),
    )


def attend_part(ranks, lengths, queries, pages, groups, first, some, before=None):
    count, width, heads = queries.shape
    slots = pages.shape[2]
    each = math.gcd(some, 2)
    skip = first // each

    def kernel(ranks_ref, lengths_ref, query_ref, page_ref, *refs):
        start = device_of(ranks_ref, groups) * count + first + pl.program_id(0) * each
        for i in range(each):
            refs[-1][i] = attend_body(query_ref[i], page_ref[i], lengths_ref[start + i])

    earlier = [] if before is None else [before]
    return pl.pallas_call(
        kernel,
        out_shape=jax.ShapeDtypeStruct((count, heads, LAT), jnp.bfloat16),
        grid_spec=pltpu.PrefetchScalarGridSpec(
            num_scalar_prefetch=2,
            grid=(some // each,),
            in_specs=[
                pl.BlockSpec((each, width, heads), lambda i, *_: (skip + i, 0, 0)),
                pl.BlockSpec((each, width, slots), lambda i, *_: (skip + i, 0, 0)),
            ]
            + [ANYWHERE] * len(earlier),
            out_specs=pl.BlockSpec((each, heads, LAT), lambda i, *_: (skip + i, 0, 0)),
        ),
        input_output_aliases={4: 0} if earlier else {},
        compiler_params=pltpu.CompilerParams(vmem_limit_bytes=8 * MIB),
        cost_estimate=pl.CostEstimate(
            flops=2 * some * heads * slots * (width + LAT),
            bytes_accessed=2 * some * (heads * (width + LAT) + slots * width),
            transcendentals=some * heads * slots,
        ),
        name="attend_local",
    )(ranks, lengths, in_hbm(queries), in_hbm(pages), *earlier)


def load_kernel(*refs):
    count = len(refs) // 2
    copies = [
        pltpu.make_async_copy(refs[i], refs[count + i], refs[-1].at[i]) for i in range(count)
    ]
    for one in copies:
        one.start()
    for one in copies:
        one.wait()


def load(*arrays):
    return pl.pallas_call(
        load_kernel,
        out_shape=[pltpu.VMEM(w.shape, w.dtype) for w in arrays],
        in_specs=[ANYWHERE] * len(arrays),
        out_specs=[ANYWHERE] * len(arrays),
        scratch_shapes=[pltpu.SemaphoreType.DMA((len(arrays),))],
        compiler_params=pltpu.CompilerParams(vmem_limit_bytes=MIB),
        cost_estimate=pl.CostEstimate(
            flops=0, bytes_accessed=sum(2 * math.prod(w.shape) for w in arrays), transcendentals=0
        ),
        name="load",
    )(*[in_hbm(w) for w in arrays])


def attend_traded_kernel(
    groups, ranks_ref, lengths_ref, slots_ref, mask_ref, query_ref, page_ref, old_ref, out_ref
):
    partner = device_of(ranks_ref, groups, mask_ref[0])
    length = lengths_ref[partner * old_ref.shape[0] + slots_ref[partner]]
    out_ref[0] = attend_body(query_ref[0], page_ref[...], length)


def attend_traded(ranks, lengths, swap_slot, swap_mask, queries, page, attended, groups):
    _, width, heads = queries.shape
    slots = page.shape[1]

    def mine(i, ranks_ref, lengths_ref, slots_ref, mask_ref):
        return slots_ref[device_of(ranks_ref, groups)], 0, 0

    return pl.pallas_call(
        functools.partial(attend_traded_kernel, groups),
        out_shape=jax.ShapeDtypeStruct(attended.shape, attended.dtype),
        grid_spec=pltpu.PrefetchScalarGridSpec(
            num_scalar_prefetch=4,
            grid=(1,),
            in_specs=[
                pl.BlockSpec((1, width, heads), mine),
                pl.BlockSpec((width, slots), lambda i, *_: (0, 0)),
                ANYWHERE,
            ],
            out_specs=pl.BlockSpec((1, heads, LAT), mine),
        ),
        input_output_aliases={6: 0},
        compiler_params=pltpu.CompilerParams(vmem_limit_bytes=4 * MIB),
        cost_estimate=pl.CostEstimate(
            flops=2 * heads * slots * (width + LAT),
            bytes_accessed=2 * (heads * (width + LAT) + slots * width),
            transcendentals=heads * slots,
        ),
        name="attend_traded",
    )(ranks, lengths, swap_slot, swap_mask, in_hbm(queries), page, attended)


def experts_kernel(
    top,
    fetch,
    ranks_ref,
    pieces,
    gate_ref,
    up_ref,
    source_ref,
    given_ref,
    kept_ref,
    *refs,
):
    if fetch:
        down_ref, *refs = refs
    else:
        down_ref = source_ref
    rows_ref, meta_ref, inner_ref, table_ref, sems, down_sem = refs
    experts, _, units = gate_ref.shape
    total_rows = rows_ref.shape[0]
    quarter = kept_ref.shape[1]
    ep_rank, tp_rank = ranks_ref[0], ranks_ref[1]

    def columns_of(part):
        return pl.ds(pl.multiple_of((tp_rank ^ part) * quarter, 128), quarter)

    copies = []
    for start, parts, has_meta, piece in pieces:
        rows = pl.ds(start, piece.shape[0])
        if parts is None:
            copies.append((piece, rows_ref.at[rows, :]))
            continue
        for i, part in enumerate(parts):
            copies.append(
                (piece.at[:, pl.ds(i * quarter, quarter)], rows_ref.at[rows, columns_of(part)])
            )
        if has_meta:
            copies.append((piece.at[:, pl.ds(piece.shape[1] - 128, 128)], meta_ref.at[rows, :]))
    copies = [
        pltpu.make_async_copy(source, target, sems.at[i])
        for i, (source, target) in enumerate(copies)
    ]
    for one in copies:
        one.start()
    if fetch:
        down_copy = pltpu.make_async_copy(source_ref, down_ref, down_sem)
        down_copy.start()
    for one in copies:
        one.wait()
    meta = meta_ref[...].astype(jnp.float32)
    gates = sum(pltpu.roll(meta, 128 - i * top, 1) for i in range(1, 4))
    lane = lax.broadcasted_iota(jnp.int32, meta.shape, 1)
    for e in range(experts):
        name = (ep_rank * experts + e).astype(jnp.float32)
        mine = jnp.where((lane < top) & (meta == name), gates, 0.0)
        table_ref[:, e : e + 1] = jnp.sum(mine, axis=1, keepdims=True)
    stride = math.gcd(total_rows, ROWS)
    for e in range(experts):

        @pl.loop(0, total_rows // stride)
        def _(step):
            at = pl.ds(pl.multiple_of(step * stride, stride), stride)
            rows = rows_ref[at, :]
            gate = jnp.dot(rows, gate_ref[e], preferred_element_type=jnp.float32)
            up = jnp.dot(rows, up_ref[e], preferred_element_type=jnp.float32)
            act = gate / (1.0 + jnp.exp(-gate)) * up * table_ref[at, e : e + 1]
            inner_ref[at, e * units : (e + 1) * units] = act.astype(jnp.bfloat16)

    if fetch:
        down_copy.wait()
    for part, out_ref, half in ((3, given_ref, 0), (1, given_ref, 1), (2, kept_ref, 0), (0, kept_ref, 1)):

        @pl.loop(0, total_rows // stride)
        def _(step):
            at = pl.ds(pl.multiple_of(step * stride, stride), stride)
            to = pl.ds(pl.multiple_of(half * total_rows + step * stride, stride), stride)
            weight = down_ref[:, :, columns_of(part)].reshape(experts * units, quarter)
            out_ref[to, :] = jnp.dot(
                inner_ref[at, :], weight, preferred_element_type=jnp.float32
            ).astype(jnp.bfloat16)


def run_experts(ranks, pieces, w_gate, w_up, w_down, rows, columns, top, fetch):
    experts, width, units = w_gate.shape
    arrays = [piece for *_, piece in pieces]
    count = sum(1 if parts is None else len(parts) + has_meta for _, parts, has_meta, _ in pieces)

    def kernel(ranks_ref, refs, *others):
        named = [(*about[:3], ref) for about, ref in zip(pieces, refs)]
        experts_kernel(top, fetch, ranks_ref, named, *others)

    need = 2 * rows * (width + 128 + experts * units) + 512 * rows
    down_shape = [pltpu.VMEM(w_down.shape, w_down.dtype)] if fetch else []
    return pl.pallas_call(
        kernel,
        out_shape=[pltpu.VMEM((2 * rows, columns), jnp.bfloat16)] * 2 + down_shape,
        in_specs=[
            IN_SMEM,
            [ANYWHERE] * len(arrays),
            IN_VMEM,
            IN_VMEM,
            ANYWHERE if fetch else IN_VMEM,
        ],
        out_specs=[IN_VMEM] * (2 + len(down_shape)),
        scratch_shapes=[
            pltpu.VMEM((rows, width), jnp.bfloat16),
            pltpu.VMEM((rows, 128), jnp.bfloat16),
            pltpu.VMEM((rows, experts * units), jnp.bfloat16),
            pltpu.VMEM((rows, 128), jnp.float32),
            pltpu.SemaphoreType.DMA((count,)),
            pltpu.SemaphoreType.DMA,
        ],
        compiler_params=pltpu.CompilerParams(vmem_limit_bytes=need + 6 * MIB),
        cost_estimate=pl.CostEstimate(
            flops=6 * rows * width * units * experts,
            bytes_accessed=4 * rows * width,
            transcendentals=rows * units * experts,
        ),
        name="experts",
    )(
        ranks,
        arrays,
        in_vmem(w_gate),
        in_vmem(w_up),
        in_hbm(w_down) if fetch else in_vmem(w_down),
    )


def total_of(*terms):
    value = terms[0].astype(jnp.float32)
    for term in terms[1:]:
        value = value + term.astype(jnp.float32)
    return value.astype(jnp.bfloat16)


def local(
    cache_pages,
    queries,
    lengths,
    swap_slot,
    swap_mask,
    hidden,
    expert_ids,
    gate_weights,
    w_gate,
    w_up,
    w_down,
):
    groups = lax.axis_size("tp")
    ep_size = lax.axis_size("ep")
    ranks = jnp.stack([lax.axis_index("ep"), lax.axis_index("tp")]).astype(jnp.int32)
    mask_value = swap_mask[0]
    columns = hidden.shape[1] // groups
    top = expert_ids.shape[1]
    cache_pages = jnp.swapaxes(cache_pages, 1, 2)
    queries = jnp.swapaxes(queries, 1, 2)

    rows = hidden.shape[0]
    pairs = ep_size // 2
    late = list(range(2, pairs))
    half = len(late) // 2
    rest = len(late) - half
    levels = ep_size.bit_length() - 1
    tie = lax.optimization_barrier

    def cut(array, start, count):
        return lax.slice_in_dim(array, start * rows, (start + count) * rows, axis=0)

    def bare(array):
        return array[:, :columns]

    def page_take(page, swapped, level):
        bit = jnp.bitwise_and(jnp.right_shift(mask_value, level), 1) == 1
        return jnp.where(bit, swapped, page)

    def page_hop(page, level):
        return page_take(page, flip(page, "ep", 1 << level), level)

    def page_far(page):
        for level in range(levels - 1, 2, -1):
            page = page_hop(page, level)
        return flip(page, "ep", 4) if levels > 2 else page, page

    own, both, page = pick(
        ranks, swap_slot, expert_ids, gate_weights, hidden, cache_pages, groups
    )
    late_pieces = [flip(own, "ep", 2 * m) for m in late]
    near_2 = flip(own, "ep", 2)
    both_1 = flip(both, "ep", 1)

    near_2, w_gate, w_up = tie((near_2, w_gate, w_up))
    far_2 = flip(bare(near_2), "tp", 2)
    near_3 = flip(near_2, "ep", 1)
    w_gate, w_up = load(w_gate, w_up)
    far_2, near_3, w_gate, w_up, page, both_1, *late_pieces = tie(
        (far_2, near_3, w_gate, w_up, page, both_1, *late_pieces)
    )
    far_3 = flip(bare(near_3), "tp", 2)

    near_late = jnp.concatenate(late_pieces, axis=0)
    far_late = flip(bare(near_late), "tp", 2)
    near_odds = flip(near_late, "ep", 1)
    early = [flip(array, "tp", 1) for array in (both_1, near_2, far_2, near_3)]

    def with_core(start, part, array, other):
        start = start * rows
        return [(start, (part,), part == 0, array), (start, (part ^ 1,), False, other)]

    pieces = [(0, None, False, hidden), (0, (), True, own)]
    pieces += [(rows, (0, 2), True, both_1), (rows, (1, 3), False, early[0])]
    pieces += with_core(2, 0, near_2, early[1]) + with_core(2, 2, far_2, early[2])
    pieces += with_core(3, 0, near_3, early[3])
    pieces += with_core(3, 2, far_3, flip(far_3, "tp", 1))
    *first, w_down = run_experts(
        ranks, pieces, w_gate, w_up, w_down, 4 * rows, columns, top, True
    )
    first, far_late, near_odds, page = tie((first, far_late, near_odds, page))

    def add_core(given, own):
        total = total_of(own, flip(given, "tp", 1))
        return jnp.split(total, 2, axis=0)

    far_odds_y = flip(bare(cut(near_odds, 0, half)), "tp", 2)
    far_odds_x = flip(cut(far_late, half, rest), "ep", 1)
    sent, kept = add_core(*first)
    swapped = flip(page, "ep", 2)
    far_odds_y, far_odds_x, sent, kept, swapped, near_late, far_late, near_odds = tie(
        (far_odds_y, far_odds_x, sent, kept, swapped, near_late, far_late, near_odds)
    )
    early = [flip(array, "tp", 1) for array in (near_late, far_late, near_odds)]
    last = [flip(array, "tp", 1) for array in (far_odds_y, far_odds_x)]
    over_23 = flip(cut(sent, 2, 2), "tp", 2)
    over_1 = flip(jnp.concatenate([cut(kept, 1, 1), cut(sent, 1, 1)], axis=1), "ep", 1)

    pieces = with_core(0, 0, near_late, early[0]) + with_core(0, 2, far_late, early[1])
    pieces += with_core(len(late), 0, near_odds, early[2])
    pieces += with_core(len(late), 2, far_odds_y, last[0])
    pieces += with_core(len(late) + half, 2, far_odds_x, last[1])
    second = [
        *run_experts(
            ranks, pieces, w_gate, w_up, w_down, 2 * len(late) * rows, columns, top, False
        )
    ]
    second, over_23, over_1 = tie((second, over_23, over_1))
    page = page_take(page, swapped, 1)
    late_sent, late_kept = add_core(*second)
    over_3 = flip(total_of(cut(kept, 3, 1), cut(over_23, 1, 1)), "ep", 1)
    zero = flip(total_of(cut(sent, 0, 1), over_1[:, columns:]), "tp", 2)
    late_sent, late_kept, queries, page = tie((late_sent, late_kept, queries, page))

    over_y = flip(cut(late_sent, len(late), half), "tp", 2)
    over_x = flip(cut(late_sent, len(late) + half, rest), "ep", 1)
    swapped, page = page_far(page)
    count = queries.shape[0]
    starts = [0, count // 4, 3 * count // 4, count]
    attend = functools.partial(attend_part, ranks, lengths, queries, cache_pages, groups)
    attended = attend(starts[0], starts[1])
    over_y, over_x, attended = tie((over_y, over_x, attended))
    odd = total_of(
        cut(late_kept, len(late), len(late)), jnp.pad(over_y, ((0, rest * rows), (0, 0)))
    )
    odd = flip(odd, "ep", 1)
    even = total_of(cut(late_sent, 0, len(late)), jnp.pad(over_x, ((half * rows, 0), (0, 0))))
    even = flip(even, "tp", 2)
    attended = attend(starts[1], starts[2] - starts[1], attended)
    odd, even, over_3, zero, attended, swapped = tie(
        (odd, even, over_3, zero, attended, swapped)
    )
    even = total_of(cut(late_kept, 0, len(late)), even, odd)
    back = [flip(cut(even, i, 1), "ep", 2 * m) for i, m in enumerate(late)]
    back.append(flip(total_of(cut(kept, 2, 1), cut(over_23, 0, 1), over_3), "ep", 2))
    page = page_hop(page_take(page, swapped, 2) if levels > 2 else page, 0)
    attended = attend(starts[2], starts[3] - starts[2], attended)
    attended = attend_traded(
        ranks, lengths, swap_slot, swap_mask, queries, page, attended, groups
    )
    *back, attended = tie((*back, attended))
    moe_out = total_of(cut(kept, 0, 1), over_1[:, :columns], zero, *back)
    return attended, moe_out


def solution(mesh):
    in_specs = (
        P(("ep", "tp"), None, None),
        P(("ep", "tp"), None, None),
        P(),
        P(),
        P(),
        P("ep", None),
        P("ep", None),
        P("ep", None),
        P("ep", None, "tp"),
        P("ep", None, "tp"),
        P("ep", "tp", None),
    )
    out_specs = (P(("ep", "tp"), None, None), P("ep", "tp"))
    return jax.shard_map(local, mesh=mesh, in_specs=in_specs, out_specs=out_specs, check_vma=False)
```

```python
import functools
import math

import jax
import jax.numpy as jnp
from jax import lax
from jax.experimental import pallas as pl
from jax.experimental.pallas import tpu as pltpu
from jax.sharding import PartitionSpec as P

LAT = 512
SCORE_SCALE = 192.0 ** (-0.5)
MASK_FLOOR = -1e30
ROWS = 512
MIB = 1 << 20


def flip(block, axis, apart):
    count = lax.axis_size(axis)
    return lax.ppermute(block, axis, [(i, i ^ apart) for i in range(count)])


def attend_body(query, page, length):
    scores = (
        lax.dot_general(query, page, (((0,), (0,)), ((), ())), preferred_element_type=jnp.float32)
        * SCORE_SCALE
    )
    live = lax.broadcasted_iota(jnp.int32, scores.shape, 1) < length
    scores = jnp.where(live, scores, MASK_FLOOR)
    top = jnp.max(scores, axis=1, keepdims=True)
    weight = jnp.where(live, jnp.exp(scores - top), 0.0)
    total = jnp.sum(weight, axis=1, keepdims=True)
    blended = lax.dot_general(
        weight.astype(jnp.bfloat16),
        page[:LAT],
        (((1,), (1,)), ((), ())),
        preferred_element_type=jnp.float32,
    )
    return (blended / total).astype(jnp.bfloat16)


def in_hbm(array):
    return pltpu.with_memory_space_constraint(array, pltpu.HBM)


def in_vmem(array):
    return pltpu.with_memory_space_constraint(array, pltpu.VMEM)


ANYWHERE = pl.BlockSpec(memory_space=pl.ANY)
IN_VMEM = pl.BlockSpec(memory_space=pltpu.VMEM)
IN_SMEM = pl.BlockSpec(memory_space=pltpu.SMEM)


def device_of(ranks_ref, groups, mask=0):
    return (ranks_ref[0] ^ mask) * groups + ranks_ref[1]


def pick_kernel(groups, ranks_ref, slots_ref, ids_ref, gates_ref, hidden_ref, pages_ref, near_ref, both_ref, page_ref, sems):
    rows = hidden_ref.shape[0]
    columns = hidden_ref.shape[1] // groups

    def quarter(part):
        start = pl.multiple_of((ranks_ref[1] ^ part) * columns, 128)
        return hidden_ref.at[:, pl.ds(start, columns)]

    copies = [
        (quarter(0), near_ref.at[:, pl.ds(0, columns)]),
        (quarter(0), both_ref.at[:, pl.ds(0, columns)]),
        (quarter(2), both_ref.at[:, pl.ds(columns, columns)]),
        (pages_ref.at[slots_ref[device_of(ranks_ref, groups)]], page_ref),
    ]
    copies = [pltpu.make_async_copy(*pair, sems.at[i]) for i, pair in enumerate(copies)]
    for one in copies:
        one.start()
    gates = gates_ref[...]
    high = gates.astype(jnp.bfloat16).astype(jnp.float32)
    middle = (gates - high).astype(jnp.bfloat16).astype(jnp.float32)
    low = gates - high - middle
    top = gates.shape[0]
    table = jnp.concatenate(
        [ids_ref[...].astype(jnp.float32), high, middle, low, jnp.zeros((128 - 4 * top, rows), jnp.float32)],
        axis=0,
    )
    table = jnp.concatenate([table, jnp.zeros((128, 128 - rows), jnp.float32)], axis=1)
    table = table.T[:rows].astype(jnp.bfloat16)
    near_ref[:, columns:] = table
    both_ref[:, 2 * columns :] = table
    for one in copies:
        one.wait()


def pick(ranks, swap_slot, expert_ids, gate_weights, hidden, pages, groups):
    rows, width = hidden.shape
    columns = width // groups
    return pl.pallas_call(
        functools.partial(pick_kernel, groups),
        out_shape=(
            pltpu.VMEM((rows, columns + 128), jnp.bfloat16),
            pltpu.VMEM((rows, 2 * columns + 128), jnp.bfloat16),
            pltpu.VMEM(pages.shape[1:], jnp.bfloat16),
        ),
        in_specs=[IN_SMEM, IN_SMEM, IN_VMEM, IN_VMEM, ANYWHERE, ANYWHERE],
        out_specs=(IN_VMEM, IN_VMEM, IN_VMEM),
        scratch_shapes=[pltpu.SemaphoreType.DMA((4,))],
        compiler_params=pltpu.CompilerParams(vmem_limit_bytes=2 * MIB),
        name="pick",
    )(
        ranks,
        in_hbm(swap_slot),
        in_hbm(expert_ids.T),
        in_hbm(gate_weights.T),
        in_hbm(hidden),
        in_hbm(pages),
    )


def attend_part(ranks, lengths, queries, pages, groups, first, some, before=None):
    count, width, heads = queries.shape
    slots = pages.shape[2]
    each = math.gcd(some, 2)
    skip = first // each

    def kernel(ranks_ref, lengths_ref, query_ref, page_ref, *refs):
        start = device_of(ranks_ref, groups) * count + first + pl.program_id(0) * each
        for i in range(each):
            refs[-1][i] = attend_body(query_ref[i], page_ref[i], lengths_ref[start + i])

    earlier = [] if before is None else [before]
    return pl.pallas_call(
        kernel,
        out_shape=jax.ShapeDtypeStruct((count, heads, LAT), jnp.bfloat16),
        grid_spec=pltpu.PrefetchScalarGridSpec(
            num_scalar_prefetch=2,
            grid=(some // each,),
            in_specs=[
                pl.BlockSpec((each, width, heads), lambda i, *_: (skip + i, 0, 0)),
                pl.BlockSpec((each, width, slots), lambda i, *_: (skip + i, 0, 0)),
            ]
            + [ANYWHERE] * len(earlier),
            out_specs=pl.BlockSpec((each, heads, LAT), lambda i, *_: (skip + i, 0, 0)),
        ),
        input_output_aliases={4: 0} if earlier else {},
        compiler_params=pltpu.CompilerParams(vmem_limit_bytes=8 * MIB),
        cost_estimate=pl.CostEstimate(flops=0, bytes_accessed=0, transcendentals=0),
        name="attend_local",
    )(ranks, lengths, in_hbm(queries), in_hbm(pages), *earlier)


def load_kernel(*refs):
    count = len(refs) // 2
    copies = [
        pltpu.make_async_copy(refs[i], refs[count + i], refs[-1].at[i]) for i in range(count)
    ]
    for one in copies:
        one.start()
    for one in copies:
        one.wait()


def load(*arrays):
    return pl.pallas_call(
        load_kernel,
        out_shape=[pltpu.VMEM(w.shape, w.dtype) for w in arrays],
        in_specs=[ANYWHERE] * len(arrays),
        out_specs=[ANYWHERE] * len(arrays),
        scratch_shapes=[pltpu.SemaphoreType.DMA((len(arrays),))],
        compiler_params=pltpu.CompilerParams(vmem_limit_bytes=MIB),
        cost_estimate=pl.CostEstimate(
            flops=0, bytes_accessed=sum(2 * math.prod(w.shape) for w in arrays), transcendentals=0
        ),
        name="load",
    )(*[in_hbm(w) for w in arrays])


def attend_traded_kernel(
    groups, ranks_ref, lengths_ref, slots_ref, mask_ref, query_ref, page_ref, old_ref, out_ref
):
    partner = device_of(ranks_ref, groups, mask_ref[0])
    length = lengths_ref[partner * old_ref.shape[0] + slots_ref[partner]]
    out_ref[0] = attend_body(query_ref[0], page_ref[...], length)


def attend_traded(ranks, lengths, swap_slot, swap_mask, queries, page, attended, groups):
    _, width, heads = queries.shape
    slots = page.shape[1]

    def mine(i, ranks_ref, lengths_ref, slots_ref, mask_ref):
        return slots_ref[device_of(ranks_ref, groups)], 0, 0

    return pl.pallas_call(
        functools.partial(attend_traded_kernel, groups),
        out_shape=jax.ShapeDtypeStruct(attended.shape, attended.dtype),
        grid_spec=pltpu.PrefetchScalarGridSpec(
            num_scalar_prefetch=4,
            grid=(1,),
            in_specs=[
                pl.BlockSpec((1, width, heads), mine),
                pl.BlockSpec((width, slots), lambda i, *_: (0, 0)),
                ANYWHERE,
            ],
            out_specs=pl.BlockSpec((1, heads, LAT), mine),
        ),
        input_output_aliases={6: 0},
        compiler_params=pltpu.CompilerParams(vmem_limit_bytes=4 * MIB),
        cost_estimate=pl.CostEstimate(
            flops=2 * heads * slots * (width + LAT),
            bytes_accessed=2 * (heads * (width + LAT) + slots * width),
            transcendentals=heads * slots,
        ),
        name="attend_traded",
    )(ranks, lengths, swap_slot, swap_mask, in_hbm(queries), page, attended)


def experts_kernel(
    top,
    fetch,
    ranks_ref,
    pieces,
    gate_ref,
    up_ref,
    source_ref,
    given_ref,
    kept_ref,
    *refs,
):
    if fetch:
        down_ref, *refs = refs
    else:
        down_ref = source_ref
    rows_ref, meta_ref, inner_ref, table_ref, sems, down_sem = refs
    experts, _, units = gate_ref.shape
    total_rows = rows_ref.shape[0]
    quarter = kept_ref.shape[1]
    ep_rank, tp_rank = ranks_ref[0], ranks_ref[1]

    def columns_of(part):
        return pl.ds(pl.multiple_of((tp_rank ^ part) * quarter, 128), quarter)

    copies = []
    for start, parts, has_meta, piece in pieces:
        rows = pl.ds(start, piece.shape[0])
        if parts is None:
            copies.append((piece, rows_ref.at[rows, :]))
            continue
        for i, part in enumerate(parts):
            copies.append(
                (piece.at[:, pl.ds(i * quarter, quarter)], rows_ref.at[rows, columns_of(part)])
            )
        if has_meta:
            copies.append((piece.at[:, pl.ds(piece.shape[1] - 128, 128)], meta_ref.at[rows, :]))
    copies = [
        pltpu.make_async_copy(source, target, sems.at[i])
        for i, (source, target) in enumerate(copies)
    ]
    for one in copies:
        one.start()
    if fetch:
        down_copy = pltpu.make_async_copy(source_ref, down_ref, down_sem)
        down_copy.start()
    for one in copies:
        one.wait()
    meta = meta_ref[...].astype(jnp.float32)
    gates = sum(pltpu.roll(meta, 128 - i * top, 1) for i in range(1, 4))
    lane = lax.broadcasted_iota(jnp.int32, meta.shape, 1)
    for e in range(experts):
        name = (ep_rank * experts + e).astype(jnp.float32)
        mine = jnp.where((lane < top) & (meta == name), gates, 0.0)
        table_ref[:, e : e + 1] = jnp.sum(mine, axis=1, keepdims=True)
    stride = math.gcd(total_rows, ROWS)
    for e in range(experts):

        @pl.loop(0, total_rows // stride)
        def _(step):
            at = pl.ds(pl.multiple_of(step * stride, stride), stride)
            rows = rows_ref[at, :]
            gate = jnp.dot(rows, gate_ref[e], preferred_element_type=jnp.float32)
            up = jnp.dot(rows, up_ref[e], preferred_element_type=jnp.float32)
            act = gate / (1.0 + jnp.exp(-gate)) * up * table_ref[at, e : e + 1]
            inner_ref[at, e * units : (e + 1) * units] = act.astype(jnp.bfloat16)

    if fetch:
        down_copy.wait()
    for part, out_ref, half in ((3, given_ref, 0), (1, given_ref, 1), (2, kept_ref, 0), (0, kept_ref, 1)):

        @pl.loop(0, total_rows // stride)
        def _(step):
            at = pl.ds(pl.multiple_of(step * stride, stride), stride)
            to = pl.ds(pl.multiple_of(half * total_rows + step * stride, stride), stride)
            weight = down_ref[:, :, columns_of(part)].reshape(experts * units, quarter)
            out_ref[to, :] = jnp.dot(
                inner_ref[at, :], weight, preferred_element_type=jnp.float32
            ).astype(jnp.bfloat16)


def run_experts(ranks, pieces, w_gate, w_up, w_down, rows, columns, top, fetch):
    experts, width, units = w_gate.shape
    arrays = [piece for *_, piece in pieces]
    count = sum(1 if parts is None else len(parts) + has_meta for _, parts, has_meta, _ in pieces)

    def kernel(ranks_ref, refs, *others):
        named = [(*about[:3], ref) for about, ref in zip(pieces, refs)]
        experts_kernel(top, fetch, ranks_ref, named, *others)

    need = 2 * rows * (width + 128 + experts * units) + 512 * rows
    down_shape = [pltpu.VMEM(w_down.shape, w_down.dtype)] if fetch else []
    return pl.pallas_call(
        kernel,
        out_shape=[pltpu.VMEM((2 * rows, columns), jnp.bfloat16)] * 2 + down_shape,
        in_specs=[
            IN_SMEM,
            [ANYWHERE] * len(arrays),
            IN_VMEM,
            IN_VMEM,
            ANYWHERE if fetch else IN_VMEM,
        ],
        out_specs=[IN_VMEM] * (2 + len(down_shape)),
        scratch_shapes=[
            pltpu.VMEM((rows, width), jnp.bfloat16),
            pltpu.VMEM((rows, 128), jnp.bfloat16),
            pltpu.VMEM((rows, experts * units), jnp.bfloat16),
            pltpu.VMEM((rows, 128), jnp.float32),
            pltpu.SemaphoreType.DMA((count,)),
            pltpu.SemaphoreType.DMA,
        ],
        compiler_params=pltpu.CompilerParams(vmem_limit_bytes=need + 6 * MIB),
        cost_estimate=pl.CostEstimate(
            flops=0,
            bytes_accessed=0,
            transcendentals=0,
        ),
        name="experts",
    )(
        ranks,
        arrays,
        in_vmem(w_gate),
        in_vmem(w_up),
        in_hbm(w_down) if fetch else in_vmem(w_down),
    )


def total_of(*terms):
    value = terms[0].astype(jnp.float32)
    for term in terms[1:]:
        value = value + term.astype(jnp.float32)
    return value.astype(jnp.bfloat16)


def local(
    cache_pages,
    queries,
    lengths,
    swap_slot,
    swap_mask,
    hidden,
    expert_ids,
    gate_weights,
    w_gate,
    w_up,
    w_down,
):
    groups = lax.axis_size("tp")
    ep_size = lax.axis_size("ep")
    ranks = jnp.stack([lax.axis_index("ep"), lax.axis_index("tp")]).astype(jnp.int32)
    mask_value = swap_mask[0]
    columns = hidden.shape[1] // groups
    top = expert_ids.shape[1]
    cache_pages = jnp.swapaxes(cache_pages, 1, 2)
    queries = jnp.swapaxes(queries, 1, 2)

    rows = hidden.shape[0]
    pairs = ep_size // 2
    late = list(range(2, pairs))
    half = len(late) // 2
    rest = len(late) - half
    levels = ep_size.bit_length() - 1
    tie = lax.optimization_barrier

    def cut(array, start, count):
        return lax.slice_in_dim(array, start * rows, (start + count) * rows, axis=0)

    def bare(array):
        return array[:, :columns]

    def page_take(page, swapped, level):
        bit = jnp.bitwise_and(jnp.right_shift(mask_value, level), 1) == 1
        return jnp.where(bit, swapped, page)

    def page_hop(page, level):
        return page_take(page, flip(page, "ep", 1 << level), level)

    def page_far(page):
        for level in range(levels - 1, 2, -1):
            page = page_hop(page, level)
        return flip(page, "ep", 4) if levels > 2 else page, page

    own, both, page = pick(
        ranks, swap_slot, expert_ids, gate_weights, hidden, cache_pages, groups
    )
    late_pieces = [flip(own, "ep", 2 * m) for m in late]
    near_2 = flip(own, "ep", 2)
    both_1 = flip(both, "ep", 1)

    near_2, w_gate, w_up = tie((near_2, w_gate, w_up))
    far_2 = flip(bare(near_2), "tp", 2)
    near_3 = flip(near_2, "ep", 1)
    w_gate, w_up = load(w_gate, w_up)
    far_2, near_3, w_gate, w_up, page, both_1, *late_pieces = tie(
        (far_2, near_3, w_gate, w_up, page, both_1, *late_pieces)
    )
    far_3 = flip(bare(near_3), "tp", 2)

    near_late = jnp.concatenate(late_pieces, axis=0)
    far_late = flip(bare(near_late), "tp", 2)
    near_odds = flip(near_late, "ep", 1)
    near_23 = flip(jnp.concatenate([near_2, near_3], axis=0), "tp", 1)
    early = [flip(array, "tp", 1) for array in (both_1, far_2)]
    queries, near_23, early = tie((queries, near_23, early))
    count = queries.shape[0]
    attended = attend_part(ranks, lengths, queries, cache_pages, groups, 0, count // 2)
    far_3, far_late, near_late, near_odds, attended = tie(
        (far_3, far_late, near_late, near_odds, attended)
    )
    far_odds_y = flip(bare(cut(near_odds, 0, half)), "tp", 2)
    far_odds_x = flip(cut(far_late, half, rest), "ep", 1)

    def piece(start, part, array):
        return start * rows, (part,), part == 0, array

    pieces = [(0, None, False, hidden), (0, (), True, own)]
    pieces += [(rows, (0, 2), True, both_1), (rows, (1, 3), False, early[0])]
    pieces += [piece(2, 0, near_2), piece(3, 0, near_3), (2 * rows, (1,), False, near_23)]
    pieces += [piece(2, 2, far_2), piece(2, 3, early[1])]
    pieces += [piece(3, 2, far_3), piece(3, 3, flip(far_3, "tp", 1))]
    *first, w_down = run_experts(
        ranks, pieces, w_gate, w_up, w_down, 4 * rows, columns, top, True
    )
    near_both = jnp.concatenate([near_late, near_odds], axis=0)
    early = [flip(array, "tp", 1) for array in (near_both, far_late)]
    swapped = flip(page, "ep", 2)
    first, far_odds_y, far_odds_x, early, swapped = tie(
        (first, far_odds_y, far_odds_x, early, swapped)
    )
    page = page_take(page, swapped, 1)

    def add_core(given, own):
        total = total_of(own, flip(given, "tp", 1))
        return jnp.split(total, 2, axis=0)

    sent, kept = add_core(*first)
    last = [flip(array, "tp", 1) for array in (far_odds_y, far_odds_x)]
    over_23 = flip(cut(sent, 2, 2), "tp", 2)
    over_1 = flip(jnp.concatenate([cut(kept, 1, 1), cut(sent, 1, 1)], axis=1), "ep", 1)
    swapped = flip(page, "ep", 1)
    odds = len(late)
    pieces = [piece(0, 0, near_both), (0, (1,), False, early[0])]
    pieces += [piece(0, 2, far_late), piece(0, 3, early[1])]
    pieces += [piece(odds, 2, far_odds_y), piece(odds, 3, last[0])]
    pieces += [piece(odds + half, 2, far_odds_x), piece(odds + half, 3, last[1])]
    second = [
        *run_experts(
            ranks, pieces, w_gate, w_up, w_down, 2 * len(late) * rows, columns, top, False
        )
    ]
    second, over_23, swapped = tie((second, over_23, swapped))
    swapped, page = page_far(page_take(page, swapped, 0))
    late_sent, late_kept = add_core(*second)
    over_3 = flip(total_of(cut(kept, 3, 1), cut(over_23, 1, 1)), "ep", 1)
    late_sent, late_kept = tie((late_sent, late_kept))

    over_y = flip(cut(late_sent, len(late), half), "tp", 2)
    over_x = flip(cut(late_sent, len(late) + half, rest), "ep", 1)
    over_y, over_x, over_1, queries = tie((over_y, over_x, over_1, queries))
    zero = flip(total_of(cut(sent, 0, 1), over_1[:, columns:]), "tp", 2)
    odd = total_of(
        cut(late_kept, len(late), len(late)), jnp.pad(over_y, ((0, rest * rows), (0, 0)))
    )
    odd = flip(odd, "ep", 1)
    even = total_of(cut(late_sent, 0, len(late)), jnp.pad(over_x, ((half * rows, 0), (0, 0))))
    even = flip(even, "tp", 2)
    attended = attend_part(
        ranks, lengths, queries, cache_pages, groups, count // 2, count - count // 2, attended
    )
    odd, even, over_3, attended, swapped = tie((odd, even, over_3, attended, swapped))
    if levels > 2:
        page = page_take(page, swapped, 2)
    even = total_of(cut(late_kept, 0, len(late)), even, odd)
    back = [flip(cut(even, i, 1), "ep", 2 * m) for i, m in enumerate(late)]
    back.append(flip(total_of(cut(kept, 2, 1), cut(over_23, 0, 1), over_3), "ep", 2))
    attended = attend_traded(
        ranks, lengths, swap_slot, swap_mask, queries, page, attended, groups
    )
    *back, attended = tie((*back, attended))
    moe_out = total_of(cut(kept, 0, 1), over_1[:, :columns], zero, *back)
    return attended, moe_out


def solution(mesh):
    in_specs = (
        P(("ep", "tp"), None, None),
        P(("ep", "tp"), None, None),
        P(),
        P(),
        P(),
        P("ep", None),
        P("ep", None),
        P("ep", None),
        P("ep", None, "tp"),
        P("ep", None, "tp"),
        P("ep", "tp", None),
    )
    out_specs = (P(("ep", "tp"), None, None), P("ep", "tp"))
    return jax.shard_map(local, mesh=mesh, in_specs=in_specs, out_specs=out_specs, check_vma=False)
```

```python
import functools
import math

import jax
import jax.numpy as jnp
from jax import lax
from jax.experimental import pallas as pl
from jax.experimental.pallas import tpu as pltpu
from jax.sharding import PartitionSpec as P

LAT = 512
SCORE_SCALE = 192.0 ** (-0.5)
MASK_FLOOR = -1e30
ROWS = 512
MIB = 1 << 20


def flip(block, axis, apart):
    count = lax.axis_size(axis)
    return lax.ppermute(block, axis, [(i, i ^ apart) for i in range(count)])


def attend_body(query, page, length):
    scores = (
        lax.dot_general(query, page, (((0,), (0,)), ((), ())), preferred_element_type=jnp.float32)
        * SCORE_SCALE
    )
    live = lax.broadcasted_iota(jnp.int32, scores.shape, 1) < length
    scores = jnp.where(live, scores, MASK_FLOOR)
    top = jnp.max(scores, axis=1, keepdims=True)
    weight = jnp.where(live, jnp.exp(scores - top), 0.0)
    total = jnp.sum(weight, axis=1, keepdims=True)
    blended = lax.dot_general(
        weight.astype(jnp.bfloat16),
        page[:LAT],
        (((1,), (1,)), ((), ())),
        preferred_element_type=jnp.float32,
    )
    return (blended / total).astype(jnp.bfloat16)


def in_hbm(array):
    return pltpu.with_memory_space_constraint(array, pltpu.HBM)


def in_vmem(array):
    return pltpu.with_memory_space_constraint(array, pltpu.VMEM)


ANYWHERE = pl.BlockSpec(memory_space=pl.ANY)
IN_VMEM = pl.BlockSpec(memory_space=pltpu.VMEM)
IN_SMEM = pl.BlockSpec(memory_space=pltpu.SMEM)


def device_of(ranks_ref, groups, mask=0):
    return (ranks_ref[0] ^ mask) * groups + ranks_ref[1]


def pick_kernel(groups, ranks_ref, slots_ref, ids_ref, gates_ref, hidden_ref, pages_ref, near_ref, both_ref, page_ref, sems):
    rows = hidden_ref.shape[0]
    columns = hidden_ref.shape[1] // groups

    def quarter(part):
        start = pl.multiple_of((ranks_ref[1] ^ part) * columns, 128)
        return hidden_ref.at[:, pl.ds(start, columns)]

    copies = [
        (quarter(0), near_ref.at[:, pl.ds(0, columns)]),
        (quarter(0), both_ref.at[:, pl.ds(0, columns)]),
        (quarter(2), both_ref.at[:, pl.ds(columns, columns)]),
        (pages_ref.at[slots_ref[device_of(ranks_ref, groups)]], page_ref),
    ]
    copies = [pltpu.make_async_copy(*pair, sems.at[i]) for i, pair in enumerate(copies)]
    for one in copies:
        one.start()
    gates = gates_ref[...]
    high = gates.astype(jnp.bfloat16).astype(jnp.float32)
    middle = (gates - high).astype(jnp.bfloat16).astype(jnp.float32)
    low = gates - high - middle
    top = gates.shape[0]
    table = jnp.concatenate(
        [ids_ref[...].astype(jnp.float32), high, middle, low, jnp.zeros((128 - 4 * top, rows), jnp.float32)],
        axis=0,
    )
    table = jnp.concatenate([table, jnp.zeros((128, 128 - rows), jnp.float32)], axis=1)
    table = table.T[:rows].astype(jnp.bfloat16)
    near_ref[:, columns:] = table
    both_ref[:, 2 * columns :] = table
    for one in copies:
        one.wait()


def pick(ranks, swap_slot, expert_ids, gate_weights, hidden, pages, groups):
    rows, width = hidden.shape
    columns = width // groups
    return pl.pallas_call(
        functools.partial(pick_kernel, groups),
        out_shape=(
            pltpu.VMEM((rows, columns + 128), jnp.bfloat16),
            pltpu.VMEM((rows, 2 * columns + 128), jnp.bfloat16),
            pltpu.VMEM(pages.shape[1:], jnp.bfloat16),
        ),
        in_specs=[IN_SMEM, IN_SMEM, IN_VMEM, IN_VMEM, ANYWHERE, ANYWHERE],
        out_specs=(IN_VMEM, IN_VMEM, IN_VMEM),
        scratch_shapes=[pltpu.SemaphoreType.DMA((4,))],
        compiler_params=pltpu.CompilerParams(vmem_limit_bytes=2 * MIB),
        name="pick",
    )(
        ranks,
        in_hbm(swap_slot),
        in_hbm(expert_ids.T),
        in_hbm(gate_weights.T),
        in_hbm(hidden),
        in_hbm(pages),
    )


def attend_part(ranks, lengths, queries, pages, groups, first, some, before=None):
    count, width, heads = queries.shape
    slots = pages.shape[2]
    each = math.gcd(some, 2)
    skip = first // each

    def kernel(ranks_ref, lengths_ref, query_ref, page_ref, *refs):
        start = device_of(ranks_ref, groups) * count + first + pl.program_id(0) * each
        for i in range(each):
            refs[-1][i] = attend_body(query_ref[i], page_ref[i], lengths_ref[start + i])

    earlier = [] if before is None else [before]
    return pl.pallas_call(
        kernel,
        out_shape=jax.ShapeDtypeStruct((count, heads, LAT), jnp.bfloat16),
        grid_spec=pltpu.PrefetchScalarGridSpec(
            num_scalar_prefetch=2,
            grid=(some // each,),
            in_specs=[
                pl.BlockSpec((each, width, heads), lambda i, *_: (skip + i, 0, 0)),
                pl.BlockSpec((each, width, slots), lambda i, *_: (skip + i, 0, 0)),
            ]
            + [ANYWHERE] * len(earlier),
            out_specs=pl.BlockSpec((each, heads, LAT), lambda i, *_: (skip + i, 0, 0)),
        ),
        input_output_aliases={4: 0} if earlier else {},
        compiler_params=pltpu.CompilerParams(vmem_limit_bytes=8 * MIB),
        cost_estimate=pl.CostEstimate(flops=0, bytes_accessed=0, transcendentals=0),
        name="attend_local",
    )(ranks, lengths, in_hbm(queries), in_hbm(pages), *earlier)


def load_kernel(*refs):
    count = len(refs) // 2
    copies = [
        pltpu.make_async_copy(refs[i], refs[count + i], refs[-1].at[i]) for i in range(count)
    ]
    for one in copies:
        one.start()
    for one in copies:
        one.wait()


def load(*arrays):
    return pl.pallas_call(
        load_kernel,
        out_shape=[pltpu.VMEM(w.shape, w.dtype) for w in arrays],
        in_specs=[ANYWHERE] * len(arrays),
        out_specs=[ANYWHERE] * len(arrays),
        scratch_shapes=[pltpu.SemaphoreType.DMA((len(arrays),))],
        compiler_params=pltpu.CompilerParams(vmem_limit_bytes=MIB),
        cost_estimate=pl.CostEstimate(
            flops=0, bytes_accessed=sum(2 * math.prod(w.shape) for w in arrays), transcendentals=0
        ),
        name="load",
    )(*[in_hbm(w) for w in arrays])


def attend_traded_kernel(
    groups, ranks_ref, lengths_ref, slots_ref, mask_ref, query_ref, page_ref, old_ref, out_ref
):
    partner = device_of(ranks_ref, groups, mask_ref[0])
    length = lengths_ref[partner * old_ref.shape[0] + slots_ref[partner]]
    out_ref[0] = attend_body(query_ref[0], page_ref[...], length)


def attend_traded(ranks, lengths, swap_slot, swap_mask, queries, page, attended, groups):
    _, width, heads = queries.shape
    slots = page.shape[1]

    def mine(i, ranks_ref, lengths_ref, slots_ref, mask_ref):
        return slots_ref[device_of(ranks_ref, groups)], 0, 0

    return pl.pallas_call(
        functools.partial(attend_traded_kernel, groups),
        out_shape=jax.ShapeDtypeStruct(attended.shape, attended.dtype),
        grid_spec=pltpu.PrefetchScalarGridSpec(
            num_scalar_prefetch=4,
            grid=(1,),
            in_specs=[
                pl.BlockSpec((1, width, heads), mine),
                pl.BlockSpec((width, slots), lambda i, *_: (0, 0)),
                ANYWHERE,
            ],
            out_specs=pl.BlockSpec((1, heads, LAT), mine),
        ),
        input_output_aliases={6: 0},
        compiler_params=pltpu.CompilerParams(vmem_limit_bytes=4 * MIB),
        cost_estimate=pl.CostEstimate(
            flops=2 * heads * slots * (width + LAT),
            bytes_accessed=2 * (heads * (width + LAT) + slots * width),
            transcendentals=heads * slots,
        ),
        name="attend_traded",
    )(ranks, lengths, swap_slot, swap_mask, in_hbm(queries), page, attended)


def experts_kernel(
    top,
    fetch,
    ranks_ref,
    pieces,
    gate_ref,
    up_ref,
    source_ref,
    given_ref,
    kept_ref,
    *refs,
):
    if fetch:
        down_ref, *refs = refs
    else:
        down_ref = source_ref
    rows_ref, meta_ref, inner_ref, table_ref, sems, down_sem = refs
    experts, _, units = gate_ref.shape
    total_rows = rows_ref.shape[0]
    quarter = kept_ref.shape[1]
    ep_rank, tp_rank = ranks_ref[0], ranks_ref[1]

    def columns_of(part):
        return pl.ds(pl.multiple_of((tp_rank ^ part) * quarter, 128), quarter)

    copies = []
    for start, parts, has_meta, piece in pieces:
        rows = pl.ds(start, piece.shape[0])
        if parts is None:
            copies.append((piece, rows_ref.at[rows, :]))
            continue
        for i, part in enumerate(parts):
            copies.append(
                (piece.at[:, pl.ds(i * quarter, quarter)], rows_ref.at[rows, columns_of(part)])
            )
        if has_meta:
            copies.append((piece.at[:, pl.ds(piece.shape[1] - 128, 128)], meta_ref.at[rows, :]))
    copies = [
        pltpu.make_async_copy(source, target, sems.at[i])
        for i, (source, target) in enumerate(copies)
    ]
    for one in copies:
        one.start()
    if fetch:
        down_copy = pltpu.make_async_copy(source_ref, down_ref, down_sem)
        down_copy.start()
    for one in copies:
        one.wait()
    meta = meta_ref[...].astype(jnp.float32)
    gates = sum(pltpu.roll(meta, 128 - i * top, 1) for i in range(1, 4))
    lane = lax.broadcasted_iota(jnp.int32, meta.shape, 1)
    for e in range(experts):
        name = (ep_rank * experts + e).astype(jnp.float32)
        mine = jnp.where((lane < top) & (meta == name), gates, 0.0)
        table_ref[:, e : e + 1] = jnp.sum(mine, axis=1, keepdims=True)
    stride = math.gcd(total_rows, ROWS)
    for e in range(experts):

        @pl.loop(0, total_rows // stride)
        def _(step):
            at = pl.ds(pl.multiple_of(step * stride, stride), stride)
            rows = rows_ref[at, :]
            gate = jnp.dot(rows, gate_ref[e], preferred_element_type=jnp.float32)
            up = jnp.dot(rows, up_ref[e], preferred_element_type=jnp.float32)
            act = gate / (1.0 + jnp.exp(-gate)) * up * table_ref[at, e : e + 1]
            inner_ref[at, e * units : (e + 1) * units] = act.astype(jnp.bfloat16)

    if fetch:
        down_copy.wait()
    for part, out_ref, half in ((3, given_ref, 0), (1, given_ref, 1), (2, kept_ref, 0), (0, kept_ref, 1)):

        @pl.loop(0, total_rows // stride)
        def _(step):
            at = pl.ds(pl.multiple_of(step * stride, stride), stride)
            to = pl.ds(pl.multiple_of(half * total_rows + step * stride, stride), stride)
            weight = down_ref[:, :, columns_of(part)].reshape(experts * units, quarter)
            out_ref[to, :] = jnp.dot(
                inner_ref[at, :], weight, preferred_element_type=jnp.float32
            ).astype(jnp.bfloat16)


def run_experts(ranks, pieces, w_gate, w_up, w_down, rows, columns, top, fetch):
    experts, width, units = w_gate.shape
    arrays = [piece for *_, piece in pieces]
    count = sum(1 if parts is None else len(parts) + has_meta for _, parts, has_meta, _ in pieces)

    def kernel(ranks_ref, refs, *others):
        named = [(*about[:3], ref) for about, ref in zip(pieces, refs)]
        experts_kernel(top, fetch, ranks_ref, named, *others)

    need = 2 * rows * (width + 128 + experts * units) + 512 * rows
    down_shape = [pltpu.VMEM(w_down.shape, w_down.dtype)] if fetch else []
    return pl.pallas_call(
        kernel,
        out_shape=[pltpu.VMEM((2 * rows, columns), jnp.bfloat16)] * 2 + down_shape,
        in_specs=[
            IN_SMEM,
            [ANYWHERE] * len(arrays),
            IN_VMEM,
            IN_VMEM,
            ANYWHERE if fetch else IN_VMEM,
        ],
        out_specs=[IN_VMEM] * (2 + len(down_shape)),
        scratch_shapes=[
            pltpu.VMEM((rows, width), jnp.bfloat16),
            pltpu.VMEM((rows, 128), jnp.bfloat16),
            pltpu.VMEM((rows, experts * units), jnp.bfloat16),
            pltpu.VMEM((rows, 128), jnp.float32),
            pltpu.SemaphoreType.DMA((count,)),
            pltpu.SemaphoreType.DMA,
        ],
        compiler_params=pltpu.CompilerParams(vmem_limit_bytes=need + 6 * MIB),
        cost_estimate=pl.CostEstimate(
            flops=0,
            bytes_accessed=0,
            transcendentals=0,
        ),
        name="experts",
    )(
        ranks,
        arrays,
        in_vmem(w_gate),
        in_vmem(w_up),
        in_hbm(w_down) if fetch else in_vmem(w_down),
    )


def total_of(*terms):
    value = terms[0].astype(jnp.float32)
    for term in terms[1:]:
        value = value + term.astype(jnp.float32)
    return value.astype(jnp.bfloat16)


def local(
    cache_pages,
    queries,
    lengths,
    swap_slot,
    swap_mask,
    hidden,
    expert_ids,
    gate_weights,
    w_gate,
    w_up,
    w_down,
):
    groups = lax.axis_size("tp")
    ep_size = lax.axis_size("ep")
    ranks = jnp.stack([lax.axis_index("ep"), lax.axis_index("tp")]).astype(jnp.int32)
    mask_value = swap_mask[0]
    columns = hidden.shape[1] // groups
    top = expert_ids.shape[1]
    cache_pages = jnp.swapaxes(cache_pages, 1, 2)
    queries = jnp.swapaxes(queries, 1, 2)

    rows = hidden.shape[0]
    pairs = ep_size // 2
    late = list(range(2, pairs))
    half = len(late) // 2
    rest = len(late) - half
    levels = ep_size.bit_length() - 1
    tie = lax.optimization_barrier

    def cut(array, start, count):
        return lax.slice_in_dim(array, start * rows, (start + count) * rows, axis=0)

    def bare(array):
        return array[:, :columns]

    def page_take(page, swapped, level):
        bit = jnp.bitwise_and(jnp.right_shift(mask_value, level), 1) == 1
        return jnp.where(bit, swapped, page)

    def page_hop(page, level):
        return page_take(page, flip(page, "ep", 1 << level), level)

    def page_far(page):
        for level in range(levels - 1, 2, -1):
            page = page_hop(page, level)
        return flip(page, "ep", 4) if levels > 2 else page, page

    own, both, page = pick(
        ranks, swap_slot, expert_ids, gate_weights, hidden, cache_pages, groups
    )
    late_pieces = [flip(own, "ep", 2 * m) for m in late]
    near_2 = flip(own, "ep", 2)
    both_1 = flip(both, "ep", 1)

    near_2, w_gate, w_up = tie((near_2, w_gate, w_up))
    far_2 = flip(bare(near_2), "tp", 2)
    near_3 = flip(near_2, "ep", 1)
    w_gate, w_up = load(w_gate, w_up)
    far_2, near_3, w_gate, w_up, page, both_1, *late_pieces = tie(
        (far_2, near_3, w_gate, w_up, page, both_1, *late_pieces)
    )
    near_late = jnp.concatenate(late_pieces, axis=0)
    far_3 = flip(jnp.concatenate([bare(near_3), bare(near_late)], axis=0), "tp", 2)
    near_odds = flip(near_late, "ep", 1)
    near_23 = flip(jnp.concatenate([near_2, near_3], axis=0), "tp", 1)
    early = [flip(array, "tp", 1) for array in (both_1, far_2)]
    queries, near_23, early = tie((queries, near_23, early))
    count = queries.shape[0]
    some = count * 5 // 8
    attended = attend_part(ranks, lengths, queries, cache_pages, groups, 0, some)
    far_3, near_late, near_odds, attended, page = tie(
        (far_3, near_late, near_odds, attended, page)
    )
    far_3, far_late = cut(far_3, 0, 1), cut(far_3, 1, len(late))
    far_odds = flip(bare(near_odds), "tp", 2)

    def piece(start, part, array):
        return start * rows, (part,), part == 0, array

    pieces = [(0, None, False, hidden), (0, (), True, own)]
    pieces += [(rows, (0, 2), True, both_1), (rows, (1, 3), False, early[0])]
    pieces += [piece(2, 0, near_2), piece(3, 0, near_3), (2 * rows, (1,), False, near_23)]
    pieces += [piece(2, 2, far_2), piece(2, 3, early[1])]
    pieces += [piece(3, 2, far_3), piece(3, 3, flip(far_3, "tp", 1))]
    *first, w_down = run_experts(
        ranks, pieces, w_gate, w_up, w_down, 4 * rows, columns, top, True
    )
    near_both = jnp.concatenate([near_late, near_odds], axis=0)
    early = [flip(array, "tp", 1) for array in (near_both, far_late)]
    swapped = flip(page, "ep", 1)
    first, far_odds, early, swapped = tie((first, far_odds, early, swapped))
    page = page_take(page, swapped, 0)

    def add_core(given, own):
        total = total_of(own, flip(given, "tp", 1))
        return jnp.split(total, 2, axis=0)

    sent, kept = add_core(*first)
    last = flip(far_odds, "tp", 1)
    over_23 = flip(cut(sent, 2, 2), "tp", 2)
    over_1 = flip(jnp.concatenate([cut(kept, 1, 1), cut(sent, 1, 1)], axis=1), "ep", 1)
    swapped = flip(page, "ep", 2)
    odds = len(late)
    pieces = [piece(0, 0, near_both), (0, (1,), False, early[0])]
    pieces += [piece(0, 2, far_late), piece(0, 3, early[1])]
    pieces += [piece(odds, 2, far_odds), piece(odds, 3, last)]
    second = [
        *run_experts(
            ranks, pieces, w_gate, w_up, w_down, 2 * len(late) * rows, columns, top, False
        )
    ]
    second, over_23, over_1, swapped = tie((second, over_23, over_1, swapped))
    swapped, page = page_far(page_take(page, swapped, 1))
    late_sent, late_kept = add_core(*second)
    over_3 = flip(total_of(cut(kept, 3, 1), cut(over_23, 1, 1)), "ep", 1)
    zero = flip(total_of(cut(sent, 0, 1), over_1[:, columns:]), "tp", 2)
    late_sent, late_kept = tie((late_sent, late_kept))

    over_y = flip(cut(late_sent, len(late), half), "tp", 2)
    over_x = flip(cut(late_sent, len(late) + half, rest), "ep", 1)
    over_y, over_x, over_3, zero, queries = tie((over_y, over_x, over_3, zero, queries))
    odd = total_of(
        cut(late_kept, len(late), len(late)), jnp.pad(over_y, ((0, rest * rows), (0, 0)))
    )
    odd = flip(odd, "ep", 1)
    even = total_of(cut(late_sent, 0, len(late)), jnp.pad(over_x, ((half * rows, 0), (0, 0))))
    even = flip(even, "tp", 2)
    attended = attend_part(
        ranks, lengths, queries, cache_pages, groups, some, count - some, attended
    )
    odd, even, attended, swapped = tie((odd, even, attended, swapped))
    if levels > 2:
        page = page_take(page, swapped, 2)
    even = total_of(cut(late_kept, 0, len(late)), even, odd)
    back = [flip(cut(even, i, 1), "ep", 2 * m) for i, m in enumerate(late)]
    back.append(flip(total_of(cut(kept, 2, 1), cut(over_23, 0, 1), over_3), "ep", 2))
    attended = attend_traded(
        ranks, lengths, swap_slot, swap_mask, queries, page, attended, groups
    )
    *back, attended = tie((*back, attended))
    moe_out = total_of(cut(kept, 0, 1), over_1[:, :columns], zero, *back)
    return attended, moe_out


def solution(mesh):
    in_specs = (
        P(("ep", "tp"), None, None),
        P(("ep", "tp"), None, None),
        P(),
        P(),
        P(),
        P("ep", None),
        P("ep", None),
        P("ep", None),
        P("ep", None, "tp"),
        P("ep", None, "tp"),
        P("ep", "tp", None),
    )
    out_specs = (P(("ep", "tp"), None, None), P("ep", "tp"))
    return jax.shard_map(local, mesh=mesh, in_specs=in_specs, out_specs=out_specs, check_vma=False)
```

```python
import functools
import math

import jax
import jax.numpy as jnp
from jax import lax
from jax.experimental import pallas as pl
from jax.experimental.pallas import tpu as pltpu
from jax.sharding import PartitionSpec as P

LAT = 512
SCORE_SCALE = 192.0 ** (-0.5)
MASK_FLOOR = -1e30
ROWS = 512
MIB = 1 << 20


def flip(block, axis, apart):
    count = lax.axis_size(axis)
    return lax.ppermute(block, axis, [(i, i ^ apart) for i in range(count)])


def attend_body(query, page, length):
    scores = (
        lax.dot_general(query, page, (((0,), (0,)), ((), ())), preferred_element_type=jnp.float32)
        * SCORE_SCALE
    )
    live = lax.broadcasted_iota(jnp.int32, scores.shape, 1) < length
    scores = jnp.where(live, scores, MASK_FLOOR)
    top = jnp.max(scores, axis=1, keepdims=True)
    weight = jnp.where(live, jnp.exp(scores - top), 0.0)
    total = jnp.sum(weight, axis=1, keepdims=True)
    blended = lax.dot_general(
        weight.astype(jnp.bfloat16),
        page[:LAT],
        (((1,), (1,)), ((), ())),
        preferred_element_type=jnp.float32,
    )
    return (blended / total).astype(jnp.bfloat16)


def in_hbm(array):
    return pltpu.with_memory_space_constraint(array, pltpu.HBM)


def in_vmem(array):
    return pltpu.with_memory_space_constraint(array, pltpu.VMEM)


ANYWHERE = pl.BlockSpec(memory_space=pl.ANY)
IN_VMEM = pl.BlockSpec(memory_space=pltpu.VMEM)
IN_SMEM = pl.BlockSpec(memory_space=pltpu.SMEM)


def device_of(ranks_ref, groups, mask=0):
    return (ranks_ref[0] ^ mask) * groups + ranks_ref[1]


def pick_kernel(groups, ranks_ref, slots_ref, ids_ref, gates_ref, hidden_ref, pages_ref, near_ref, both_ref, page_ref, sems):
    rows = hidden_ref.shape[0]
    columns = hidden_ref.shape[1] // groups

    def quarter(part):
        start = pl.multiple_of((ranks_ref[1] ^ part) * columns, 128)
        return hidden_ref.at[:, pl.ds(start, columns)]

    copies = [
        (quarter(0), near_ref.at[:, pl.ds(0, columns)]),
        (quarter(0), both_ref.at[:, pl.ds(0, columns)]),
        (quarter(2), both_ref.at[:, pl.ds(columns, columns)]),
        (pages_ref.at[slots_ref[device_of(ranks_ref, groups)]], page_ref),
    ]
    copies = [pltpu.make_async_copy(*pair, sems.at[i]) for i, pair in enumerate(copies)]
    for one in copies:
        one.start()
    gates = gates_ref[...]
    high = gates.astype(jnp.bfloat16).astype(jnp.float32)
    middle = (gates - high).astype(jnp.bfloat16).astype(jnp.float32)
    low = gates - high - middle
    top = gates.shape[0]
    table = jnp.concatenate(
        [ids_ref[...].astype(jnp.float32), high, middle, low, jnp.zeros((128 - 4 * top, rows), jnp.float32)],
        axis=0,
    )
    table = jnp.concatenate([table, jnp.zeros((128, 128 - rows), jnp.float32)], axis=1)
    table = table.T[:rows].astype(jnp.bfloat16)
    near_ref[:, columns:] = table
    both_ref[:, 2 * columns :] = table
    for one in copies:
        one.wait()


def pick(ranks, swap_slot, expert_ids, gate_weights, hidden, pages, groups):
    rows, width = hidden.shape
    columns = width // groups
    return pl.pallas_call(
        functools.partial(pick_kernel, groups),
        out_shape=(
            pltpu.VMEM((rows, columns + 128), jnp.bfloat16),
            pltpu.VMEM((rows, 2 * columns + 128), jnp.bfloat16),
            pltpu.VMEM(pages.shape[1:], jnp.bfloat16),
        ),
        in_specs=[IN_SMEM, IN_SMEM, IN_VMEM, IN_VMEM, ANYWHERE, ANYWHERE],
        out_specs=(IN_VMEM, IN_VMEM, IN_VMEM),
        scratch_shapes=[pltpu.SemaphoreType.DMA((4,))],
        compiler_params=pltpu.CompilerParams(vmem_limit_bytes=2 * MIB),
        name="pick",
    )(
        ranks,
        in_hbm(swap_slot),
        in_hbm(expert_ids.T),
        in_hbm(gate_weights.T),
        in_hbm(hidden),
        in_hbm(pages),
    )


def attend_part(ranks, lengths, queries, pages, groups, first, some, before=None):
    count, width, heads = queries.shape
    slots = pages.shape[2]
    each = math.gcd(some, 2)
    skip = first // each

    def kernel(ranks_ref, lengths_ref, query_ref, page_ref, *refs):
        start = device_of(ranks_ref, groups) * count + first + pl.program_id(0) * each
        for i in range(each):
            refs[-1][i] = attend_body(query_ref[i], page_ref[i], lengths_ref[start + i])

    earlier = [] if before is None else [before]
    return pl.pallas_call(
        kernel,
        out_shape=jax.ShapeDtypeStruct((count, heads, LAT), jnp.bfloat16),
        grid_spec=pltpu.PrefetchScalarGridSpec(
            num_scalar_prefetch=2,
            grid=(some // each,),
            in_specs=[
                pl.BlockSpec((each, width, heads), lambda i, *_: (skip + i, 0, 0)),
                pl.BlockSpec((each, width, slots), lambda i, *_: (skip + i, 0, 0)),
            ]
            + [ANYWHERE] * len(earlier),
            out_specs=pl.BlockSpec((each, heads, LAT), lambda i, *_: (skip + i, 0, 0)),
        ),
        input_output_aliases={4: 0} if earlier else {},
        compiler_params=pltpu.CompilerParams(vmem_limit_bytes=8 * MIB),
        cost_estimate=pl.CostEstimate(flops=0, bytes_accessed=0, transcendentals=0),
        name="attend_local",
    )(ranks, lengths, in_hbm(queries), in_hbm(pages), *earlier)


def load_kernel(*refs):
    count = len(refs) // 2
    copies = [
        pltpu.make_async_copy(refs[i], refs[count + i], refs[-1].at[i]) for i in range(count)
    ]
    for one in copies:
        one.start()
    for one in copies:
        one.wait()


def load(*arrays):
    return pl.pallas_call(
        load_kernel,
        out_shape=[pltpu.VMEM(w.shape, w.dtype) for w in arrays],
        in_specs=[ANYWHERE] * len(arrays),
        out_specs=[ANYWHERE] * len(arrays),
        scratch_shapes=[pltpu.SemaphoreType.DMA((len(arrays),))],
        compiler_params=pltpu.CompilerParams(vmem_limit_bytes=MIB),
        cost_estimate=pl.CostEstimate(
            flops=0, bytes_accessed=sum(2 * math.prod(w.shape) for w in arrays), transcendentals=0
        ),
        name="load",
    )(*[in_hbm(w) for w in arrays])


def attend_traded_kernel(
    groups, ranks_ref, lengths_ref, slots_ref, mask_ref, query_ref, page_ref, old_ref, out_ref
):
    partner = device_of(ranks_ref, groups, mask_ref[0])
    length = lengths_ref[partner * old_ref.shape[0] + slots_ref[partner]]
    out_ref[0] = attend_body(query_ref[0], page_ref[...], length)


def attend_traded(ranks, lengths, swap_slot, swap_mask, queries, page, attended, groups):
    _, width, heads = queries.shape
    slots = page.shape[1]

    def mine(i, ranks_ref, lengths_ref, slots_ref, mask_ref):
        return slots_ref[device_of(ranks_ref, groups)], 0, 0

    return pl.pallas_call(
        functools.partial(attend_traded_kernel, groups),
        out_shape=jax.ShapeDtypeStruct(attended.shape, attended.dtype),
        grid_spec=pltpu.PrefetchScalarGridSpec(
            num_scalar_prefetch=4,
            grid=(1,),
            in_specs=[
                pl.BlockSpec((1, width, heads), mine),
                pl.BlockSpec((width, slots), lambda i, *_: (0, 0)),
                ANYWHERE,
            ],
            out_specs=pl.BlockSpec((1, heads, LAT), mine),
        ),
        input_output_aliases={6: 0},
        compiler_params=pltpu.CompilerParams(vmem_limit_bytes=4 * MIB),
        cost_estimate=pl.CostEstimate(
            flops=2 * heads * slots * (width + LAT),
            bytes_accessed=2 * (heads * (width + LAT) + slots * width),
            transcendentals=heads * slots,
        ),
        name="attend_traded",
    )(ranks, lengths, swap_slot, swap_mask, in_hbm(queries), page, attended)


def experts_kernel(
    top,
    fetch,
    ranks_ref,
    pieces,
    gate_ref,
    up_ref,
    source_ref,
    given_ref,
    kept_ref,
    *refs,
):
    if fetch:
        down_ref, *refs = refs
    else:
        down_ref = source_ref
    rows_ref, meta_ref, inner_ref, table_ref, sems, down_sem = refs
    experts, _, units = gate_ref.shape
    total_rows = rows_ref.shape[0]
    quarter = kept_ref.shape[1]
    ep_rank, tp_rank = ranks_ref[0], ranks_ref[1]

    def columns_of(part):
        return pl.ds(pl.multiple_of((tp_rank ^ part) * quarter, 128), quarter)

    copies = []
    for start, parts, has_meta, piece in pieces:
        rows = pl.ds(start, piece.shape[0])
        if parts is None:
            copies.append((piece, rows_ref.at[rows, :]))
            continue
        for i, part in enumerate(parts):
            copies.append(
                (piece.at[:, pl.ds(i * quarter, quarter)], rows_ref.at[rows, columns_of(part)])
            )
        if has_meta:
            copies.append((piece.at[:, pl.ds(piece.shape[1] - 128, 128)], meta_ref.at[rows, :]))
    copies = [
        pltpu.make_async_copy(source, target, sems.at[i])
        for i, (source, target) in enumerate(copies)
    ]
    for one in copies:
        one.start()
    if fetch:
        down_copy = pltpu.make_async_copy(source_ref, down_ref, down_sem)
        down_copy.start()
    for one in copies:
        one.wait()
    meta = meta_ref[...].astype(jnp.float32)
    gates = sum(pltpu.roll(meta, 128 - i * top, 1) for i in range(1, 4))
    lane = lax.broadcasted_iota(jnp.int32, meta.shape, 1)
    for e in range(experts):
        name = (ep_rank * experts + e).astype(jnp.float32)
        mine = jnp.where((lane < top) & (meta == name), gates, 0.0)
        table_ref[:, e : e + 1] = jnp.sum(mine, axis=1, keepdims=True)
    stride = math.gcd(total_rows, ROWS)
    for e in range(experts):

        @pl.loop(0, total_rows // stride)
        def _(step):
            at = pl.ds(pl.multiple_of(step * stride, stride), stride)
            rows = rows_ref[at, :]
            gate = jnp.dot(rows, gate_ref[e], preferred_element_type=jnp.float32)
            up = jnp.dot(rows, up_ref[e], preferred_element_type=jnp.float32)
            act = gate / (1.0 + jnp.exp(-gate)) * up * table_ref[at, e : e + 1]
            inner_ref[at, e * units : (e + 1) * units] = act.astype(jnp.bfloat16)

    if fetch:
        down_copy.wait()
    for part, out_ref, half in ((3, given_ref, 0), (1, given_ref, 1), (2, kept_ref, 0), (0, kept_ref, 1)):

        @pl.loop(0, total_rows // stride)
        def _(step):
            at = pl.ds(pl.multiple_of(step * stride, stride), stride)
            to = pl.ds(pl.multiple_of(half * total_rows + step * stride, stride), stride)
            weight = down_ref[:, :, columns_of(part)].reshape(experts * units, quarter)
            out_ref[to, :] = jnp.dot(
                inner_ref[at, :], weight, preferred_element_type=jnp.float32
            ).astype(jnp.bfloat16)


def run_experts(ranks, pieces, w_gate, w_up, w_down, rows, columns, top, fetch):
    experts, width, units = w_gate.shape
    arrays = [piece for *_, piece in pieces]
    count = sum(1 if parts is None else len(parts) + has_meta for _, parts, has_meta, _ in pieces)

    def kernel(ranks_ref, refs, *others):
        named = [(*about[:3], ref) for about, ref in zip(pieces, refs)]
        experts_kernel(top, fetch, ranks_ref, named, *others)

    need = 2 * rows * (width + 128 + experts * units) + 512 * rows
    down_shape = [pltpu.VMEM(w_down.shape, w_down.dtype)] if fetch else []
    return pl.pallas_call(
        kernel,
        out_shape=[pltpu.VMEM((2 * rows, columns), jnp.bfloat16)] * 2 + down_shape,
        in_specs=[
            IN_SMEM,
            [ANYWHERE] * len(arrays),
            IN_VMEM,
            IN_VMEM,
            ANYWHERE if fetch else IN_VMEM,
        ],
        out_specs=[IN_VMEM] * (2 + len(down_shape)),
        scratch_shapes=[
            pltpu.VMEM((rows, width), jnp.bfloat16),
            pltpu.VMEM((rows, 128), jnp.bfloat16),
            pltpu.VMEM((rows, experts * units), jnp.bfloat16),
            pltpu.VMEM((rows, 128), jnp.float32),
            pltpu.SemaphoreType.DMA((count,)),
            pltpu.SemaphoreType.DMA,
        ],
        compiler_params=pltpu.CompilerParams(vmem_limit_bytes=need + 6 * MIB),
        cost_estimate=pl.CostEstimate(
            flops=0,
            bytes_accessed=0,
            transcendentals=0,
        ),
        name="experts",
    )(
        ranks,
        arrays,
        in_vmem(w_gate),
        in_vmem(w_up),
        in_hbm(w_down) if fetch else in_vmem(w_down),
    )


def total_of(*terms):
    value = terms[0].astype(jnp.float32)
    for term in terms[1:]:
        value = value + term.astype(jnp.float32)
    return value.astype(jnp.bfloat16)


def local(
    cache_pages,
    queries,
    lengths,
    swap_slot,
    swap_mask,
    hidden,
    expert_ids,
    gate_weights,
    w_gate,
    w_up,
    w_down,
):
    groups = lax.axis_size("tp")
    ep_size = lax.axis_size("ep")
    ranks = jnp.stack([lax.axis_index("ep"), lax.axis_index("tp")]).astype(jnp.int32)
    mask_value = swap_mask[0]
    columns = hidden.shape[1] // groups
    top = expert_ids.shape[1]
    cache_pages = jnp.swapaxes(cache_pages, 1, 2)
    queries = jnp.swapaxes(queries, 1, 2)

    rows = hidden.shape[0]
    pairs = ep_size // 2
    late = list(range(2, pairs))
    half = len(late) // 2
    rest = len(late) - half
    levels = ep_size.bit_length() - 1
    tie = lax.optimization_barrier

    def cut(array, start, count):
        return lax.slice_in_dim(array, start * rows, (start + count) * rows, axis=0)

    def bare(array):
        return array[:, :columns]

    def page_take(page, swapped, level):
        bit = jnp.bitwise_and(jnp.right_shift(mask_value, level), 1) == 1
        return jnp.where(bit, swapped, page)

    def page_hop(page, level):
        return page_take(page, flip(page, "ep", 1 << level), level)

    def page_far(page):
        for level in range(levels - 1, 2, -1):
            page = page_hop(page, level)
        return flip(page, "ep", 4) if levels > 2 else page, page

    own, both, page = pick(
        ranks, swap_slot, expert_ids, gate_weights, hidden, cache_pages, groups
    )
    late_pieces = [flip(own, "ep", 2 * m) for m in late]
    near_2 = flip(own, "ep", 2)
    both_1 = flip(both, "ep", 1)

    near_2, w_gate, w_up = tie((near_2, w_gate, w_up))
    far_2 = flip(bare(near_2), "tp", 2)
    near_3 = flip(near_2, "ep", 1)
    w_gate, w_up = load(w_gate, w_up)
    far_2, near_3, w_gate, w_up, page, both_1, *late_pieces = tie(
        (far_2, near_3, w_gate, w_up, page, both_1, *late_pieces)
    )
    near_late = jnp.concatenate(late_pieces, axis=0)
    far_3 = flip(jnp.concatenate([bare(near_3), bare(near_late)], axis=0), "tp", 2)
    near_odds = flip(near_late, "ep", 1)
    near_23 = flip(jnp.concatenate([near_2, near_3], axis=0), "tp", 1)
    early = [flip(array, "tp", 1) for array in (both_1, far_2)]
    queries, near_23, early = tie((queries, near_23, early))
    count = queries.shape[0]
    some = count // 2
    attended = attend_part(ranks, lengths, queries, cache_pages, groups, 0, some)
    upper, lower = jnp.split(page, 2, axis=0)
    swapped, upper = page_far(upper)
    far_3, near_late, near_odds, attended, swapped = tie(
        (far_3, near_late, near_odds, attended, swapped)
    )
    upper = page_take(upper, swapped, 2) if levels > 2 else upper
    page = jnp.concatenate([upper, lower], axis=0)
    core_3 = flip(far_3, "tp", 1)
    far_late, core_late = cut(far_3, 1, len(late)), cut(core_3, 1, len(late))
    far_3, core_3 = cut(far_3, 0, 1), cut(core_3, 0, 1)
    far_odds = flip(bare(near_odds), "tp", 2)

    def piece(start, part, array):
        return start * rows, (part,), part == 0, array

    pieces = [(0, None, False, hidden), (0, (), True, own)]
    pieces += [(rows, (0, 2), True, both_1), (rows, (1, 3), False, early[0])]
    pieces += [piece(2, 0, near_2), piece(3, 0, near_3), (2 * rows, (1,), False, near_23)]
    pieces += [piece(2, 2, far_2), piece(2, 3, early[1])]
    pieces += [piece(3, 2, far_3), piece(3, 3, core_3)]
    *first, w_down = run_experts(
        ranks, pieces, w_gate, w_up, w_down, 4 * rows, columns, top, True
    )
    near_both = jnp.concatenate([near_late, near_odds], axis=0)
    early = flip(near_both, "tp", 1)
    swapped = flip(page, "ep", 1)
    first, far_odds, early, swapped = tie((first, far_odds, early, swapped))
    page = page_take(page, swapped, 0)

    def add_core(given, own):
        total = total_of(own, flip(given, "tp", 1))
        return jnp.split(total, 2, axis=0)

    sent, kept = add_core(*first)
    last = flip(far_odds, "tp", 1)
    over_23 = flip(cut(sent, 2, 2), "tp", 2)
    over_1 = flip(jnp.concatenate([cut(kept, 1, 1), cut(sent, 1, 1)], axis=1), "ep", 1)
    swapped = flip(page, "ep", 2)
    odds = len(late)
    pieces = [piece(0, 0, near_both), (0, (1,), False, early)]
    pieces += [piece(0, 2, far_late), piece(0, 3, core_late)]
    pieces += [piece(odds, 2, far_odds), piece(odds, 3, last)]
    second = [
        *run_experts(
            ranks, pieces, w_gate, w_up, w_down, 2 * len(late) * rows, columns, top, False
        )
    ]
    second, over_23, over_1, swapped = tie((second, over_23, over_1, swapped))
    page = page_take(page, swapped, 1)
    upper, lower = jnp.split(page, 2, axis=0)
    swapped, lower = page_far(lower)
    late_sent, late_kept = add_core(*second)
    over_3 = flip(total_of(cut(kept, 3, 1), cut(over_23, 1, 1)), "ep", 1)
    zero = flip(total_of(cut(sent, 0, 1), over_1[:, columns:]), "tp", 2)
    late_sent, late_kept = tie((late_sent, late_kept))

    over_y = flip(cut(late_sent, len(late), half), "tp", 2)
    over_x = flip(cut(late_sent, len(late) + half, rest), "ep", 1)
    over_y, over_x, over_3, zero, queries = tie((over_y, over_x, over_3, zero, queries))
    odd = total_of(
        cut(late_kept, len(late), len(late)), jnp.pad(over_y, ((0, rest * rows), (0, 0)))
    )
    odd = flip(odd, "ep", 1)
    even = total_of(cut(late_sent, 0, len(late)), jnp.pad(over_x, ((half * rows, 0), (0, 0))))
    even = flip(even, "tp", 2)
    attended = attend_part(
        ranks, lengths, queries, cache_pages, groups, some, count - some, attended
    )
    odd, even, attended, swapped = tie((odd, even, attended, swapped))
    lower = page_take(lower, swapped, 2) if levels > 2 else lower
    page = jnp.concatenate([upper, lower], axis=0)
    even = total_of(cut(late_kept, 0, len(late)), even, odd)
    back = [flip(cut(even, i, 1), "ep", 2 * m) for i, m in enumerate(late)]
    back.append(flip(total_of(cut(kept, 2, 1), cut(over_23, 0, 1), over_3), "ep", 2))
    attended = attend_traded(
        ranks, lengths, swap_slot, swap_mask, queries, page, attended, groups
    )
    *back, attended = tie((*back, attended))
    moe_out = total_of(cut(kept, 0, 1), over_1[:, :columns], zero, *back)
    return attended, moe_out


def solution(mesh):
    in_specs = (
        P(("ep", "tp"), None, None),
        P(("ep", "tp"), None, None),
        P(),
        P(),
        P(),
        P("ep", None),
        P("ep", None),
        P("ep", None),
        P("ep", None, "tp"),
        P("ep", None, "tp"),
        P("ep", "tp", None),
    )
    out_specs = (P(("ep", "tp"), None, None), P("ep", "tp"))
    return jax.shard_map(local, mesh=mesh, in_specs=in_specs, out_specs=out_specs, check_vma=False)
```

```python
import functools
import math

import jax
import jax.numpy as jnp
from jax import lax
from jax.experimental import pallas as pl
from jax.experimental.pallas import tpu as pltpu
from jax.sharding import PartitionSpec as P

LAT = 512
SCORE_SCALE = 192.0 ** (-0.5)
MASK_FLOOR = -1e30
ROWS = 512
MIB = 1 << 20


def flip(block, axis, apart):
    count = lax.axis_size(axis)
    return lax.ppermute(block, axis, [(i, i ^ apart) for i in range(count)])


def attend_body(query, page, length):
    scores = (
        lax.dot_general(query, page, (((0,), (0,)), ((), ())), preferred_element_type=jnp.float32)
        * SCORE_SCALE
    )
    live = lax.broadcasted_iota(jnp.int32, scores.shape, 1) < length
    scores = jnp.where(live, scores, MASK_FLOOR)
    top = jnp.max(scores, axis=1, keepdims=True)
    weight = jnp.where(live, jnp.exp(scores - top), 0.0)
    total = jnp.sum(weight, axis=1, keepdims=True)
    blended = lax.dot_general(
        weight.astype(jnp.bfloat16),
        page[:LAT],
        (((1,), (1,)), ((), ())),
        preferred_element_type=jnp.float32,
    )
    return (blended / total).astype(jnp.bfloat16)


def in_hbm(array):
    return pltpu.with_memory_space_constraint(array, pltpu.HBM)


def in_vmem(array):
    return pltpu.with_memory_space_constraint(array, pltpu.VMEM)


ANYWHERE = pl.BlockSpec(memory_space=pl.ANY)
IN_VMEM = pl.BlockSpec(memory_space=pltpu.VMEM)
IN_SMEM = pl.BlockSpec(memory_space=pltpu.SMEM)


def device_of(ranks_ref, groups, mask=0):
    return (ranks_ref[0] ^ mask) * groups + ranks_ref[1]


def pick_kernel(groups, ranks_ref, slots_ref, ids_ref, gates_ref, hidden_ref, pages_ref, near_ref, both_ref, page_ref, sems):
    rows = hidden_ref.shape[0]
    columns = hidden_ref.shape[1] // groups

    def quarter(part):
        start = pl.multiple_of((ranks_ref[1] ^ part) * columns, 128)
        return hidden_ref.at[:, pl.ds(start, columns)]

    copies = [
        (quarter(0), near_ref.at[:, pl.ds(0, columns)]),
        (quarter(0), both_ref.at[:, pl.ds(0, columns)]),
        (quarter(2), both_ref.at[:, pl.ds(columns, columns)]),
        (pages_ref.at[slots_ref[device_of(ranks_ref, groups)]], page_ref),
    ]
    copies = [pltpu.make_async_copy(*pair, sems.at[i]) for i, pair in enumerate(copies)]
    for one in copies:
        one.start()
    gates = gates_ref[...]
    high = gates.astype(jnp.bfloat16).astype(jnp.float32)
    middle = (gates - high).astype(jnp.bfloat16).astype(jnp.float32)
    low = gates - high - middle
    top = gates.shape[0]
    table = jnp.concatenate(
        [ids_ref[...].astype(jnp.float32), high, middle, low, jnp.zeros((128 - 4 * top, rows), jnp.float32)],
        axis=0,
    )
    table = jnp.concatenate([table, jnp.zeros((128, 128 - rows), jnp.float32)], axis=1)
    table = table.T[:rows].astype(jnp.bfloat16)
    near_ref[:, columns:] = table
    both_ref[:, 2 * columns :] = table
    for one in copies:
        one.wait()


def pick(ranks, swap_slot, expert_ids, gate_weights, hidden, pages, groups):
    rows, width = hidden.shape
    columns = width // groups
    return pl.pallas_call(
        functools.partial(pick_kernel, groups),
        out_shape=(
            pltpu.VMEM((rows, columns + 128), jnp.bfloat16),
            pltpu.VMEM((rows, 2 * columns + 128), jnp.bfloat16),
            pltpu.VMEM(pages.shape[1:], jnp.bfloat16),
        ),
        in_specs=[IN_SMEM, IN_SMEM, IN_VMEM, IN_VMEM, ANYWHERE, ANYWHERE],
        out_specs=(IN_VMEM, IN_VMEM, IN_VMEM),
        scratch_shapes=[pltpu.SemaphoreType.DMA((4,))],
        compiler_params=pltpu.CompilerParams(vmem_limit_bytes=2 * MIB),
        name="pick",
    )(
        ranks,
        in_hbm(swap_slot),
        in_hbm(expert_ids.T),
        in_hbm(gate_weights.T),
        in_hbm(hidden),
        in_hbm(pages),
    )


def attend_part(ranks, lengths, queries, pages, groups, first, some, before=None):
    count, width, heads = queries.shape
    slots = pages.shape[2]
    each = math.gcd(some, 2)
    skip = first // each

    def kernel(ranks_ref, lengths_ref, query_ref, page_ref, *refs):
        start = device_of(ranks_ref, groups) * count + first + pl.program_id(0) * each
        for i in range(each):
            refs[-1][i] = attend_body(query_ref[i], page_ref[i], lengths_ref[start + i])

    earlier = [] if before is None else [before]
    return pl.pallas_call(
        kernel,
        out_shape=jax.ShapeDtypeStruct((count, heads, LAT), jnp.bfloat16),
        grid_spec=pltpu.PrefetchScalarGridSpec(
            num_scalar_prefetch=2,
            grid=(some // each,),
            in_specs=[
                pl.BlockSpec((each, width, heads), lambda i, *_: (skip + i, 0, 0)),
                pl.BlockSpec((each, width, slots), lambda i, *_: (skip + i, 0, 0)),
            ]
            + [ANYWHERE] * len(earlier),
            out_specs=pl.BlockSpec((each, heads, LAT), lambda i, *_: (skip + i, 0, 0)),
        ),
        input_output_aliases={4: 0} if earlier else {},
        compiler_params=pltpu.CompilerParams(vmem_limit_bytes=8 * MIB),
        cost_estimate=pl.CostEstimate(
            flops=2 * some * heads * slots * (width + LAT),
            bytes_accessed=2 * some * (heads * (width + LAT) + slots * width),
            transcendentals=some * heads * slots,
        ),
        name="attend_local",
    )(ranks, lengths, in_hbm(queries), in_hbm(pages), *earlier)


def load_kernel(*refs):
    count = len(refs) // 2
    copies = [
        pltpu.make_async_copy(refs[i], refs[count + i], refs[-1].at[i]) for i in range(count)
    ]
    for one in copies:
        one.start()
    for one in copies:
        one.wait()


def load(*arrays):
    return pl.pallas_call(
        load_kernel,
        out_shape=[pltpu.VMEM(w.shape, w.dtype) for w in arrays],
        in_specs=[ANYWHERE] * len(arrays),
        out_specs=[ANYWHERE] * len(arrays),
        scratch_shapes=[pltpu.SemaphoreType.DMA((len(arrays),))],
        compiler_params=pltpu.CompilerParams(vmem_limit_bytes=MIB),
        cost_estimate=pl.CostEstimate(
            flops=0, bytes_accessed=sum(2 * math.prod(w.shape) for w in arrays), transcendentals=0
        ),
        name="load",
    )(*[in_hbm(w) for w in arrays])


def attend_traded_kernel(
    groups, ranks_ref, lengths_ref, slots_ref, mask_ref, query_ref, page_ref, old_ref, out_ref
):
    partner = device_of(ranks_ref, groups, mask_ref[0])
    length = lengths_ref[partner * old_ref.shape[0] + slots_ref[partner]]
    out_ref[0] = attend_body(query_ref[0], page_ref[...], length)


def attend_traded(ranks, lengths, swap_slot, swap_mask, queries, page, attended, groups):
    _, width, heads = queries.shape
    slots = page.shape[1]

    def mine(i, ranks_ref, lengths_ref, slots_ref, mask_ref):
        return slots_ref[device_of(ranks_ref, groups)], 0, 0

    return pl.pallas_call(
        functools.partial(attend_traded_kernel, groups),
        out_shape=jax.ShapeDtypeStruct(attended.shape, attended.dtype),
        grid_spec=pltpu.PrefetchScalarGridSpec(
            num_scalar_prefetch=4,
            grid=(1,),
            in_specs=[
                pl.BlockSpec((1, width, heads), mine),
                pl.BlockSpec((width, slots), lambda i, *_: (0, 0)),
                ANYWHERE,
            ],
            out_specs=pl.BlockSpec((1, heads, LAT), mine),
        ),
        input_output_aliases={6: 0},
        compiler_params=pltpu.CompilerParams(vmem_limit_bytes=4 * MIB),
        cost_estimate=pl.CostEstimate(
            flops=2 * heads * slots * (width + LAT),
            bytes_accessed=2 * (heads * (width + LAT) + slots * width),
            transcendentals=heads * slots,
        ),
        name="attend_traded",
    )(ranks, lengths, swap_slot, swap_mask, in_hbm(queries), page, attended)


def experts_kernel(
    top,
    fetch,
    ranks_ref,
    pieces,
    gate_ref,
    up_ref,
    source_ref,
    given,
    kept_ref,
    *refs,
):
    if fetch:
        down_ref, *refs = refs
    else:
        down_ref = source_ref
    rows_ref, meta_ref, inner_ref, table_ref, sems, down_sem = refs
    experts, _, units = gate_ref.shape
    total_rows = rows_ref.shape[0]
    quarter = kept_ref.shape[1]
    ep_rank, tp_rank = ranks_ref[0], ranks_ref[1]

    def columns_of(part):
        return pl.ds(pl.multiple_of((tp_rank ^ part) * quarter, 128), quarter)

    copies = []
    for start, parts, has_meta, piece in pieces:
        rows = pl.ds(start, piece.shape[0])
        if parts is None:
            copies.append((piece, rows_ref.at[rows, :]))
            continue
        for i, part in enumerate(parts):
            copies.append(
                (piece.at[:, pl.ds(i * quarter, quarter)], rows_ref.at[rows, columns_of(part)])
            )
        if has_meta:
            copies.append((piece.at[:, pl.ds(piece.shape[1] - 128, 128)], meta_ref.at[rows, :]))
    copies = [
        pltpu.make_async_copy(source, target, sems.at[i])
        for i, (source, target) in enumerate(copies)
    ]
    for one in copies:
        one.start()
    if fetch:
        down_copy = pltpu.make_async_copy(source_ref, down_ref, down_sem)
        down_copy.start()
    for one in copies:
        one.wait()
    meta = meta_ref[...].astype(jnp.float32)
    gates = sum(pltpu.roll(meta, 128 - i * top, 1) for i in range(1, 4))
    lane = lax.broadcasted_iota(jnp.int32, meta.shape, 1)
    for e in range(experts):
        name = (ep_rank * experts + e).astype(jnp.float32)
        mine = jnp.where((lane < top) & (meta == name), gates, 0.0)
        table_ref[:, e : e + 1] = jnp.sum(mine, axis=1, keepdims=True)
    stride = math.gcd(total_rows, ROWS)
    for e in range(experts):

        @pl.loop(0, total_rows // stride)
        def _(step):
            at = pl.ds(pl.multiple_of(step * stride, stride), stride)
            rows = rows_ref[at, :]
            gate = jnp.dot(rows, gate_ref[e], preferred_element_type=jnp.float32)
            up = jnp.dot(rows, up_ref[e], preferred_element_type=jnp.float32)
            act = gate / (1.0 + jnp.exp(-gate)) * up * table_ref[at, e : e + 1]
            inner_ref[at, e * units : (e + 1) * units] = act.astype(jnp.bfloat16)

    if fetch:
        down_copy.wait()
    last = len(given) - 1
    for part, out_ref, half in (
        (3, given[0], 0),
        (1, given[last], 1 - last),
        (2, kept_ref, 0),
        (0, kept_ref, 1),
    ):

        @pl.loop(0, total_rows // stride)
        def _(step):
            at = pl.ds(pl.multiple_of(step * stride, stride), stride)
            to = pl.ds(pl.multiple_of(half * total_rows + step * stride, stride), stride)
            weight = down_ref[:, :, columns_of(part)].reshape(experts * units, quarter)
            out_ref[to, :] = jnp.dot(
                inner_ref[at, :], weight, preferred_element_type=jnp.float32
            ).astype(jnp.bfloat16)


def run_experts(ranks, pieces, w_gate, w_up, w_down, rows, columns, top, fetch, given):
    experts, width, units = w_gate.shape
    arrays = [piece for *_, piece in pieces]
    count = sum(1 if parts is None else len(parts) + has_meta for _, parts, has_meta, _ in pieces)

    def kernel(ranks_ref, refs, *others):
        named = [(*about[:3], ref) for about, ref in zip(pieces, refs)]
        experts_kernel(top, fetch, ranks_ref, named, *others)

    need = 2 * rows * (width + 128 + experts * units) + 512 * rows
    down_shape = [pltpu.VMEM(w_down.shape, w_down.dtype)] if fetch else []
    return pl.pallas_call(
        kernel,
        out_shape=[
            [pltpu.VMEM((2 * rows // given, columns), jnp.bfloat16)] * given,
            pltpu.VMEM((2 * rows, columns), jnp.bfloat16),
        ]
        + down_shape,
        in_specs=[
            IN_SMEM,
            [ANYWHERE] * len(arrays),
            IN_VMEM,
            IN_VMEM,
            ANYWHERE if fetch else IN_VMEM,
        ],
        out_specs=[[IN_VMEM] * given, IN_VMEM] + [IN_VMEM] * len(down_shape),
        scratch_shapes=[
            pltpu.VMEM((rows, width), jnp.bfloat16),
            pltpu.VMEM((rows, 128), jnp.bfloat16),
            pltpu.VMEM((rows, experts * units), jnp.bfloat16),
            pltpu.VMEM((rows, 128), jnp.float32),
            pltpu.SemaphoreType.DMA((count,)),
            pltpu.SemaphoreType.DMA,
        ],
        compiler_params=pltpu.CompilerParams(vmem_limit_bytes=need + 6 * MIB),
        cost_estimate=pl.CostEstimate(
            flops=0,
            bytes_accessed=0,
            transcendentals=0,
        ),
        name="experts",
    )(
        ranks,
        arrays,
        in_vmem(w_gate),
        in_vmem(w_up),
        in_hbm(w_down) if fetch else in_vmem(w_down),
    )


def total_of(*terms):
    value = terms[0].astype(jnp.float32)
    for term in terms[1:]:
        value = value + term.astype(jnp.float32)
    return value.astype(jnp.bfloat16)


def local(
    cache_pages,
    queries,
    lengths,
    swap_slot,
    swap_mask,
    hidden,
    expert_ids,
    gate_weights,
    w_gate,
    w_up,
    w_down,
):
    groups = lax.axis_size("tp")
    ep_size = lax.axis_size("ep")
    ranks = jnp.stack([lax.axis_index("ep"), lax.axis_index("tp")]).astype(jnp.int32)
    mask_value = swap_mask[0]
    columns = hidden.shape[1] // groups
    top = expert_ids.shape[1]
    cache_pages = jnp.swapaxes(cache_pages, 1, 2)
    queries = jnp.swapaxes(queries, 1, 2)

    rows = hidden.shape[0]
    pairs = ep_size // 2
    late = list(range(2, pairs))
    half = len(late) // 2
    rest = len(late) - half
    levels = ep_size.bit_length() - 1
    tie = lax.optimization_barrier

    def cut(array, start, count):
        return lax.slice_in_dim(array, start * rows, (start + count) * rows, axis=0)

    def bare(array):
        return array[:, :columns]

    def page_take(page, swapped, level):
        bit = jnp.bitwise_and(jnp.right_shift(mask_value, level), 1) == 1
        return jnp.where(bit, swapped, page)

    def page_hop(page, level):
        return page_take(page, flip(page, "ep", 1 << level), level)

    def page_far(page):
        for level in range(levels - 1, 2, -1):
            page = page_hop(page, level)
        return flip(page, "ep", 4) if levels > 2 else page, page

    own, both, page = pick(
        ranks, swap_slot, expert_ids, gate_weights, hidden, cache_pages, groups
    )
    late_pieces = [flip(own, "ep", 2 * m) for m in late]
    near_2 = flip(own, "ep", 2)
    both_1 = flip(both, "ep", 1)

    near_2, w_gate, w_up = tie((near_2, w_gate, w_up))
    far_2 = flip(bare(near_2), "tp", 2)
    near_3 = flip(near_2, "ep", 1)
    w_gate, w_up = load(w_gate, w_up)
    far_2, near_3, w_gate, w_up, page, both_1, *late_pieces = tie(
        (far_2, near_3, w_gate, w_up, page, both_1, *late_pieces)
    )
    near_late = jnp.concatenate(late_pieces, axis=0)
    far_3 = flip(jnp.concatenate([bare(near_3), bare(near_late)], axis=0), "tp", 2)
    near_odds = flip(near_late, "ep", 1)
    near_23 = flip(jnp.concatenate([near_2, near_3], axis=0), "tp", 1)
    early = [flip(array, "tp", 1) for array in (both_1, far_2)]
    queries, near_23, early = tie((queries, near_23, early))
    count = queries.shape[0]
    some = count // 4
    attended = attend_part(ranks, lengths, queries, cache_pages, groups, 0, some)
    least = page.shape[0] // 4
    upper, lower = jnp.split(page, [least], axis=0)
    swapped, upper = page_far(upper)
    far_3, near_late, near_odds, attended, swapped = tie(
        (far_3, near_late, near_odds, attended, swapped)
    )
    upper = page_take(upper, swapped, 2) if levels > 2 else upper
    page = jnp.concatenate([upper, lower], axis=0)
    core_3 = flip(far_3, "tp", 1)
    far_late, core_late = cut(far_3, 1, len(late)), cut(core_3, 1, len(late))
    far_3, core_3 = cut(far_3, 0, 1), cut(core_3, 0, 1)
    far_odds = flip(bare(near_odds), "tp", 2)

    def piece(start, part, array):
        return start * rows, (part,), part == 0, array

    pieces = [(0, None, False, hidden), (0, (), True, own)]
    pieces += [(rows, (0, 2), True, both_1), (rows, (1, 3), False, early[0])]
    pieces += [piece(2, 0, near_2), piece(3, 0, near_3), (2 * rows, (1,), False, near_23)]
    pieces += [piece(2, 2, far_2), piece(2, 3, early[1])]
    pieces += [piece(3, 2, far_3), piece(3, 3, core_3)]
    *first, w_down = run_experts(
        ranks, pieces, w_gate, w_up, w_down, 4 * rows, columns, top, True, 1
    )
    near_both = jnp.concatenate([near_late, near_odds], axis=0)
    early = flip(near_both, "tp", 1)
    swapped = flip(page, "ep", 1)
    first, far_odds, early, swapped = tie((first, far_odds, early, swapped))
    page = page_take(page, swapped, 0)

    (given,), own = first
    sent, kept = jnp.split(total_of(own, flip(given, "tp", 1)), 2, axis=0)
    last = flip(far_odds, "tp", 1)
    over_23 = flip(cut(sent, 2, 2), "tp", 2)
    over_1 = flip(jnp.concatenate([cut(kept, 1, 1), cut(sent, 1, 1)], axis=1), "ep", 1)
    swapped = flip(page, "ep", 2)
    odds = len(late)
    pieces = [piece(0, 0, near_both), (0, (1,), False, early)]
    pieces += [piece(0, 2, far_late), piece(0, 3, core_late)]
    pieces += [piece(odds, 2, far_odds), piece(odds, 3, last)]
    second = [
        *run_experts(
            ranks, pieces, w_gate, w_up, w_down, 2 * len(late) * rows, columns, top, False, 2
        )
    ]
    second, over_23, over_1, swapped = tie((second, over_23, over_1, swapped))
    page = page_take(page, swapped, 1)
    upper, lower = jnp.split(page, [least], axis=0)
    swapped, lower = page_far(lower)
    (cross, side), own = second
    late_sent, late_kept = jnp.split(own, 2, axis=0)
    late_sent = total_of(late_sent, flip(cross, "tp", 1))
    over_3 = flip(total_of(cut(kept, 3, 1), cut(over_23, 1, 1)), "ep", 1)
    zero = flip(total_of(cut(sent, 0, 1), over_1[:, columns:]), "tp", 2)
    late_sent, side, queries = tie((late_sent, side, queries))
    side = flip(side, "tp", 1)

    over_y = flip(cut(late_sent, len(late), half), "tp", 2)
    over_x = flip(cut(late_sent, len(late) + half, rest), "ep", 1)
    attended = attend_part(
        ranks, lengths, queries, cache_pages, groups, some, some, attended
    )
    over_y, over_x, over_3, side, attended = tie((over_y, over_x, over_3, side, attended))
    late_kept = total_of(late_kept, side)
    odd = total_of(
        cut(late_kept, len(late), len(late)), jnp.pad(over_y, ((0, rest * rows), (0, 0)))
    )
    odd = flip(odd, "ep", 1)
    even = total_of(cut(late_sent, 0, len(late)), jnp.pad(over_x, ((half * rows, 0), (0, 0))))
    even = flip(even, "tp", 2)
    attended = attend_part(
        ranks, lengths, queries, cache_pages, groups, 2 * some, count - 2 * some, attended
    )
    odd, even, attended, swapped = tie((odd, even, attended, swapped))
    lower = page_take(lower, swapped, 2) if levels > 2 else lower
    page = jnp.concatenate([upper, lower], axis=0)
    even = total_of(cut(late_kept, 0, len(late)), even, odd)
    back = [flip(cut(even, i, 1), "ep", 2 * m) for i, m in enumerate(late)]
    back.append(flip(total_of(cut(kept, 2, 1), cut(over_23, 0, 1), over_3), "ep", 2))
    attended = attend_traded(
        ranks, lengths, swap_slot, swap_mask, queries, page, attended, groups
    )
    *back, attended = tie((*back, attended))
    moe_out = total_of(cut(kept, 0, 1), over_1[:, :columns], zero, *back)
    return attended, moe_out


def solution(mesh):
    in_specs = (
        P(("ep", "tp"), None, None),
        P(("ep", "tp"), None, None),
        P(),
        P(),
        P(),
        P("ep", None),
        P("ep", None),
        P("ep", None),
        P("ep", None, "tp"),
        P("ep", None, "tp"),
        P("ep", "tp", None),
    )
    out_specs = (P(("ep", "tp"), None, None), P("ep", "tp"))
    return jax.shard_map(local, mesh=mesh, in_specs=in_specs, out_specs=out_specs, check_vma=False)
```

```python
import functools
import math

import jax
import jax.numpy as jnp
from jax import lax
from jax.experimental import pallas as pl
from jax.experimental.pallas import tpu as pltpu
from jax.sharding import PartitionSpec as P

LAT = 512
SCORE_SCALE = 192.0 ** (-0.5)
MASK_FLOOR = -1e30
ROWS = 512
MIB = 1 << 20


def flip(block, axis, apart):
    count = lax.axis_size(axis)
    return lax.ppermute(block, axis, [(i, i ^ apart) for i in range(count)])


def attend_body(query, page, length):
    scores = (
        lax.dot_general(query, page, (((0,), (0,)), ((), ())), preferred_element_type=jnp.float32)
        * SCORE_SCALE
    )
    live = lax.broadcasted_iota(jnp.int32, scores.shape, 1) < length
    scores = jnp.where(live, scores, MASK_FLOOR)
    top = jnp.max(scores, axis=1, keepdims=True)
    weight = jnp.where(live, jnp.exp(scores - top), 0.0)
    total = jnp.sum(weight, axis=1, keepdims=True)
    blended = lax.dot_general(
        weight.astype(jnp.bfloat16),
        page[:LAT],
        (((1,), (1,)), ((), ())),
        preferred_element_type=jnp.float32,
    )
    return (blended / total).astype(jnp.bfloat16)


def in_hbm(array):
    return pltpu.with_memory_space_constraint(array, pltpu.HBM)


def in_vmem(array):
    return pltpu.with_memory_space_constraint(array, pltpu.VMEM)


ANYWHERE = pl.BlockSpec(memory_space=pl.ANY)
IN_VMEM = pl.BlockSpec(memory_space=pltpu.VMEM)
IN_SMEM = pl.BlockSpec(memory_space=pltpu.SMEM)


def device_of(ranks_ref, groups, mask=0):
    return (ranks_ref[0] ^ mask) * groups + ranks_ref[1]


def pick_kernel(groups, ranks_ref, slots_ref, ids_ref, gates_ref, hidden_ref, pages_ref, near_ref, both_ref, page_ref, sems):
    rows = hidden_ref.shape[0]
    columns = hidden_ref.shape[1] // groups

    def quarter(part):
        start = pl.multiple_of((ranks_ref[1] ^ part) * columns, 128)
        return hidden_ref.at[:, pl.ds(start, columns)]

    copies = [
        (quarter(0), near_ref.at[:, pl.ds(0, columns)]),
        (quarter(0), both_ref.at[:, pl.ds(0, columns)]),
        (quarter(2), both_ref.at[:, pl.ds(columns, columns)]),
        (pages_ref.at[slots_ref[device_of(ranks_ref, groups)]], page_ref),
    ]
    copies = [pltpu.make_async_copy(*pair, sems.at[i]) for i, pair in enumerate(copies)]
    for one in copies:
        one.start()
    gates = gates_ref[...]
    high = gates.astype(jnp.bfloat16).astype(jnp.float32)
    middle = (gates - high).astype(jnp.bfloat16).astype(jnp.float32)
    low = gates - high - middle
    top = gates.shape[0]
    table = jnp.concatenate(
        [ids_ref[...].astype(jnp.float32), high, middle, low, jnp.zeros((128 - 4 * top, rows), jnp.float32)],
        axis=0,
    )
    table = jnp.concatenate([table, jnp.zeros((128, 128 - rows), jnp.float32)], axis=1)
    table = table.T[:rows].astype(jnp.bfloat16)
    near_ref[:, columns:] = table
    both_ref[:, 2 * columns :] = table
    for one in copies:
        one.wait()


def pick(ranks, swap_slot, expert_ids, gate_weights, hidden, pages, groups):
    rows, width = hidden.shape
    columns = width // groups
    return pl.pallas_call(
        functools.partial(pick_kernel, groups),
        out_shape=(
            pltpu.VMEM((rows, columns + 128), jnp.bfloat16),
            pltpu.VMEM((rows, 2 * columns + 128), jnp.bfloat16),
            pltpu.VMEM(pages.shape[1:], jnp.bfloat16),
        ),
        in_specs=[IN_SMEM, IN_SMEM, IN_VMEM, IN_VMEM, ANYWHERE, ANYWHERE],
        out_specs=(IN_VMEM, IN_VMEM, IN_VMEM),
        scratch_shapes=[pltpu.SemaphoreType.DMA((4,))],
        compiler_params=pltpu.CompilerParams(vmem_limit_bytes=2 * MIB),
        name="pick",
    )(
        ranks,
        in_hbm(swap_slot),
        in_hbm(expert_ids.T),
        in_hbm(gate_weights.T),
        in_hbm(hidden),
        in_hbm(pages),
    )


def attend_part(ranks, lengths, queries, pages, groups, first, some, before=None):
    count, width, heads = queries.shape
    slots = pages.shape[2]
    each = math.gcd(some, 2)
    skip = first // each

    def kernel(ranks_ref, lengths_ref, query_ref, page_ref, *refs):
        start = device_of(ranks_ref, groups) * count + first + pl.program_id(0) * each
        for i in range(each):
            refs[-1][i] = attend_body(query_ref[i], page_ref[i], lengths_ref[start + i])

    earlier = [] if before is None else [before]
    return pl.pallas_call(
        kernel,
        out_shape=jax.ShapeDtypeStruct((count, heads, LAT), jnp.bfloat16),
        grid_spec=pltpu.PrefetchScalarGridSpec(
            num_scalar_prefetch=2,
            grid=(some // each,),
            in_specs=[
                pl.BlockSpec((each, width, heads), lambda i, *_: (skip + i, 0, 0)),
                pl.BlockSpec((each, width, slots), lambda i, *_: (skip + i, 0, 0)),
            ]
            + [ANYWHERE] * len(earlier),
            out_specs=pl.BlockSpec((each, heads, LAT), lambda i, *_: (skip + i, 0, 0)),
        ),
        input_output_aliases={4: 0} if earlier else {},
        compiler_params=pltpu.CompilerParams(vmem_limit_bytes=8 * MIB),
        cost_estimate=pl.CostEstimate(
            flops=2 * some * heads * slots * (width + LAT),
            bytes_accessed=2 * some * (heads * (width + LAT) + slots * width),
            transcendentals=some * heads * slots,
        ),
        name="attend_local",
    )(ranks, lengths, in_hbm(queries), in_hbm(pages), *earlier)


def load_kernel(*refs):
    count = len(refs) // 2
    copies = [
        pltpu.make_async_copy(refs[i], refs[count + i], refs[-1].at[i]) for i in range(count)
    ]
    for one in copies:
        one.start()
    for one in copies:
        one.wait()


def load(*arrays):
    return pl.pallas_call(
        load_kernel,
        out_shape=[pltpu.VMEM(w.shape, w.dtype) for w in arrays],
        in_specs=[ANYWHERE] * len(arrays),
        out_specs=[ANYWHERE] * len(arrays),
        scratch_shapes=[pltpu.SemaphoreType.DMA((len(arrays),))],
        compiler_params=pltpu.CompilerParams(vmem_limit_bytes=MIB),
        cost_estimate=pl.CostEstimate(
            flops=0, bytes_accessed=sum(2 * math.prod(w.shape) for w in arrays), transcendentals=0
        ),
        name="load",
    )(*[in_hbm(w) for w in arrays])


def attend_traded_kernel(
    groups, ranks_ref, lengths_ref, slots_ref, mask_ref, query_ref, page_ref, old_ref, out_ref
):
    partner = device_of(ranks_ref, groups, mask_ref[0])
    length = lengths_ref[partner * old_ref.shape[0] + slots_ref[partner]]
    out_ref[0] = attend_body(query_ref[0], page_ref[...], length)


def attend_traded(ranks, lengths, swap_slot, swap_mask, queries, page, attended, groups):
    _, width, heads = queries.shape
    slots = page.shape[1]

    def mine(i, ranks_ref, lengths_ref, slots_ref, mask_ref):
        return slots_ref[device_of(ranks_ref, groups)], 0, 0

    return pl.pallas_call(
        functools.partial(attend_traded_kernel, groups),
        out_shape=jax.ShapeDtypeStruct(attended.shape, attended.dtype),
        grid_spec=pltpu.PrefetchScalarGridSpec(
            num_scalar_prefetch=4,
            grid=(1,),
            in_specs=[
                pl.BlockSpec((1, width, heads), mine),
                pl.BlockSpec((width, slots), lambda i, *_: (0, 0)),
                ANYWHERE,
            ],
            out_specs=pl.BlockSpec((1, heads, LAT), mine),
        ),
        input_output_aliases={6: 0},
        compiler_params=pltpu.CompilerParams(vmem_limit_bytes=4 * MIB),
        cost_estimate=pl.CostEstimate(
            flops=2 * heads * slots * (width + LAT),
            bytes_accessed=2 * (heads * (width + LAT) + slots * width),
            transcendentals=heads * slots,
        ),
        name="attend_traded",
    )(ranks, lengths, swap_slot, swap_mask, in_hbm(queries), page, attended)


def experts_kernel(
    top,
    fetch,
    ranks_ref,
    pieces,
    gate_ref,
    up_ref,
    source_ref,
    given,
    kept_ref,
    *refs,
):
    if fetch:
        down_ref, *refs = refs
    else:
        down_ref = source_ref
    rows_ref, meta_ref, inner_ref, table_ref, sems, down_sem = refs
    experts, _, units = gate_ref.shape
    total_rows = rows_ref.shape[0]
    quarter = kept_ref.shape[1]
    ep_rank, tp_rank = ranks_ref[0], ranks_ref[1]

    def columns_of(part):
        return pl.ds(pl.multiple_of((tp_rank ^ part) * quarter, 128), quarter)

    copies = []
    for start, parts, has_meta, piece in pieces:
        rows = pl.ds(start, piece.shape[0])
        if parts is None:
            copies.append((piece, rows_ref.at[rows, :]))
            continue
        for i, part in enumerate(parts):
            copies.append(
                (piece.at[:, pl.ds(i * quarter, quarter)], rows_ref.at[rows, columns_of(part)])
            )
        if has_meta:
            copies.append((piece.at[:, pl.ds(piece.shape[1] - 128, 128)], meta_ref.at[rows, :]))
    copies = [
        pltpu.make_async_copy(source, target, sems.at[i])
        for i, (source, target) in enumerate(copies)
    ]
    for one in copies:
        one.start()
    if fetch:
        down_copy = pltpu.make_async_copy(source_ref, down_ref, down_sem)
        down_copy.start()
    for one in copies:
        one.wait()
    meta = meta_ref[...].astype(jnp.float32)
    gates = sum(pltpu.roll(meta, 128 - i * top, 1) for i in range(1, 4))
    lane = lax.broadcasted_iota(jnp.int32, meta.shape, 1)
    for e in range(experts):
        name = (ep_rank * experts + e).astype(jnp.float32)
        mine = jnp.where((lane < top) & (meta == name), gates, 0.0)
        table_ref[:, e : e + 1] = jnp.sum(mine, axis=1, keepdims=True)
    stride = math.gcd(total_rows, ROWS)
    for e in range(experts):

        @pl.loop(0, total_rows // stride)
        def _(step):
            at = pl.ds(pl.multiple_of(step * stride, stride), stride)
            rows = rows_ref[at, :]
            gate = jnp.dot(rows, gate_ref[e], preferred_element_type=jnp.float32)
            up = jnp.dot(rows, up_ref[e], preferred_element_type=jnp.float32)
            act = gate / (1.0 + jnp.exp(-gate)) * up * table_ref[at, e : e + 1]
            inner_ref[at, e * units : (e + 1) * units] = act.astype(jnp.bfloat16)

    if fetch:
        down_copy.wait()
    last = len(given) - 1
    for part, out_ref, half in (
        (3, given[0], 0),
        (1, given[last], 1 - last),
        (2, kept_ref, 0),
        (0, kept_ref, 1),
    ):

        @pl.loop(0, total_rows // stride)
        def _(step):
            at = pl.ds(pl.multiple_of(step * stride, stride), stride)
            to = pl.ds(pl.multiple_of(half * total_rows + step * stride, stride), stride)
            weight = down_ref[:, :, columns_of(part)].reshape(experts * units, quarter)
            out_ref[to, :] = jnp.dot(
                inner_ref[at, :], weight, preferred_element_type=jnp.float32
            ).astype(jnp.bfloat16)


def run_experts(ranks, pieces, w_gate, w_up, w_down, rows, columns, top, fetch, given):
    experts, width, units = w_gate.shape
    arrays = [piece for *_, piece in pieces]
    count = sum(1 if parts is None else len(parts) + has_meta for _, parts, has_meta, _ in pieces)

    def kernel(ranks_ref, refs, *others):
        named = [(*about[:3], ref) for about, ref in zip(pieces, refs)]
        experts_kernel(top, fetch, ranks_ref, named, *others)

    need = 2 * rows * (width + 128 + experts * units) + 512 * rows
    down_shape = [pltpu.VMEM(w_down.shape, w_down.dtype)] if fetch else []
    return pl.pallas_call(
        kernel,
        out_shape=[
            [pltpu.VMEM((2 * rows // given, columns), jnp.bfloat16)] * given,
            pltpu.VMEM((2 * rows, columns), jnp.bfloat16),
        ]
        + down_shape,
        in_specs=[
            IN_SMEM,
            [ANYWHERE] * len(arrays),
            IN_VMEM,
            IN_VMEM,
            ANYWHERE if fetch else IN_VMEM,
        ],
        out_specs=[[IN_VMEM] * given, IN_VMEM] + [IN_VMEM] * len(down_shape),
        scratch_shapes=[
            pltpu.VMEM((rows, width), jnp.bfloat16),
            pltpu.VMEM((rows, 128), jnp.bfloat16),
            pltpu.VMEM((rows, experts * units), jnp.bfloat16),
            pltpu.VMEM((rows, 128), jnp.float32),
            pltpu.SemaphoreType.DMA((count,)),
            pltpu.SemaphoreType.DMA,
        ],
        compiler_params=pltpu.CompilerParams(vmem_limit_bytes=need + 6 * MIB),
        cost_estimate=pl.CostEstimate(
            flops=0,
            bytes_accessed=0,
            transcendentals=0,
        ),
        name="experts",
    )(
        ranks,
        arrays,
        in_vmem(w_gate),
        in_vmem(w_up),
        in_hbm(w_down) if fetch else in_vmem(w_down),
    )


def total_of(*terms):
    value = terms[0].astype(jnp.float32)
    for term in terms[1:]:
        value = value + term.astype(jnp.float32)
    return value.astype(jnp.bfloat16)


def local(
    cache_pages,
    queries,
    lengths,
    swap_slot,
    swap_mask,
    hidden,
    expert_ids,
    gate_weights,
    w_gate,
    w_up,
    w_down,
):
    groups = lax.axis_size("tp")
    ep_size = lax.axis_size("ep")
    ranks = jnp.stack([lax.axis_index("ep"), lax.axis_index("tp")]).astype(jnp.int32)
    mask_value = swap_mask[0]
    columns = hidden.shape[1] // groups
    top = expert_ids.shape[1]
    cache_pages = jnp.swapaxes(cache_pages, 1, 2)
    queries = jnp.swapaxes(queries, 1, 2)

    rows = hidden.shape[0]
    pairs = ep_size // 2
    late = list(range(2, pairs))
    levels = ep_size.bit_length() - 1
    tie = lax.optimization_barrier

    def cut(array, start, count):
        return lax.slice_in_dim(array, start * rows, (start + count) * rows, axis=0)

    def bare(array):
        return array[:, :columns]

    def page_take(page, swapped, level):
        bit = jnp.bitwise_and(jnp.right_shift(mask_value, level), 1) == 1
        return jnp.where(bit, swapped, page)

    def page_hop(page, level):
        return page_take(page, flip(page, "ep", 1 << level), level)

    def page_far(page):
        for level in range(levels - 1, 2, -1):
            page = page_hop(page, level)
        return flip(page, "ep", 4) if levels > 2 else page, page

    own, both, page = pick(
        ranks, swap_slot, expert_ids, gate_weights, hidden, cache_pages, groups
    )
    late_pieces = [flip(own, "ep", 2 * m) for m in late]
    near_2 = flip(own, "ep", 2)
    both_1 = flip(both, "ep", 1)

    near_2, w_gate, w_up = tie((near_2, w_gate, w_up))
    far_2 = flip(bare(near_2), "tp", 2)
    near_3 = flip(near_2, "ep", 1)
    w_gate, w_up = load(w_gate, w_up)
    far_2, near_3, w_gate, w_up, page, both_1, *late_pieces = tie(
        (far_2, near_3, w_gate, w_up, page, both_1, *late_pieces)
    )
    near_late = jnp.concatenate(late_pieces, axis=0)
    far_3 = flip(jnp.concatenate([bare(near_3), bare(near_late)], axis=0), "tp", 2)
    near_odds = flip(near_late, "ep", 1)
    near_23 = flip(jnp.concatenate([near_2, near_3], axis=0), "tp", 1)
    early = [flip(array, "tp", 1) for array in (both_1, far_2)]
    queries, near_23, early = tie((queries, near_23, early))
    count = queries.shape[0]
    some = count // 4
    attended = attend_part(ranks, lengths, queries, cache_pages, groups, 0, some)
    least = page.shape[0] // 4
    upper, lower = jnp.split(page, [least], axis=0)
    swapped, upper = page_far(upper)
    far_3, near_late, near_odds, attended, swapped = tie(
        (far_3, near_late, near_odds, attended, swapped)
    )
    upper = page_take(upper, swapped, 2) if levels > 2 else upper
    page = jnp.concatenate([upper, lower], axis=0)
    core_3 = flip(far_3, "tp", 1)
    far_late, core_late = cut(far_3, 1, len(late)), cut(core_3, 1, len(late))
    far_3, core_3 = cut(far_3, 0, 1), cut(core_3, 0, 1)
    far_odds = flip(bare(near_odds), "tp", 2)

    def piece(start, part, array):
        return start * rows, (part,), part == 0, array

    pieces = [(0, None, False, hidden), (0, (), True, own)]
    pieces += [(rows, (0, 2), True, both_1), (rows, (1, 3), False, early[0])]
    pieces += [piece(2, 0, near_2), piece(3, 0, near_3), (2 * rows, (1,), False, near_23)]
    pieces += [piece(2, 2, far_2), piece(2, 3, early[1])]
    pieces += [piece(3, 2, far_3), piece(3, 3, core_3)]
    *first, w_down = run_experts(
        ranks, pieces, w_gate, w_up, w_down, 4 * rows, columns, top, True, 1
    )
    near_both = jnp.concatenate([near_late, near_odds], axis=0)
    early = flip(near_both, "tp", 1)
    swapped = flip(page, "ep", 1)
    first, far_odds, early, swapped = tie((first, far_odds, early, swapped))
    page = page_take(page, swapped, 0)

    (given,), own = first
    sent, kept = jnp.split(total_of(own, flip(given, "tp", 1)), 2, axis=0)
    last = flip(far_odds, "tp", 1)
    sent, kept, last = tie((sent, kept, last))
    over_23 = flip(cut(sent, 2, 2), "tp", 2)
    over_1 = flip(jnp.concatenate([cut(kept, 1, 1), cut(sent, 1, 1)], axis=1), "ep", 1)
    swapped = flip(page, "ep", 2)
    odds = len(late)
    pieces = [piece(0, 0, near_both), (0, (1,), False, early)]
    pieces += [piece(0, 2, far_late), piece(0, 3, core_late)]
    pieces += [piece(odds, 2, far_odds), piece(odds, 3, last)]
    second = [
        *run_experts(
            ranks, pieces, w_gate, w_up, w_down, 2 * len(late) * rows, columns, top, False, 2
        )
    ]
    second, over_23, swapped = tie((second, over_23, swapped))
    page = page_take(page, swapped, 1)
    upper, lower = jnp.split(page, [least], axis=0)
    swapped, lower = page_far(lower)
    (cross, side), own = second
    late_sent, late_kept = jnp.split(own, 2, axis=0)
    late_sent = total_of(late_sent, flip(cross, "tp", 1))
    over_3 = flip(total_of(cut(kept, 3, 1), cut(over_23, 1, 1)), "ep", 1)
    late_sent, side, queries = tie((late_sent, side, queries))
    side = flip(side, "tp", 1)

    odd = flip(cut(late_sent, len(late), len(late)), "tp", 2)
    even = flip(cut(late_sent, 0, len(late)), "tp", 2)
    attended = attend_part(
        ranks, lengths, queries, cache_pages, groups, some, some, attended
    )
    odd, over_1, over_3, side, attended = tie((odd, over_1, over_3, side, attended))
    zero = flip(total_of(cut(sent, 0, 1), over_1[:, columns:]), "tp", 2)
    late_kept = total_of(late_kept, side)
    odd = flip(total_of(cut(late_kept, len(late), len(late)), odd), "ep", 1)
    attended = attend_part(
        ranks, lengths, queries, cache_pages, groups, 2 * some, count - 2 * some, attended
    )
    odd, even, attended, swapped = tie((odd, even, attended, swapped))
    lower = page_take(lower, swapped, 2) if levels > 2 else lower
    page = jnp.concatenate([upper, lower], axis=0)
    even = total_of(cut(late_kept, 0, len(late)), even, odd)
    back = [flip(cut(even, i, 1), "ep", 2 * m) for i, m in enumerate(late)]
    back.append(flip(total_of(cut(kept, 2, 1), cut(over_23, 0, 1), over_3), "ep", 2))
    attended = attend_traded(
        ranks, lengths, swap_slot, swap_mask, queries, page, attended, groups
    )
    *back, attended = tie((*back, attended))
    moe_out = total_of(cut(kept, 0, 1), over_1[:, :columns], zero, *back)
    return attended, moe_out


def solution(mesh):
    in_specs = (
        P(("ep", "tp"), None, None),
        P(("ep", "tp"), None, None),
        P(),
        P(),
        P(),
        P("ep", None),
        P("ep", None),
        P("ep", None),
        P("ep", None, "tp"),
        P("ep", None, "tp"),
        P("ep", "tp", None),
    )
    out_specs = (P(("ep", "tp"), None, None), P("ep", "tp"))
    return jax.shard_map(local, mesh=mesh, in_specs=in_specs, out_specs=out_specs, check_vma=False)
```

```python
import functools
import math

import jax
import jax.numpy as jnp
from jax import lax
from jax.experimental import pallas as pl
from jax.experimental.pallas import tpu as pltpu
from jax.sharding import PartitionSpec as P

LAT = 512
SCORE_SCALE = 192.0 ** (-0.5)
MASK_FLOOR = -1e30
ROWS = 512
MIB = 1 << 20


def flip(block, axis, apart):
    count = lax.axis_size(axis)
    return lax.ppermute(block, axis, [(i, i ^ apart) for i in range(count)])


def attend_body(query, page, length):
    scores = (
        lax.dot_general(query, page, (((0,), (0,)), ((), ())), preferred_element_type=jnp.float32)
        * SCORE_SCALE
    )
    live = lax.broadcasted_iota(jnp.int32, scores.shape, 1) < length
    scores = jnp.where(live, scores, MASK_FLOOR)
    top = jnp.max(scores, axis=1, keepdims=True)
    weight = jnp.where(live, jnp.exp(scores - top), 0.0)
    total = jnp.sum(weight, axis=1, keepdims=True)
    blended = lax.dot_general(
        weight.astype(jnp.bfloat16),
        page[:LAT],
        (((1,), (1,)), ((), ())),
        preferred_element_type=jnp.float32,
    )
    return (blended / total).astype(jnp.bfloat16)


def in_hbm(array):
    return pltpu.with_memory_space_constraint(array, pltpu.HBM)


def in_vmem(array):
    return pltpu.with_memory_space_constraint(array, pltpu.VMEM)


ANYWHERE = pl.BlockSpec(memory_space=pl.ANY)
IN_VMEM = pl.BlockSpec(memory_space=pltpu.VMEM)
IN_SMEM = pl.BlockSpec(memory_space=pltpu.SMEM)


def device_of(ranks_ref, groups, mask=0):
    return (ranks_ref[0] ^ mask) * groups + ranks_ref[1]


def pick_kernel(groups, ranks_ref, slots_ref, ids_ref, gates_ref, hidden_ref, pages_ref, near_ref, both_ref, page_ref, sems):
    rows = hidden_ref.shape[0]
    columns = hidden_ref.shape[1] // groups

    def quarter(part):
        start = pl.multiple_of((ranks_ref[1] ^ part) * columns, 128)
        return hidden_ref.at[:, pl.ds(start, columns)]

    copies = [
        (quarter(0), near_ref.at[:, pl.ds(0, columns)]),
        (quarter(0), both_ref.at[:, pl.ds(0, columns)]),
        (quarter(2), both_ref.at[:, pl.ds(columns, columns)]),
        (pages_ref.at[slots_ref[device_of(ranks_ref, groups)]], page_ref),
    ]
    copies = [pltpu.make_async_copy(*pair, sems.at[i]) for i, pair in enumerate(copies)]
    for one in copies:
        one.start()
    gates = gates_ref[...]
    high = gates.astype(jnp.bfloat16).astype(jnp.float32)
    middle = (gates - high).astype(jnp.bfloat16).astype(jnp.float32)
    low = gates - high - middle
    top = gates.shape[0]
    table = jnp.concatenate(
        [ids_ref[...].astype(jnp.float32), high, middle, low, jnp.zeros((128 - 4 * top, rows), jnp.float32)],
        axis=0,
    )
    table = jnp.concatenate([table, jnp.zeros((128, 128 - rows), jnp.float32)], axis=1)
    table = table.T[:rows].astype(jnp.bfloat16)
    near_ref[:, columns:] = table
    both_ref[:, 2 * columns :] = table
    for one in copies:
        one.wait()


def pick(ranks, swap_slot, expert_ids, gate_weights, hidden, pages, groups):
    rows, width = hidden.shape
    columns = width // groups
    return pl.pallas_call(
        functools.partial(pick_kernel, groups),
        out_shape=(
            pltpu.VMEM((rows, columns + 128), jnp.bfloat16),
            pltpu.VMEM((rows, 2 * columns + 128), jnp.bfloat16),
            pltpu.VMEM(pages.shape[1:], jnp.bfloat16),
        ),
        in_specs=[IN_SMEM, IN_SMEM, IN_VMEM, IN_VMEM, ANYWHERE, ANYWHERE],
        out_specs=(IN_VMEM, IN_VMEM, IN_VMEM),
        scratch_shapes=[pltpu.SemaphoreType.DMA((4,))],
        compiler_params=pltpu.CompilerParams(vmem_limit_bytes=2 * MIB),
        name="pick",
    )(
        ranks,
        in_hbm(swap_slot),
        in_hbm(expert_ids.T),
        in_hbm(gate_weights.T),
        in_hbm(hidden),
        in_hbm(pages),
    )


def attend_part(ranks, lengths, queries, pages, groups, first, some, before=None):
    count, width, heads = queries.shape
    slots = pages.shape[2]
    each = math.gcd(some, 2)
    skip = first // each

    def kernel(ranks_ref, lengths_ref, query_ref, page_ref, *refs):
        start = device_of(ranks_ref, groups) * count + first + pl.program_id(0) * each
        for i in range(each):
            refs[-1][i] = attend_body(query_ref[i], page_ref[i], lengths_ref[start + i])

    earlier = [] if before is None else [before]
    return pl.pallas_call(
        kernel,
        out_shape=jax.ShapeDtypeStruct((count, heads, LAT), jnp.bfloat16),
        grid_spec=pltpu.PrefetchScalarGridSpec(
            num_scalar_prefetch=2,
            grid=(some // each,),
            in_specs=[
                pl.BlockSpec((each, width, heads), lambda i, *_: (skip + i, 0, 0)),
                pl.BlockSpec((each, width, slots), lambda i, *_: (skip + i, 0, 0)),
            ]
            + [ANYWHERE] * len(earlier),
            out_specs=pl.BlockSpec((each, heads, LAT), lambda i, *_: (skip + i, 0, 0)),
        ),
        input_output_aliases={4: 0} if earlier else {},
        compiler_params=pltpu.CompilerParams(vmem_limit_bytes=8 * MIB),
        cost_estimate=pl.CostEstimate(flops=0, bytes_accessed=0, transcendentals=0),
        name="attend_local",
    )(ranks, lengths, in_hbm(queries), in_hbm(pages), *earlier)


def load_kernel(*refs):
    count = len(refs) // 2
    copies = [
        pltpu.make_async_copy(refs[i], refs[count + i], refs[-1].at[i]) for i in range(count)
    ]
    for one in copies:
        one.start()
    for one in copies:
        one.wait()


def load(*arrays):
    return pl.pallas_call(
        load_kernel,
        out_shape=[pltpu.VMEM(w.shape, w.dtype) for w in arrays],
        in_specs=[ANYWHERE] * len(arrays),
        out_specs=[ANYWHERE] * len(arrays),
        scratch_shapes=[pltpu.SemaphoreType.DMA((len(arrays),))],
        compiler_params=pltpu.CompilerParams(vmem_limit_bytes=MIB),
        cost_estimate=pl.CostEstimate(
            flops=0, bytes_accessed=sum(2 * math.prod(w.shape) for w in arrays), transcendentals=0
        ),
        name="load",
    )(*[in_hbm(w) for w in arrays])


def attend_rest(
    ranks, lengths, swap_slot, swap_mask, queries, pages, page, attended, groups, first
):
    count, width, heads = queries.shape
    slots = pages.shape[2]
    some = count - first

    def kernel(
        ranks_ref,
        lengths_ref,
        slots_ref,
        mask_ref,
        query_ref,
        pages_ref,
        page_ref,
        old_ref,
        out_ref,
    ):
        step = pl.program_id(0)

        @pl.when(step < some)
        def _():
            at = device_of(ranks_ref, groups) * count + first + step
            out_ref[0] = attend_body(query_ref[0], pages_ref[0], lengths_ref[at])

        @pl.when(step == some)
        def _():
            partner = device_of(ranks_ref, groups, mask_ref[0])
            length = lengths_ref[partner * count + slots_ref[partner]]
            out_ref[0] = attend_body(query_ref[0], page_ref[...], length)

    def request(i, ranks_ref, lengths_ref, slots_ref, mask_ref):
        return jnp.where(i < some, first + i, slots_ref[device_of(ranks_ref, groups)]), 0, 0

    return pl.pallas_call(
        kernel,
        out_shape=jax.ShapeDtypeStruct(attended.shape, attended.dtype),
        grid_spec=pltpu.PrefetchScalarGridSpec(
            num_scalar_prefetch=4,
            grid=(some + 1,),
            in_specs=[
                pl.BlockSpec((1, width, heads), request),
                pl.BlockSpec(
                    (1, width, slots), lambda i, *_: (jnp.minimum(first + i, count - 1), 0, 0)
                ),
                pl.BlockSpec((width, slots), lambda i, *_: (0, 0)),
                ANYWHERE,
            ],
            out_specs=pl.BlockSpec((1, heads, LAT), request),
        ),
        input_output_aliases={7: 0},
        compiler_params=pltpu.CompilerParams(vmem_limit_bytes=6 * MIB),
        cost_estimate=pl.CostEstimate(
            flops=2 * heads * slots * (width + LAT),
            bytes_accessed=2 * (heads * (width + LAT) + slots * width),
            transcendentals=heads * slots,
        ),
        name="attend_rest",
    )(
        ranks,
        lengths,
        swap_slot,
        swap_mask,
        in_hbm(queries),
        in_hbm(pages),
        page,
        attended,
    )


def experts_kernel(
    top,
    fetch,
    ranks_ref,
    pieces,
    gate_ref,
    up_ref,
    source_ref,
    given,
    kept_ref,
    *refs,
):
    if fetch:
        down_ref, *refs = refs
    else:
        down_ref = source_ref
    rows_ref, meta_ref, inner_ref, table_ref, sems, down_sem = refs
    experts, _, units = gate_ref.shape
    total_rows = rows_ref.shape[0]
    quarter = kept_ref.shape[1]
    ep_rank, tp_rank = ranks_ref[0], ranks_ref[1]

    def columns_of(part):
        return pl.ds(pl.multiple_of((tp_rank ^ part) * quarter, 128), quarter)

    copies = []
    for start, parts, has_meta, piece in pieces:
        rows = pl.ds(start, piece.shape[0])
        if parts is None:
            copies.append((piece, rows_ref.at[rows, :]))
            continue
        for i, part in enumerate(parts):
            copies.append(
                (piece.at[:, pl.ds(i * quarter, quarter)], rows_ref.at[rows, columns_of(part)])
            )
        if has_meta:
            copies.append((piece.at[:, pl.ds(piece.shape[1] - 128, 128)], meta_ref.at[rows, :]))
    copies = [
        pltpu.make_async_copy(source, target, sems.at[i])
        for i, (source, target) in enumerate(copies)
    ]
    for one in copies:
        one.start()
    if fetch:
        down_copy = pltpu.make_async_copy(source_ref, down_ref, down_sem)
        down_copy.start()
    for one in copies:
        one.wait()
    meta = meta_ref[...].astype(jnp.float32)
    gates = sum(pltpu.roll(meta, 128 - i * top, 1) for i in range(1, 4))
    lane = lax.broadcasted_iota(jnp.int32, meta.shape, 1)
    for e in range(experts):
        name = (ep_rank * experts + e).astype(jnp.float32)
        mine = jnp.where((lane < top) & (meta == name), gates, 0.0)
        table_ref[:, e : e + 1] = jnp.sum(mine, axis=1, keepdims=True)
    stride = math.gcd(total_rows, ROWS)
    for e in range(experts):

        @pl.loop(0, total_rows // stride)
        def _(step):
            at = pl.ds(pl.multiple_of(step * stride, stride), stride)
            rows = rows_ref[at, :]
            gate = jnp.dot(rows, gate_ref[e], preferred_element_type=jnp.float32)
            up = jnp.dot(rows, up_ref[e], preferred_element_type=jnp.float32)
            act = gate / (1.0 + jnp.exp(-gate)) * up * table_ref[at, e : e + 1]
            inner_ref[at, e * units : (e + 1) * units] = act.astype(jnp.bfloat16)

    if fetch:
        down_copy.wait()
    last = len(given) - 1
    for part, out_ref, half in (
        (3, given[0], 0),
        (1, given[last], 1 - last),
        (2, kept_ref, 0),
        (0, kept_ref, 1),
    ):

        @pl.loop(0, total_rows // stride)
        def _(step):
            at = pl.ds(pl.multiple_of(step * stride, stride), stride)
            to = pl.ds(pl.multiple_of(half * total_rows + step * stride, stride), stride)
            weight = down_ref[:, :, columns_of(part)].reshape(experts * units, quarter)
            out_ref[to, :] = jnp.dot(
                inner_ref[at, :], weight, preferred_element_type=jnp.float32
            ).astype(jnp.bfloat16)


def run_experts(ranks, pieces, w_gate, w_up, w_down, rows, columns, top, fetch, given):
    experts, width, units = w_gate.shape
    arrays = [piece for *_, piece in pieces]
    count = sum(1 if parts is None else len(parts) + has_meta for _, parts, has_meta, _ in pieces)

    def kernel(ranks_ref, refs, *others):
        named = [(*about[:3], ref) for about, ref in zip(pieces, refs)]
        experts_kernel(top, fetch, ranks_ref, named, *others)

    need = 2 * rows * (width + 128 + experts * units) + 512 * rows
    down_shape = [pltpu.VMEM(w_down.shape, w_down.dtype)] if fetch else []
    return pl.pallas_call(
        kernel,
        out_shape=[
            [pltpu.VMEM((2 * rows // given, columns), jnp.bfloat16)] * given,
            pltpu.VMEM((2 * rows, columns), jnp.bfloat16),
        ]
        + down_shape,
        in_specs=[
            IN_SMEM,
            [ANYWHERE] * len(arrays),
            IN_VMEM,
            IN_VMEM,
            ANYWHERE if fetch else IN_VMEM,
        ],
        out_specs=[[IN_VMEM] * given, IN_VMEM] + [IN_VMEM] * len(down_shape),
        scratch_shapes=[
            pltpu.VMEM((rows, width), jnp.bfloat16),
            pltpu.VMEM((rows, 128), jnp.bfloat16),
            pltpu.VMEM((rows, experts * units), jnp.bfloat16),
            pltpu.VMEM((rows, 128), jnp.float32),
            pltpu.SemaphoreType.DMA((count,)),
            pltpu.SemaphoreType.DMA,
        ],
        compiler_params=pltpu.CompilerParams(vmem_limit_bytes=need + 6 * MIB),
        cost_estimate=pl.CostEstimate(
            flops=0,
            bytes_accessed=0,
            transcendentals=0,
        ),
        name="experts",
    )(
        ranks,
        arrays,
        in_vmem(w_gate),
        in_vmem(w_up),
        in_hbm(w_down) if fetch else in_vmem(w_down),
    )


def total_of(*terms):
    value = terms[0].astype(jnp.float32)
    for term in terms[1:]:
        value = value + term.astype(jnp.float32)
    return value.astype(jnp.bfloat16)


def local(
    cache_pages,
    queries,
    lengths,
    swap_slot,
    swap_mask,
    hidden,
    expert_ids,
    gate_weights,
    w_gate,
    w_up,
    w_down,
):
    groups = lax.axis_size("tp")
    ep_size = lax.axis_size("ep")
    ranks = jnp.stack([lax.axis_index("ep"), lax.axis_index("tp")]).astype(jnp.int32)
    mask_value = swap_mask[0]
    columns = hidden.shape[1] // groups
    top = expert_ids.shape[1]
    cache_pages = jnp.swapaxes(cache_pages, 1, 2)
    queries = jnp.swapaxes(queries, 1, 2)

    rows = hidden.shape[0]
    pairs = ep_size // 2
    late = list(range(2, pairs))
    half = len(late) // 2
    rest = len(late) - half
    levels = ep_size.bit_length() - 1
    tie = lax.optimization_barrier

    def cut(array, start, count):
        return lax.slice_in_dim(array, start * rows, (start + count) * rows, axis=0)

    def bare(array):
        return array[:, :columns]

    def page_take(page, swapped, level):
        bit = jnp.bitwise_and(jnp.right_shift(mask_value, level), 1) == 1
        return jnp.where(bit, swapped, page)

    def page_hop(page, level):
        return page_take(page, flip(page, "ep", 1 << level), level)

    def page_far(page):
        for level in range(levels - 1, 2, -1):
            page = page_hop(page, level)
        return flip(page, "ep", 4) if levels > 2 else page, page

    own, both, page = pick(
        ranks, swap_slot, expert_ids, gate_weights, hidden, cache_pages, groups
    )
    late_pieces = [flip(own, "ep", 2 * m) for m in late]
    near_2 = flip(own, "ep", 2)
    both_1 = flip(both, "ep", 1)

    near_2, w_gate, w_up = tie((near_2, w_gate, w_up))
    far_2 = flip(bare(near_2), "tp", 2)
    near_3 = flip(near_2, "ep", 1)
    w_gate, w_up = load(w_gate, w_up)
    far_2, near_3, w_gate, w_up, page, *late_pieces = tie(
        (far_2, near_3, w_gate, w_up, page, *late_pieces)
    )
    near_late = jnp.concatenate(late_pieces, axis=0)
    far_3 = flip(jnp.concatenate([bare(near_3), bare(near_late)], axis=0), "tp", 2)
    near_odds = flip(near_late, "ep", 1)
    near_23 = flip(jnp.concatenate([near_2, near_3], axis=0), "tp", 1)
    early = [flip(array, "tp", 1) for array in (both_1, far_2)]
    queries, near_23, early = tie((queries, near_23, early))
    count = queries.shape[0]
    some = count // 4
    attended = attend_part(ranks, lengths, queries, cache_pages, groups, 0, some)
    least = page.shape[0] // 4
    upper, lower = jnp.split(page, [least], axis=0)
    swapped, upper = page_far(upper)
    far_3, near_late, near_odds, attended, swapped = tie(
        (far_3, near_late, near_odds, attended, swapped)
    )
    upper = page_take(upper, swapped, 2) if levels > 2 else upper
    page = jnp.concatenate([upper, lower], axis=0)
    core_3 = flip(far_3, "tp", 1)
    far_late, core_late = cut(far_3, 1, len(late)), cut(core_3, 1, len(late))
    far_3, core_3 = cut(far_3, 0, 1), cut(core_3, 0, 1)
    far_odds = flip(bare(near_odds), "tp", 2)

    def piece(start, part, array):
        return start * rows, (part,), part == 0, array

    pieces = [(0, None, False, hidden), (0, (), True, own)]
    pieces += [(rows, (0, 2), True, both_1), (rows, (1, 3), False, early[0])]
    pieces += [piece(2, 0, near_2), piece(3, 0, near_3), (2 * rows, (1,), False, near_23)]
    pieces += [piece(2, 2, far_2), piece(2, 3, early[1])]
    pieces += [piece(3, 2, far_3), piece(3, 3, core_3)]
    *first, w_down = run_experts(
        ranks, pieces, w_gate, w_up, w_down, 4 * rows, columns, top, True, 1
    )
    near_both = jnp.concatenate([near_late, near_odds], axis=0)
    early = flip(near_both, "tp", 1)
    swapped = flip(page, "ep", 1)
    first, far_odds, early, swapped = tie((first, far_odds, early, swapped))
    page = page_take(page, swapped, 0)

    (given,), own = first
    sent, kept = jnp.split(total_of(own, flip(given, "tp", 1)), 2, axis=0)
    last = flip(far_odds, "tp", 1)
    over_23 = flip(cut(sent, 2, 2), "tp", 2)
    over_1 = flip(jnp.concatenate([cut(kept, 1, 1), cut(sent, 1, 1)], axis=1), "ep", 1)
    swapped = flip(page, "ep", 2)
    odds = len(late)
    pieces = [piece(0, 0, near_both), (0, (1,), False, early)]
    pieces += [piece(0, 2, far_late), piece(0, 3, core_late)]
    pieces += [piece(odds, 2, far_odds), piece(odds, 3, last)]
    second = [
        *run_experts(
            ranks, pieces, w_gate, w_up, w_down, 2 * len(late) * rows, columns, top, False, 2
        )
    ]
    second, over_23, over_1, swapped = tie((second, over_23, over_1, swapped))
    page = page_take(page, swapped, 1)
    upper, lower = jnp.split(page, [least], axis=0)
    swapped, lower = page_far(lower)
    (cross, side), own = second
    late_sent, late_kept = jnp.split(own, 2, axis=0)
    late_sent = total_of(late_sent, flip(cross, "tp", 1))
    over_3 = flip(total_of(cut(kept, 3, 1), cut(over_23, 1, 1)), "ep", 1)
    zero = flip(total_of(cut(sent, 0, 1), over_1[:, columns:]), "tp", 2)
    late_sent, side, queries = tie((late_sent, side, queries))
    side = flip(side, "tp", 1)

    over_y = flip(cut(late_sent, len(late), half), "tp", 2)
    over_x = flip(cut(late_sent, len(late) + half, rest), "ep", 1)
    over_y, over_x, over_3, side, queries = tie((over_y, over_x, over_3, side, queries))
    late_kept = total_of(late_kept, side)
    odd = total_of(
        cut(late_kept, len(late), len(late)), jnp.pad(over_y, ((0, rest * rows), (0, 0)))
    )
    odd = flip(odd, "ep", 1)
    even = total_of(cut(late_sent, 0, len(late)), jnp.pad(over_x, ((half * rows, 0), (0, 0))))
    even = flip(even, "tp", 2)
    attended = attend_part(
        ranks, lengths, queries, cache_pages, groups, some, 2 * some, attended
    )
    odd, even, attended, swapped = tie((odd, even, attended, swapped))
    lower = page_take(lower, swapped, 2) if levels > 2 else lower
    page = jnp.concatenate([upper, lower], axis=0)
    even = total_of(cut(late_kept, 0, len(late)), even, odd)
    back = [flip(cut(even, i, 1), "ep", 2 * m) for i, m in enumerate(late)]
    back.append(flip(total_of(cut(kept, 2, 1), cut(over_23, 0, 1), over_3), "ep", 2))
    attended = attend_rest(
        ranks,
        lengths,
        swap_slot,
        swap_mask,
        queries,
        cache_pages,
        page,
        attended,
        groups,
        3 * some,
    )
    *back, attended = tie((*back, attended))
    moe_out = total_of(cut(kept, 0, 1), over_1[:, :columns], zero, *back)
    return attended, moe_out


def solution(mesh):
    in_specs = (
        P(("ep", "tp"), None, None),
        P(("ep", "tp"), None, None),
        P(),
        P(),
        P(),
        P("ep", None),
        P("ep", None),
        P("ep", None),
        P("ep", None, "tp"),
        P("ep", None, "tp"),
        P("ep", "tp", None),
    )
    out_specs = (P(("ep", "tp"), None, None), P("ep", "tp"))
    return jax.shard_map(local, mesh=mesh, in_specs=in_specs, out_specs=out_specs, check_vma=False)
```

```python
import functools
import math

import jax
import jax.numpy as jnp
from jax import lax
from jax.experimental import pallas as pl
from jax.experimental.pallas import tpu as pltpu
from jax.sharding import PartitionSpec as P

LAT = 512
SCORE_SCALE = 192.0 ** (-0.5)
MASK_FLOOR = -1e30
ROWS = 512
MIB = 1 << 20


def flip(block, axis, apart):
    count = lax.axis_size(axis)
    return lax.ppermute(block, axis, [(i, i ^ apart) for i in range(count)])


def attend_body(query, page, length):
    scores = (
        lax.dot_general(query, page, (((0,), (0,)), ((), ())), preferred_element_type=jnp.float32)
        * SCORE_SCALE
    )
    live = lax.broadcasted_iota(jnp.int32, scores.shape, 1) < length
    scores = jnp.where(live, scores, MASK_FLOOR)
    top = jnp.max(scores, axis=1, keepdims=True)
    weight = jnp.where(live, jnp.exp(scores - top), 0.0)
    total = jnp.sum(weight, axis=1, keepdims=True)
    blended = lax.dot_general(
        weight.astype(jnp.bfloat16),
        page[:LAT],
        (((1,), (1,)), ((), ())),
        preferred_element_type=jnp.float32,
    )
    return (blended / total).astype(jnp.bfloat16)


def in_hbm(array):
    return pltpu.with_memory_space_constraint(array, pltpu.HBM)


def in_vmem(array):
    return pltpu.with_memory_space_constraint(array, pltpu.VMEM)


ANYWHERE = pl.BlockSpec(memory_space=pl.ANY)
IN_VMEM = pl.BlockSpec(memory_space=pltpu.VMEM)
IN_SMEM = pl.BlockSpec(memory_space=pltpu.SMEM)


def device_of(ranks_ref, groups, mask=0):
    return (ranks_ref[0] ^ mask) * groups + ranks_ref[1]


def pick_kernel(groups, ranks_ref, slots_ref, ids_ref, gates_ref, hidden_ref, pages_ref, near_ref, both_ref, page_ref, sems):
    rows = hidden_ref.shape[0]
    columns = hidden_ref.shape[1] // groups

    def quarter(part):
        start = pl.multiple_of((ranks_ref[1] ^ part) * columns, 128)
        return hidden_ref.at[:, pl.ds(start, columns)]

    copies = [
        (quarter(0), near_ref.at[:, pl.ds(0, columns)]),
        (quarter(0), both_ref.at[:, pl.ds(0, columns)]),
        (quarter(2), both_ref.at[:, pl.ds(columns, columns)]),
        (pages_ref.at[slots_ref[device_of(ranks_ref, groups)]], page_ref),
    ]
    copies = [pltpu.make_async_copy(*pair, sems.at[i]) for i, pair in enumerate(copies)]
    for one in copies:
        one.start()
    gates = gates_ref[...]
    high = gates.astype(jnp.bfloat16).astype(jnp.float32)
    middle = (gates - high).astype(jnp.bfloat16).astype(jnp.float32)
    low = gates - high - middle
    top = gates.shape[0]
    table = jnp.concatenate(
        [ids_ref[...].astype(jnp.float32), high, middle, low, jnp.zeros((128 - 4 * top, rows), jnp.float32)],
        axis=0,
    )
    table = jnp.concatenate([table, jnp.zeros((128, 128 - rows), jnp.float32)], axis=1)
    table = table.T[:rows].astype(jnp.bfloat16)
    near_ref[:, columns:] = table
    both_ref[:, 2 * columns :] = table
    for one in copies:
        one.wait()


def pick(ranks, swap_slot, expert_ids, gate_weights, hidden, pages, groups):
    rows, width = hidden.shape
    columns = width // groups
    return pl.pallas_call(
        functools.partial(pick_kernel, groups),
        out_shape=(
            pltpu.VMEM((rows, columns + 128), jnp.bfloat16),
            pltpu.VMEM((rows, 2 * columns + 128), jnp.bfloat16),
            pltpu.VMEM(pages.shape[1:], jnp.bfloat16),
        ),
        in_specs=[IN_SMEM, IN_SMEM, IN_VMEM, IN_VMEM, ANYWHERE, ANYWHERE],
        out_specs=(IN_VMEM, IN_VMEM, IN_VMEM),
        scratch_shapes=[pltpu.SemaphoreType.DMA((4,))],
        compiler_params=pltpu.CompilerParams(vmem_limit_bytes=2 * MIB),
        name="pick",
    )(
        ranks,
        in_hbm(swap_slot),
        in_hbm(expert_ids.T),
        in_hbm(gate_weights.T),
        in_hbm(hidden),
        in_hbm(pages),
    )


def attend_part(ranks, lengths, queries, pages, groups, first, some, before=None):
    count, width, heads = queries.shape
    slots = pages.shape[2]
    each = math.gcd(some, 2)
    skip = first // each

    def kernel(ranks_ref, lengths_ref, query_ref, page_ref, *refs):
        start = device_of(ranks_ref, groups) * count + first + pl.program_id(0) * each
        for i in range(each):
            refs[-1][i] = attend_body(query_ref[i], page_ref[i], lengths_ref[start + i])

    earlier = [] if before is None else [before]
    return pl.pallas_call(
        kernel,
        out_shape=jax.ShapeDtypeStruct((count, heads, LAT), jnp.bfloat16),
        grid_spec=pltpu.PrefetchScalarGridSpec(
            num_scalar_prefetch=2,
            grid=(some // each,),
            in_specs=[
                pl.BlockSpec((each, width, heads), lambda i, *_: (skip + i, 0, 0)),
                pl.BlockSpec((each, width, slots), lambda i, *_: (skip + i, 0, 0)),
            ]
            + [ANYWHERE] * len(earlier),
            out_specs=pl.BlockSpec((each, heads, LAT), lambda i, *_: (skip + i, 0, 0)),
        ),
        input_output_aliases={4: 0} if earlier else {},
        compiler_params=pltpu.CompilerParams(vmem_limit_bytes=8 * MIB),
        cost_estimate=pl.CostEstimate(flops=0, bytes_accessed=0, transcendentals=0),
        name="attend_local",
    )(ranks, lengths, in_hbm(queries), in_hbm(pages), *earlier)


def load_kernel(*refs):
    count = len(refs) // 2
    copies = [
        pltpu.make_async_copy(refs[i], refs[count + i], refs[-1].at[i]) for i in range(count)
    ]
    for one in copies:
        one.start()
    for one in copies:
        one.wait()


def load(*arrays):
    return pl.pallas_call(
        load_kernel,
        out_shape=[pltpu.VMEM(w.shape, w.dtype) for w in arrays],
        in_specs=[ANYWHERE] * len(arrays),
        out_specs=[ANYWHERE] * len(arrays),
        scratch_shapes=[pltpu.SemaphoreType.DMA((len(arrays),))],
        compiler_params=pltpu.CompilerParams(vmem_limit_bytes=MIB),
        cost_estimate=pl.CostEstimate(
            flops=0, bytes_accessed=sum(2 * math.prod(w.shape) for w in arrays), transcendentals=0
        ),
        name="load",
    )(*[in_hbm(w) for w in arrays])


def attend_rest(
    ranks, lengths, swap_slot, swap_mask, queries, pages, page, attended, groups, first
):
    count, width, heads = queries.shape
    slots = pages.shape[2]
    each = 2
    steps = (count - first) // each
    skip = first // each

    def kernel(
        ranks_ref,
        lengths_ref,
        slots_ref,
        mask_ref,
        query_ref,
        pages_ref,
        page_ref,
        old_ref,
        out_ref,
    ):
        step = pl.program_id(0)
        device = device_of(ranks_ref, groups)
        partner = device_of(ranks_ref, groups, mask_ref[0])
        mine = slots_ref[device]
        far_length = lengths_ref[partner * count + slots_ref[partner]]
        block = jnp.where(step < steps, skip + step, mine // each)
        for i in range(each):
            at = block * each + i
            traded = (step == steps) & (at == mine)

            @pl.when(jnp.logical_not(traded))
            def _():
                out_ref[i] = attend_body(
                    query_ref[i], pages_ref[i], lengths_ref[device * count + at]
                )

            @pl.when(traded)
            def _():
                out_ref[i] = attend_body(query_ref[i], page_ref[...], far_length)

    def request(i, ranks_ref, lengths_ref, slots_ref, mask_ref):
        mine = slots_ref[device_of(ranks_ref, groups)]
        return jnp.where(i < steps, skip + i, mine // each), 0, 0

    return pl.pallas_call(
        kernel,
        out_shape=jax.ShapeDtypeStruct(attended.shape, attended.dtype),
        grid_spec=pltpu.PrefetchScalarGridSpec(
            num_scalar_prefetch=4,
            grid=(steps + 1,),
            in_specs=[
                pl.BlockSpec((each, width, heads), request),
                pl.BlockSpec((each, width, slots), request),
                pl.BlockSpec((width, slots), lambda i, *_: (0, 0)),
                ANYWHERE,
            ],
            out_specs=pl.BlockSpec((each, heads, LAT), request),
        ),
        input_output_aliases={7: 0},
        compiler_params=pltpu.CompilerParams(vmem_limit_bytes=8 * MIB),
        cost_estimate=pl.CostEstimate(
            flops=2 * heads * slots * (width + LAT),
            bytes_accessed=2 * (heads * (width + LAT) + slots * width),
            transcendentals=heads * slots,
        ),
        name="attend_rest",
    )(
        ranks,
        lengths,
        swap_slot,
        swap_mask,
        in_hbm(queries),
        in_hbm(pages),
        page,
        attended,
    )


def experts_kernel(
    top,
    fetch,
    ranks_ref,
    pieces,
    gate_ref,
    up_ref,
    source_ref,
    given,
    kept_ref,
    *refs,
):
    if fetch:
        down_ref, *refs = refs
    else:
        down_ref = source_ref
    rows_ref, meta_ref, inner_ref, table_ref, sems, down_sem = refs
    experts, _, units = gate_ref.shape
    total_rows = rows_ref.shape[0]
    quarter = kept_ref.shape[1]
    ep_rank, tp_rank = ranks_ref[0], ranks_ref[1]

    def columns_of(part):
        return pl.ds(pl.multiple_of((tp_rank ^ part) * quarter, 128), quarter)

    copies = []
    for start, parts, has_meta, piece in pieces:
        rows = pl.ds(start, piece.shape[0])
        if parts is None:
            copies.append((piece, rows_ref.at[rows, :]))
            continue
        for i, part in enumerate(parts):
            copies.append(
                (piece.at[:, pl.ds(i * quarter, quarter)], rows_ref.at[rows, columns_of(part)])
            )
        if has_meta:
            copies.append((piece.at[:, pl.ds(piece.shape[1] - 128, 128)], meta_ref.at[rows, :]))
    copies = [
        pltpu.make_async_copy(source, target, sems.at[i])
        for i, (source, target) in enumerate(copies)
    ]
    for one in copies:
        one.start()
    if fetch:
        down_copy = pltpu.make_async_copy(source_ref, down_ref, down_sem)
        down_copy.start()
    for one in copies:
        one.wait()
    meta = meta_ref[...].astype(jnp.float32)
    gates = sum(pltpu.roll(meta, 128 - i * top, 1) for i in range(1, 4))
    lane = lax.broadcasted_iota(jnp.int32, meta.shape, 1)
    for e in range(experts):
        name = (ep_rank * experts + e).astype(jnp.float32)
        mine = jnp.where((lane < top) & (meta == name), gates, 0.0)
        table_ref[:, e : e + 1] = jnp.sum(mine, axis=1, keepdims=True)
    stride = math.gcd(total_rows, ROWS)
    for e in range(experts):

        @pl.loop(0, total_rows // stride)
        def _(step):
            at = pl.ds(pl.multiple_of(step * stride, stride), stride)
            rows = rows_ref[at, :]
            gate = jnp.dot(rows, gate_ref[e], preferred_element_type=jnp.float32)
            up = jnp.dot(rows, up_ref[e], preferred_element_type=jnp.float32)
            act = gate / (1.0 + jnp.exp(-gate)) * up * table_ref[at, e : e + 1]
            inner_ref[at, e * units : (e + 1) * units] = act.astype(jnp.bfloat16)

    if fetch:
        down_copy.wait()
    last = len(given) - 1
    for part, out_ref, half in (
        (3, given[0], 0),
        (1, given[last], 1 - last),
        (2, kept_ref, 0),
        (0, kept_ref, 1),
    ):

        @pl.loop(0, total_rows // stride)
        def _(step):
            at = pl.ds(pl.multiple_of(step * stride, stride), stride)
            to = pl.ds(pl.multiple_of(half * total_rows + step * stride, stride), stride)
            weight = down_ref[:, :, columns_of(part)].reshape(experts * units, quarter)
            out_ref[to, :] = jnp.dot(
                inner_ref[at, :], weight, preferred_element_type=jnp.float32
            ).astype(jnp.bfloat16)


def run_experts(ranks, pieces, w_gate, w_up, w_down, rows, columns, top, fetch, given):
    experts, width, units = w_gate.shape
    arrays = [piece for *_, piece in pieces]
    count = sum(1 if parts is None else len(parts) + has_meta for _, parts, has_meta, _ in pieces)

    def kernel(ranks_ref, refs, *others):
        named = [(*about[:3], ref) for about, ref in zip(pieces, refs)]
        experts_kernel(top, fetch, ranks_ref, named, *others)

    need = 2 * rows * (width + 128 + experts * units) + 512 * rows
    down_shape = [pltpu.VMEM(w_down.shape, w_down.dtype)] if fetch else []
    return pl.pallas_call(
        kernel,
        out_shape=[
            [pltpu.VMEM((2 * rows // given, columns), jnp.bfloat16)] * given,
            pltpu.VMEM((2 * rows, columns), jnp.bfloat16),
        ]
        + down_shape,
        in_specs=[
            IN_SMEM,
            [ANYWHERE] * len(arrays),
            IN_VMEM,
            IN_VMEM,
            ANYWHERE if fetch else IN_VMEM,
        ],
        out_specs=[[IN_VMEM] * given, IN_VMEM] + [IN_VMEM] * len(down_shape),
        scratch_shapes=[
            pltpu.VMEM((rows, width), jnp.bfloat16),
            pltpu.VMEM((rows, 128), jnp.bfloat16),
            pltpu.VMEM((rows, experts * units), jnp.bfloat16),
            pltpu.VMEM((rows, 128), jnp.float32),
            pltpu.SemaphoreType.DMA((count,)),
            pltpu.SemaphoreType.DMA,
        ],
        compiler_params=pltpu.CompilerParams(vmem_limit_bytes=need + 6 * MIB),
        cost_estimate=pl.CostEstimate(
            flops=0,
            bytes_accessed=0,
            transcendentals=0,
        ),
        name="experts",
    )(
        ranks,
        arrays,
        in_vmem(w_gate),
        in_vmem(w_up),
        in_hbm(w_down) if fetch else in_vmem(w_down),
    )


def total_of(*terms):
    value = terms[0].astype(jnp.float32)
    for term in terms[1:]:
        value = value + term.astype(jnp.float32)
    return value.astype(jnp.bfloat16)


def local(
    cache_pages,
    queries,
    lengths,
    swap_slot,
    swap_mask,
    hidden,
    expert_ids,
    gate_weights,
    w_gate,
    w_up,
    w_down,
):
    groups = lax.axis_size("tp")
    ep_size = lax.axis_size("ep")
    ranks = jnp.stack([lax.axis_index("ep"), lax.axis_index("tp")]).astype(jnp.int32)
    mask_value = swap_mask[0]
    columns = hidden.shape[1] // groups
    top = expert_ids.shape[1]
    cache_pages = jnp.swapaxes(cache_pages, 1, 2)
    queries = jnp.swapaxes(queries, 1, 2)

    rows = hidden.shape[0]
    pairs = ep_size // 2
    late = list(range(2, pairs))
    half = len(late) // 2
    rest = len(late) - half
    levels = ep_size.bit_length() - 1
    tie = lax.optimization_barrier

    def cut(array, start, count):
        return lax.slice_in_dim(array, start * rows, (start + count) * rows, axis=0)

    def bare(array):
        return array[:, :columns]

    def page_take(page, swapped, level):
        bit = jnp.bitwise_and(jnp.right_shift(mask_value, level), 1) == 1
        return jnp.where(bit, swapped, page)

    def page_hop(page, level):
        return page_take(page, flip(page, "ep", 1 << level), level)

    def page_far(page):
        for level in range(levels - 1, 2, -1):
            page = page_hop(page, level)
        return flip(page, "ep", 4) if levels > 2 else page, page

    own, both, page = pick(
        ranks, swap_slot, expert_ids, gate_weights, hidden, cache_pages, groups
    )
    late_pieces = [flip(own, "ep", 2 * m) for m in late]
    near_2 = flip(own, "ep", 2)
    both_1 = flip(both, "ep", 1)

    near_2, w_gate, w_up = tie((near_2, w_gate, w_up))
    far_2 = flip(bare(near_2), "tp", 2)
    near_3 = flip(near_2, "ep", 1)
    w_gate, w_up = load(w_gate, w_up)
    far_2, near_3, w_gate, w_up, page, *late_pieces = tie(
        (far_2, near_3, w_gate, w_up, page, *late_pieces)
    )
    near_late = jnp.concatenate(late_pieces, axis=0)
    far_3 = flip(jnp.concatenate([bare(near_3), bare(near_late)], axis=0), "tp", 2)
    near_odds = flip(near_late, "ep", 1)
    wide = jnp.pad(far_2, ((0, 0), (0, near_2.shape[1] - columns)))
    core_23 = flip(jnp.concatenate([near_2, near_3, wide], axis=0), "tp", 1)
    core_1 = flip(both_1, "tp", 1)
    queries, core_1, core_23 = tie((queries, core_1, core_23))
    count = queries.shape[0]
    some, middle = count // 4, count * 5 // 8
    attended = attend_part(ranks, lengths, queries, cache_pages, groups, 0, some)
    least = page.shape[0] // 4
    upper, lower = jnp.split(page, [least], axis=0)
    swapped, upper = page_far(upper)
    far_3, near_late, near_odds, attended, swapped = tie(
        (far_3, near_late, near_odds, attended, swapped)
    )
    upper = page_take(upper, swapped, 2) if levels > 2 else upper
    page = jnp.concatenate([upper, lower], axis=0)
    core_3 = flip(far_3, "tp", 1)
    far_late, core_late = cut(far_3, 1, len(late)), cut(core_3, 1, len(late))
    far_3, core_3 = cut(far_3, 0, 1), cut(core_3, 0, 1)
    far_odds = flip(bare(near_odds), "tp", 2)

    def piece(start, part, array):
        return start * rows, (part,), part == 0, array

    pieces = [(0, None, False, hidden), (0, (), True, own)]
    pieces += [(rows, (0, 2), True, both_1), (rows, (1, 3), False, core_1)]
    pieces += [piece(2, 0, near_2), piece(3, 0, near_3), piece(2, 1, cut(core_23, 0, 2))]
    pieces += [piece(2, 2, far_2), piece(2, 3, bare(cut(core_23, 2, 1)))]
    pieces += [piece(3, 2, far_3), piece(3, 3, core_3)]
    *first, w_down = run_experts(
        ranks, pieces, w_gate, w_up, w_down, 4 * rows, columns, top, True, 1
    )
    near_both = jnp.concatenate([near_late, near_odds], axis=0)
    early = flip(near_both, "tp", 1)
    swapped = flip(page, "ep", 1)
    first, far_odds, early, swapped = tie((first, far_odds, early, swapped))
    page = page_take(page, swapped, 0)

    (given,), own = first
    sent, kept = jnp.split(total_of(own, flip(given, "tp", 1)), 2, axis=0)
    last = flip(far_odds, "tp", 1)
    over_23 = flip(cut(sent, 2, 2), "tp", 2)
    over_1 = flip(jnp.concatenate([cut(kept, 1, 1), cut(sent, 1, 1)], axis=1), "ep", 1)
    swapped = flip(page, "ep", 2)
    odds = len(late)
    pieces = [piece(0, 0, near_both), (0, (1,), False, early)]
    pieces += [piece(0, 2, far_late), piece(0, 3, core_late)]
    pieces += [piece(odds, 2, far_odds), piece(odds, 3, last)]
    second = [
        *run_experts(
            ranks, pieces, w_gate, w_up, w_down, 2 * len(late) * rows, columns, top, False, 2
        )
    ]
    second, over_23, over_1, swapped = tie((second, over_23, over_1, swapped))
    page = page_take(page, swapped, 1)
    upper, lower = jnp.split(page, [least], axis=0)
    swapped, lower = page_far(lower)
    (cross, side), own = second
    late_sent, late_kept = jnp.split(own, 2, axis=0)
    late_sent = total_of(late_sent, flip(cross, "tp", 1))
    over_3 = flip(total_of(cut(kept, 3, 1), cut(over_23, 1, 1)), "ep", 1)
    zero = flip(total_of(cut(sent, 0, 1), over_1[:, columns:]), "tp", 2)
    late_sent, side, queries = tie((late_sent, side, queries))
    side = flip(side, "tp", 1)

    over_y = flip(cut(late_sent, len(late), half), "tp", 2)
    over_x = flip(cut(late_sent, len(late) + half, rest), "ep", 1)
    over_y, over_x, over_3, side, queries = tie((over_y, over_x, over_3, side, queries))
    late_kept = total_of(late_kept, side)
    odd = total_of(
        cut(late_kept, len(late), len(late)), jnp.pad(over_y, ((0, rest * rows), (0, 0)))
    )
    odd = flip(odd, "ep", 1)
    even = total_of(cut(late_sent, 0, len(late)), jnp.pad(over_x, ((half * rows, 0), (0, 0))))
    even = flip(even, "tp", 2)
    attended = attend_part(
        ranks, lengths, queries, cache_pages, groups, some, middle - some, attended
    )
    odd, even, attended, swapped = tie((odd, even, attended, swapped))
    lower = page_take(lower, swapped, 2) if levels > 2 else lower
    page = jnp.concatenate([upper, lower], axis=0)
    even = total_of(cut(late_kept, 0, len(late)), even, odd)
    back = [flip(cut(even, i, 1), "ep", 2 * m) for i, m in enumerate(late)]
    back.append(flip(total_of(cut(kept, 2, 1), cut(over_23, 0, 1), over_3), "ep", 2))
    attended = attend_rest(
        ranks,
        lengths,
        swap_slot,
        swap_mask,
        queries,
        cache_pages,
        page,
        attended,
        groups,
        middle,
    )
    *back, attended = tie((*back, attended))
    moe_out = total_of(cut(kept, 0, 1), over_1[:, :columns], zero, *back)
    return attended, moe_out


def solution(mesh):
    in_specs = (
        P(("ep", "tp"), None, None),
        P(("ep", "tp"), None, None),
        P(),
        P(),
        P(),
        P("ep", None),
        P("ep", None),
        P("ep", None),
        P("ep", None, "tp"),
        P("ep", None, "tp"),
        P("ep", "tp", None),
    )
    out_specs = (P(("ep", "tp"), None, None), P("ep", "tp"))
    return jax.shard_map(local, mesh=mesh, in_specs=in_specs, out_specs=out_specs, check_vma=False)
```

```python
import functools
import math

import jax
import jax.numpy as jnp
from jax import lax
from jax.experimental import pallas as pl
from jax.experimental.pallas import tpu as pltpu
from jax.sharding import PartitionSpec as P

LAT = 512
SCORE_SCALE = 192.0 ** (-0.5)
MASK_FLOOR = -1e30
ROWS = 512
MIB = 1 << 20


def flip(block, axis, apart):
    count = lax.axis_size(axis)
    return lax.ppermute(block, axis, [(i, i ^ apart) for i in range(count)])


def attend_body(query, page, length):
    scores = (
        lax.dot_general(query, page, (((0,), (0,)), ((), ())), preferred_element_type=jnp.float32)
        * SCORE_SCALE
    )
    live = lax.broadcasted_iota(jnp.int32, scores.shape, 1) < length
    scores = jnp.where(live, scores, MASK_FLOOR)
    top = jnp.max(scores, axis=1, keepdims=True)
    weight = jnp.where(live, jnp.exp(scores - top), 0.0)
    total = jnp.sum(weight, axis=1, keepdims=True)
    blended = lax.dot_general(
        weight.astype(jnp.bfloat16),
        page[:LAT],
        (((1,), (1,)), ((), ())),
        preferred_element_type=jnp.float32,
    )
    return (blended / total).astype(jnp.bfloat16)


def in_hbm(array):
    return pltpu.with_memory_space_constraint(array, pltpu.HBM)


def in_vmem(array):
    return pltpu.with_memory_space_constraint(array, pltpu.VMEM)


ANYWHERE = pl.BlockSpec(memory_space=pl.ANY)
IN_VMEM = pl.BlockSpec(memory_space=pltpu.VMEM)
IN_SMEM = pl.BlockSpec(memory_space=pltpu.SMEM)


def device_of(ranks_ref, groups, mask=0):
    return (ranks_ref[0] ^ mask) * groups + ranks_ref[1]


def pick_kernel(groups, ranks_ref, slots_ref, ids_ref, gates_ref, hidden_ref, pages_ref, near_ref, both_ref, page_ref, sems):
    rows = hidden_ref.shape[0]
    columns = hidden_ref.shape[1] // groups

    def quarter(part):
        start = pl.multiple_of((ranks_ref[1] ^ part) * columns, 128)
        return hidden_ref.at[:, pl.ds(start, columns)]

    copies = [
        (quarter(0), near_ref.at[:, pl.ds(0, columns)]),
        (quarter(0), both_ref.at[:, pl.ds(0, columns)]),
        (quarter(2), both_ref.at[:, pl.ds(columns, columns)]),
        (pages_ref.at[slots_ref[device_of(ranks_ref, groups)]], page_ref),
    ]
    copies = [pltpu.make_async_copy(*pair, sems.at[i]) for i, pair in enumerate(copies)]
    for one in copies:
        one.start()
    gates = gates_ref[...]
    high = gates.astype(jnp.bfloat16).astype(jnp.float32)
    middle = (gates - high).astype(jnp.bfloat16).astype(jnp.float32)
    low = gates - high - middle
    top = gates.shape[0]
    table = jnp.concatenate(
        [ids_ref[...].astype(jnp.float32), high, middle, low, jnp.zeros((128 - 4 * top, rows), jnp.float32)],
        axis=0,
    )
    table = jnp.concatenate([table, jnp.zeros((128, 128 - rows), jnp.float32)], axis=1)
    table = table.T[:rows].astype(jnp.bfloat16)
    near_ref[:, columns:] = table
    both_ref[:, 2 * columns :] = table
    for one in copies:
        one.wait()


def pick(ranks, swap_slot, expert_ids, gate_weights, hidden, pages, groups):
    rows, width = hidden.shape
    columns = width // groups
    return pl.pallas_call(
        functools.partial(pick_kernel, groups),
        out_shape=(
            pltpu.VMEM((rows, columns + 128), jnp.bfloat16),
            pltpu.VMEM((rows, 2 * columns + 128), jnp.bfloat16),
            pltpu.VMEM(pages.shape[1:], jnp.bfloat16),
        ),
        in_specs=[IN_SMEM, IN_SMEM, IN_VMEM, IN_VMEM, ANYWHERE, ANYWHERE],
        out_specs=(IN_VMEM, IN_VMEM, IN_VMEM),
        scratch_shapes=[pltpu.SemaphoreType.DMA((4,))],
        compiler_params=pltpu.CompilerParams(vmem_limit_bytes=2 * MIB),
        name="pick",
    )(
        ranks,
        in_hbm(swap_slot),
        in_hbm(expert_ids.T),
        in_hbm(gate_weights.T),
        in_hbm(hidden),
        in_hbm(pages),
    )


def attend_part(ranks, lengths, queries, pages, groups, first, some, before=None):
    count, width, heads = queries.shape
    slots = pages.shape[2]
    each = math.gcd(some, 2)
    skip = first // each

    def kernel(ranks_ref, lengths_ref, query_ref, page_ref, *refs):
        start = device_of(ranks_ref, groups) * count + first + pl.program_id(0) * each
        for i in range(each):
            refs[-1][i] = attend_body(query_ref[i], page_ref[i], lengths_ref[start + i])

    earlier = [] if before is None else [before]
    return pl.pallas_call(
        kernel,
        out_shape=jax.ShapeDtypeStruct((count, heads, LAT), jnp.bfloat16),
        grid_spec=pltpu.PrefetchScalarGridSpec(
            num_scalar_prefetch=2,
            grid=(some // each,),
            in_specs=[
                pl.BlockSpec((each, width, heads), lambda i, *_: (skip + i, 0, 0)),
                pl.BlockSpec((each, width, slots), lambda i, *_: (skip + i, 0, 0)),
            ]
            + [ANYWHERE] * len(earlier),
            out_specs=pl.BlockSpec((each, heads, LAT), lambda i, *_: (skip + i, 0, 0)),
        ),
        input_output_aliases={4: 0} if earlier else {},
        compiler_params=pltpu.CompilerParams(vmem_limit_bytes=8 * MIB),
        cost_estimate=pl.CostEstimate(flops=0, bytes_accessed=0, transcendentals=0),
        name="attend_local",
    )(ranks, lengths, in_hbm(queries), in_hbm(pages), *earlier)


def load_kernel(*refs):
    count = len(refs) // 2
    copies = [
        pltpu.make_async_copy(refs[i], refs[count + i], refs[-1].at[i]) for i in range(count)
    ]
    for one in copies:
        one.start()
    for one in copies:
        one.wait()


def load(*arrays):
    return pl.pallas_call(
        load_kernel,
        out_shape=[pltpu.VMEM(w.shape, w.dtype) for w in arrays],
        in_specs=[ANYWHERE] * len(arrays),
        out_specs=[ANYWHERE] * len(arrays),
        scratch_shapes=[pltpu.SemaphoreType.DMA((len(arrays),))],
        compiler_params=pltpu.CompilerParams(vmem_limit_bytes=MIB),
        cost_estimate=pl.CostEstimate(
            flops=0, bytes_accessed=sum(2 * math.prod(w.shape) for w in arrays), transcendentals=0
        ),
        name="load",
    )(*[in_hbm(w) for w in arrays])


def attend_rest(
    ranks, lengths, swap_slot, swap_mask, queries, pages, page, attended, groups, first
):
    count, width, heads = queries.shape
    slots = pages.shape[2]
    each = 2
    steps = (count - first) // each
    skip = first // each

    def kernel(
        ranks_ref,
        lengths_ref,
        slots_ref,
        mask_ref,
        query_ref,
        pages_ref,
        page_ref,
        old_ref,
        out_ref,
    ):
        step = pl.program_id(0)
        device = device_of(ranks_ref, groups)
        partner = device_of(ranks_ref, groups, mask_ref[0])
        mine = slots_ref[device]
        far_length = lengths_ref[partner * count + slots_ref[partner]]

        @pl.when(step < steps)
        def _():
            for i in range(each):
                at = device * count + first + step * each + i
                out_ref[i] = attend_body(query_ref[i], pages_ref[i], lengths_ref[at])

        @pl.when(step == steps)
        def _():
            for i in range(each):
                at = mine // each * each + i
                traded = at == mine
                page = jnp.where(traded, page_ref[...], pages_ref[i])
                length = jnp.where(traded, far_length, lengths_ref[device * count + at])
                out_ref[i] = attend_body(query_ref[i], page, length)

    def request(i, ranks_ref, lengths_ref, slots_ref, mask_ref):
        mine = slots_ref[device_of(ranks_ref, groups)]
        return jnp.where(i < steps, skip + i, mine // each), 0, 0

    return pl.pallas_call(
        kernel,
        out_shape=jax.ShapeDtypeStruct(attended.shape, attended.dtype),
        grid_spec=pltpu.PrefetchScalarGridSpec(
            num_scalar_prefetch=4,
            grid=(steps + 1,),
            in_specs=[
                pl.BlockSpec((each, width, heads), request),
                pl.BlockSpec((each, width, slots), request),
                pl.BlockSpec((width, slots), lambda i, *_: (0, 0)),
                ANYWHERE,
            ],
            out_specs=pl.BlockSpec((each, heads, LAT), request),
        ),
        input_output_aliases={7: 0},
        compiler_params=pltpu.CompilerParams(vmem_limit_bytes=8 * MIB),
        cost_estimate=pl.CostEstimate(
            flops=2 * heads * slots * (width + LAT),
            bytes_accessed=2 * (heads * (width + LAT) + slots * width),
            transcendentals=heads * slots,
        ),
        name="attend_rest",
    )(
        ranks,
        lengths,
        swap_slot,
        swap_mask,
        in_hbm(queries),
        in_hbm(pages),
        page,
        attended,
    )


def experts_kernel(
    top,
    fetch,
    ranks_ref,
    pieces,
    gate_ref,
    up_ref,
    source_ref,
    given,
    kept_ref,
    *refs,
):
    if fetch:
        down_ref, *refs = refs
    else:
        down_ref = source_ref
    rows_ref, meta_ref, inner_ref, table_ref, sems, down_sem = refs
    experts, _, units = gate_ref.shape
    total_rows = rows_ref.shape[0]
    quarter = kept_ref.shape[1]
    ep_rank, tp_rank = ranks_ref[0], ranks_ref[1]

    def columns_of(part):
        return pl.ds(pl.multiple_of((tp_rank ^ part) * quarter, 128), quarter)

    copies = []
    for start, parts, has_meta, piece in pieces:
        rows = pl.ds(start, piece.shape[0])
        if parts is None:
            copies.append((piece, rows_ref.at[rows, :]))
            continue
        for i, part in enumerate(parts):
            copies.append(
                (piece.at[:, pl.ds(i * quarter, quarter)], rows_ref.at[rows, columns_of(part)])
            )
        if has_meta:
            copies.append((piece.at[:, pl.ds(piece.shape[1] - 128, 128)], meta_ref.at[rows, :]))
    copies = [
        pltpu.make_async_copy(source, target, sems.at[i])
        for i, (source, target) in enumerate(copies)
    ]
    for one in copies:
        one.start()
    if fetch:
        down_copy = pltpu.make_async_copy(source_ref, down_ref, down_sem)
        down_copy.start()
    for one in copies:
        one.wait()
    meta = meta_ref[...].astype(jnp.float32)
    gates = sum(pltpu.roll(meta, 128 - i * top, 1) for i in range(1, 4))
    lane = lax.broadcasted_iota(jnp.int32, meta.shape, 1)
    for e in range(experts):
        name = (ep_rank * experts + e).astype(jnp.float32)
        mine = jnp.where((lane < top) & (meta == name), gates, 0.0)
        table_ref[:, e : e + 1] = jnp.sum(mine, axis=1, keepdims=True)
    stride = math.gcd(total_rows, ROWS)
    for e in range(experts):

        @pl.loop(0, total_rows // stride)
        def _(step):
            at = pl.ds(pl.multiple_of(step * stride, stride), stride)
            rows = rows_ref[at, :]
            gate = jnp.dot(rows, gate_ref[e], preferred_element_type=jnp.float32)
            up = jnp.dot(rows, up_ref[e], preferred_element_type=jnp.float32)
            act = gate / (1.0 + jnp.exp(-gate)) * up * table_ref[at, e : e + 1]
            inner_ref[at, e * units : (e + 1) * units] = act.astype(jnp.bfloat16)

    if fetch:
        down_copy.wait()
    last = len(given) - 1
    for part, out_ref, half in (
        (3, given[0], 0),
        (1, given[last], 1 - last),
        (2, kept_ref, 0),
        (0, kept_ref, 1),
    ):

        @pl.loop(0, total_rows // stride)
        def _(step):
            at = pl.ds(pl.multiple_of(step * stride, stride), stride)
            to = pl.ds(pl.multiple_of(half * total_rows + step * stride, stride), stride)
            weight = down_ref[:, :, columns_of(part)].reshape(experts * units, quarter)
            out_ref[to, :] = jnp.dot(
                inner_ref[at, :], weight, preferred_element_type=jnp.float32
            ).astype(jnp.bfloat16)


def run_experts(ranks, pieces, w_gate, w_up, w_down, rows, columns, top, fetch, given):
    experts, width, units = w_gate.shape
    arrays = [piece for *_, piece in pieces]
    count = sum(1 if parts is None else len(parts) + has_meta for _, parts, has_meta, _ in pieces)

    def kernel(ranks_ref, refs, *others):
        named = [(*about[:3], ref) for about, ref in zip(pieces, refs)]
        experts_kernel(top, fetch, ranks_ref, named, *others)

    need = 2 * rows * (width + 128 + experts * units) + 512 * rows
    down_shape = [pltpu.VMEM(w_down.shape, w_down.dtype)] if fetch else []
    return pl.pallas_call(
        kernel,
        out_shape=[
            [pltpu.VMEM((2 * rows // given, columns), jnp.bfloat16)] * given,
            pltpu.VMEM((2 * rows, columns), jnp.bfloat16),
        ]
        + down_shape,
        in_specs=[
            IN_SMEM,
            [ANYWHERE] * len(arrays),
            IN_VMEM,
            IN_VMEM,
            ANYWHERE if fetch else IN_VMEM,
        ],
        out_specs=[[IN_VMEM] * given, IN_VMEM] + [IN_VMEM] * len(down_shape),
        scratch_shapes=[
            pltpu.VMEM((rows, width), jnp.bfloat16),
            pltpu.VMEM((rows, 128), jnp.bfloat16),
            pltpu.VMEM((rows, experts * units), jnp.bfloat16),
            pltpu.VMEM((rows, 128), jnp.float32),
            pltpu.SemaphoreType.DMA((count,)),
            pltpu.SemaphoreType.DMA,
        ],
        compiler_params=pltpu.CompilerParams(vmem_limit_bytes=need + 6 * MIB),
        cost_estimate=pl.CostEstimate(
            flops=0,
            bytes_accessed=0,
            transcendentals=0,
        ),
        name="experts",
    )(
        ranks,
        arrays,
        in_vmem(w_gate),
        in_vmem(w_up),
        in_hbm(w_down) if fetch else in_vmem(w_down),
    )


def total_of(*terms):
    value = terms[0].astype(jnp.float32)
    for term in terms[1:]:
        value = value + term.astype(jnp.float32)
    return value.astype(jnp.bfloat16)


def local(
    cache_pages,
    queries,
    lengths,
    swap_slot,
    swap_mask,
    hidden,
    expert_ids,
    gate_weights,
    w_gate,
    w_up,
    w_down,
):
    groups = lax.axis_size("tp")
    ep_size = lax.axis_size("ep")
    ranks = jnp.stack([lax.axis_index("ep"), lax.axis_index("tp")]).astype(jnp.int32)
    mask_value = swap_mask[0]
    columns = hidden.shape[1] // groups
    top = expert_ids.shape[1]
    cache_pages = jnp.swapaxes(cache_pages, 1, 2)
    queries = jnp.swapaxes(queries, 1, 2)

    rows = hidden.shape[0]
    pairs = ep_size // 2
    late = list(range(2, pairs))
    half = len(late) // 2
    rest = len(late) - half
    levels = ep_size.bit_length() - 1
    tie = lax.optimization_barrier

    def cut(array, start, count):
        return lax.slice_in_dim(array, start * rows, (start + count) * rows, axis=0)

    def bare(array):
        return array[:, :columns]

    def page_take(page, swapped, level):
        bit = jnp.bitwise_and(jnp.right_shift(mask_value, level), 1) == 1
        return jnp.where(bit, swapped, page)

    def page_hop(page, level):
        return page_take(page, flip(page, "ep", 1 << level), level)

    def page_far(page):
        for level in range(levels - 1, 2, -1):
            page = page_hop(page, level)
        return flip(page, "ep", 4) if levels > 2 else page, page

    own, both, page = pick(
        ranks, swap_slot, expert_ids, gate_weights, hidden, cache_pages, groups
    )
    late_pieces = [flip(own, "ep", 2 * m) for m in late]
    near_2 = flip(own, "ep", 2)
    both_1 = flip(both, "ep", 1)

    (w_gate,) = load(w_gate)
    near_2, w_gate, w_up = tie((near_2, w_gate, w_up))
    far_2 = flip(bare(near_2), "tp", 2)
    near_3 = flip(near_2, "ep", 1)
    (w_up,) = load(w_up)
    far_2, near_3, w_gate, w_up, page, *late_pieces = tie(
        (far_2, near_3, w_gate, w_up, page, *late_pieces)
    )
    near_late = jnp.concatenate(late_pieces, axis=0)
    far_3 = flip(jnp.concatenate([bare(near_3), bare(near_late)], axis=0), "tp", 2)
    near_odds = flip(near_late, "ep", 1)
    wide = jnp.pad(far_2, ((0, 0), (0, near_2.shape[1] - columns)))
    core_23 = flip(jnp.concatenate([near_2, near_3, wide], axis=0), "tp", 1)
    core_1 = flip(both_1, "tp", 1)
    queries, core_1, core_23 = tie((queries, core_1, core_23))
    count = queries.shape[0]
    some, middle = count // 4, count * 5 // 8
    attended = attend_part(ranks, lengths, queries, cache_pages, groups, 0, some)
    least = page.shape[0] // 4
    upper, lower = jnp.split(page, [least], axis=0)
    swapped, upper = page_far(upper)
    far_3, near_late, near_odds, attended, swapped = tie(
        (far_3, near_late, near_odds, attended, swapped)
    )
    upper = page_take(upper, swapped, 2) if levels > 2 else upper
    page = jnp.concatenate([upper, lower], axis=0)
    core_3 = flip(far_3, "tp", 1)
    far_late, core_late = cut(far_3, 1, len(late)), cut(core_3, 1, len(late))
    far_3, core_3 = cut(far_3, 0, 1), cut(core_3, 0, 1)
    far_odds = flip(bare(near_odds), "tp", 2)

    def piece(start, part, array):
        return start * rows, (part,), part == 0, array

    pieces = [(0, None, False, hidden), (0, (), True, own)]
    pieces += [(rows, (0, 2), True, both_1), (rows, (1, 3), False, core_1)]
    pieces += [piece(2, 0, near_2), piece(3, 0, near_3), piece(2, 1, cut(core_23, 0, 2))]
    pieces += [piece(2, 2, far_2), piece(2, 3, bare(cut(core_23, 2, 1)))]
    pieces += [piece(3, 2, far_3), piece(3, 3, core_3)]
    *first, w_down = run_experts(
        ranks, pieces, w_gate, w_up, w_down, 4 * rows, columns, top, True, 1
    )
    near_both = jnp.concatenate([near_late, near_odds], axis=0)
    early = flip(near_both, "tp", 1)
    swapped = flip(page, "ep", 1)
    first, far_odds, early, swapped = tie((first, far_odds, early, swapped))
    page = page_take(page, swapped, 0)

    (given,), own = first
    sent, kept = jnp.split(total_of(own, flip(given, "tp", 1)), 2, axis=0)
    last = flip(far_odds, "tp", 1)
    over_23 = flip(cut(sent, 2, 2), "tp", 2)
    over_1 = flip(jnp.concatenate([cut(kept, 1, 1), cut(sent, 1, 1)], axis=1), "ep", 1)
    swapped = flip(page, "ep", 2)
    odds = len(late)
    pieces = [piece(0, 0, near_both), (0, (1,), False, early)]
    pieces += [piece(0, 2, far_late), piece(0, 3, core_late)]
    pieces += [piece(odds, 2, far_odds), piece(odds, 3, last)]
    second = [
        *run_experts(
            ranks, pieces, w_gate, w_up, w_down, 2 * len(late) * rows, columns, top, False, 2
        )
    ]
    second, over_23, over_1, swapped = tie((second, over_23, over_1, swapped))
    page = page_take(page, swapped, 1)
    upper, lower = jnp.split(page, [least], axis=0)
    swapped, lower = page_far(lower)
    (cross, side), own = second
    late_sent, late_kept = jnp.split(own, 2, axis=0)
    late_sent = total_of(late_sent, flip(cross, "tp", 1))
    over_3 = flip(total_of(cut(kept, 3, 1), cut(over_23, 1, 1)), "ep", 1)
    zero = flip(total_of(cut(sent, 0, 1), over_1[:, columns:]), "tp", 2)
    late_sent, side, queries = tie((late_sent, side, queries))
    side = flip(side, "tp", 1)

    over_y = flip(cut(late_sent, len(late), half), "tp", 2)
    over_x = flip(cut(late_sent, len(late) + half, rest), "ep", 1)
    over_y, over_x, over_3, side, queries = tie((over_y, over_x, over_3, side, queries))
    late_kept = total_of(late_kept, side)
    odd = total_of(
        cut(late_kept, len(late), len(late)), jnp.pad(over_y, ((0, rest * rows), (0, 0)))
    )
    odd = flip(odd, "ep", 1)
    even = total_of(cut(late_sent, 0, len(late)), jnp.pad(over_x, ((half * rows, 0), (0, 0))))
    even = flip(even, "tp", 2)
    attended = attend_part(
        ranks, lengths, queries, cache_pages, groups, some, middle - some, attended
    )
    odd, even, attended, swapped = tie((odd, even, attended, swapped))
    lower = page_take(lower, swapped, 2) if levels > 2 else lower
    page = jnp.concatenate([upper, lower], axis=0)
    even = total_of(cut(late_kept, 0, len(late)), even, odd)
    back = [flip(cut(even, i, 1), "ep", 2 * m) for i, m in enumerate(late)]
    back.append(flip(total_of(cut(kept, 2, 1), cut(over_23, 0, 1), over_3), "ep", 2))
    attended = attend_rest(
        ranks,
        lengths,
        swap_slot,
        swap_mask,
        queries,
        cache_pages,
        page,
        attended,
        groups,
        middle,
    )
    *back, attended = tie((*back, attended))
    moe_out = total_of(cut(kept, 0, 1), over_1[:, :columns], zero, *back)
    return attended, moe_out


def solution(mesh):
    in_specs = (
        P(("ep", "tp"), None, None),
        P(("ep", "tp"), None, None),
        P(),
        P(),
        P(),
        P("ep", None),
        P("ep", None),
        P("ep", None),
        P("ep", None, "tp"),
        P("ep", None, "tp"),
        P("ep", "tp", None),
    )
    out_specs = (P(("ep", "tp"), None, None), P("ep", "tp"))
    return jax.shard_map(local, mesh=mesh, in_specs=in_specs, out_specs=out_specs, check_vma=False)
```

```python
import functools
import math

import jax
import jax.numpy as jnp
from jax import lax
from jax.experimental import pallas as pl
from jax.experimental.pallas import tpu as pltpu
from jax.sharding import PartitionSpec as P

LAT = 512
SCORE_SCALE = 192.0 ** (-0.5)
MASK_FLOOR = -1e30
ROWS = 512
MIB = 1 << 20


def flip(block, axis, apart):
    count = lax.axis_size(axis)
    return lax.ppermute(block, axis, [(i, i ^ apart) for i in range(count)])


def attend_body(query, page, length):
    scores = (
        lax.dot_general(query, page, (((0,), (0,)), ((), ())), preferred_element_type=jnp.float32)
        * SCORE_SCALE
    )
    live = lax.broadcasted_iota(jnp.int32, scores.shape, 1) < length
    scores = jnp.where(live, scores, MASK_FLOOR)
    top = jnp.max(scores, axis=1, keepdims=True)
    weight = jnp.where(live, jnp.exp(scores - top), 0.0)
    total = jnp.sum(weight, axis=1, keepdims=True)
    blended = lax.dot_general(
        weight.astype(jnp.bfloat16),
        page[:LAT],
        (((1,), (1,)), ((), ())),
        preferred_element_type=jnp.float32,
    )
    return (blended / total).astype(jnp.bfloat16)


def in_hbm(array):
    return pltpu.with_memory_space_constraint(array, pltpu.HBM)


def in_vmem(array):
    return pltpu.with_memory_space_constraint(array, pltpu.VMEM)


ANYWHERE = pl.BlockSpec(memory_space=pl.ANY)
IN_VMEM = pl.BlockSpec(memory_space=pltpu.VMEM)
IN_SMEM = pl.BlockSpec(memory_space=pltpu.SMEM)


def device_of(ranks_ref, groups, mask=0):
    return (ranks_ref[0] ^ mask) * groups + ranks_ref[1]


def pick_kernel(groups, ranks_ref, slots_ref, ids_ref, gates_ref, hidden_ref, pages_ref, near_ref, both_ref, page_ref, sems):
    rows = hidden_ref.shape[0]
    columns = hidden_ref.shape[1] // groups

    def quarter(part):
        start = pl.multiple_of((ranks_ref[1] ^ part) * columns, 128)
        return hidden_ref.at[:, pl.ds(start, columns)]

    copies = [
        (quarter(0), near_ref.at[:, pl.ds(0, columns)]),
        (quarter(0), both_ref.at[:, pl.ds(0, columns)]),
        (quarter(2), both_ref.at[:, pl.ds(columns, columns)]),
        (pages_ref.at[slots_ref[device_of(ranks_ref, groups)]], page_ref),
    ]
    copies = [pltpu.make_async_copy(*pair, sems.at[i]) for i, pair in enumerate(copies)]
    for one in copies:
        one.start()
    gates = gates_ref[...]
    high = gates.astype(jnp.bfloat16).astype(jnp.float32)
    middle = (gates - high).astype(jnp.bfloat16).astype(jnp.float32)
    low = gates - high - middle
    top = gates.shape[0]
    table = jnp.concatenate(
        [ids_ref[...].astype(jnp.float32), high, middle, low, jnp.zeros((128 - 4 * top, rows), jnp.float32)],
        axis=0,
    )
    table = jnp.concatenate([table, jnp.zeros((128, 128 - rows), jnp.float32)], axis=1)
    table = table.T[:rows].astype(jnp.bfloat16)
    near_ref[:, columns:] = table
    both_ref[:, 2 * columns :] = table
    for one in copies:
        one.wait()


def pick(ranks, swap_slot, expert_ids, gate_weights, hidden, pages, groups):
    rows, width = hidden.shape
    columns = width // groups
    return pl.pallas_call(
        functools.partial(pick_kernel, groups),
        out_shape=(
            pltpu.VMEM((rows, columns + 128), jnp.bfloat16),
            pltpu.VMEM((rows, 2 * columns + 128), jnp.bfloat16),
            pltpu.VMEM(pages.shape[1:], jnp.bfloat16),
        ),
        in_specs=[IN_SMEM, IN_SMEM, IN_VMEM, IN_VMEM, ANYWHERE, ANYWHERE],
        out_specs=(IN_VMEM, IN_VMEM, IN_VMEM),
        scratch_shapes=[pltpu.SemaphoreType.DMA((4,))],
        compiler_params=pltpu.CompilerParams(vmem_limit_bytes=2 * MIB),
        name="pick",
    )(
        ranks,
        in_hbm(swap_slot),
        in_hbm(expert_ids.T),
        in_hbm(gate_weights.T),
        in_hbm(hidden),
        in_hbm(pages),
    )


def attend_part(ranks, lengths, queries, pages, groups, first, some, before=None):
    count, width, heads = queries.shape
    slots = pages.shape[2]
    each = math.gcd(some, 2)
    skip = first // each

    def kernel(ranks_ref, lengths_ref, query_ref, page_ref, *refs):
        start = device_of(ranks_ref, groups) * count + first + pl.program_id(0) * each
        for i in range(each):
            refs[-1][i] = attend_body(query_ref[i], page_ref[i], lengths_ref[start + i])

    earlier = [] if before is None else [before]
    return pl.pallas_call(
        kernel,
        out_shape=jax.ShapeDtypeStruct((count, heads, LAT), jnp.bfloat16),
        grid_spec=pltpu.PrefetchScalarGridSpec(
            num_scalar_prefetch=2,
            grid=(some // each,),
            in_specs=[
                pl.BlockSpec((each, width, heads), lambda i, *_: (skip + i, 0, 0)),
                pl.BlockSpec((each, width, slots), lambda i, *_: (skip + i, 0, 0)),
            ]
            + [ANYWHERE] * len(earlier),
            out_specs=pl.BlockSpec((each, heads, LAT), lambda i, *_: (skip + i, 0, 0)),
        ),
        input_output_aliases={4: 0} if earlier else {},
        compiler_params=pltpu.CompilerParams(vmem_limit_bytes=8 * MIB),
        cost_estimate=pl.CostEstimate(flops=0, bytes_accessed=0, transcendentals=0),
        name="attend_local",
    )(ranks, lengths, in_hbm(queries), in_hbm(pages), *earlier)


def load_kernel(*refs):
    count = len(refs) // 2
    copies = [
        pltpu.make_async_copy(refs[i], refs[count + i], refs[-1].at[i]) for i in range(count)
    ]
    for one in copies:
        one.start()
    for one in copies:
        one.wait()


def load(*arrays):
    return pl.pallas_call(
        load_kernel,
        out_shape=[pltpu.VMEM(w.shape, w.dtype) for w in arrays],
        in_specs=[ANYWHERE] * len(arrays),
        out_specs=[ANYWHERE] * len(arrays),
        scratch_shapes=[pltpu.SemaphoreType.DMA((len(arrays),))],
        compiler_params=pltpu.CompilerParams(vmem_limit_bytes=MIB),
        cost_estimate=pl.CostEstimate(
            flops=0, bytes_accessed=sum(2 * math.prod(w.shape) for w in arrays), transcendentals=0
        ),
        name="load",
    )(*[in_hbm(w) for w in arrays])


def attend_rest(
    ranks, lengths, swap_slot, swap_mask, queries, pages, page, attended, groups, first
):
    count, width, heads = queries.shape
    slots = pages.shape[2]
    each = 2
    steps = (count - first) // each
    skip = first // each

    def kernel(
        ranks_ref,
        lengths_ref,
        slots_ref,
        mask_ref,
        query_ref,
        pages_ref,
        page_ref,
        old_ref,
        out_ref,
    ):
        step = pl.program_id(0)
        device = device_of(ranks_ref, groups)
        partner = device_of(ranks_ref, groups, mask_ref[0])
        mine = slots_ref[device]
        far_length = lengths_ref[partner * count + slots_ref[partner]]

        @pl.when(step < steps)
        def _():
            for i in range(each):
                at = device * count + first + step * each + i
                out_ref[i] = attend_body(query_ref[i], pages_ref[i], lengths_ref[at])

        @pl.when(step == steps)
        def _():
            for i in range(each):
                at = mine // each * each + i
                traded = at == mine
                page = jnp.where(traded, page_ref[...], pages_ref[i])
                length = jnp.where(traded, far_length, lengths_ref[device * count + at])
                out_ref[i] = attend_body(query_ref[i], page, length)

    def request(i, ranks_ref, lengths_ref, slots_ref, mask_ref):
        mine = slots_ref[device_of(ranks_ref, groups)]
        return jnp.where(i < steps, skip + i, mine // each), 0, 0

    return pl.pallas_call(
        kernel,
        out_shape=jax.ShapeDtypeStruct(attended.shape, attended.dtype),
        grid_spec=pltpu.PrefetchScalarGridSpec(
            num_scalar_prefetch=4,
            grid=(steps + 1,),
            in_specs=[
                pl.BlockSpec((each, width, heads), request),
                pl.BlockSpec((each, width, slots), request),
                pl.BlockSpec((width, slots), lambda i, *_: (0, 0)),
                ANYWHERE,
            ],
            out_specs=pl.BlockSpec((each, heads, LAT), request),
        ),
        input_output_aliases={7: 0},
        compiler_params=pltpu.CompilerParams(vmem_limit_bytes=8 * MIB),
        cost_estimate=pl.CostEstimate(
            flops=2 * heads * slots * (width + LAT),
            bytes_accessed=2 * (heads * (width + LAT) + slots * width),
            transcendentals=heads * slots,
        ),
        name="attend_rest",
    )(
        ranks,
        lengths,
        swap_slot,
        swap_mask,
        in_hbm(queries),
        in_hbm(pages),
        page,
        attended,
    )


def experts_kernel(
    top,
    fetch,
    ranks_ref,
    pieces,
    gate_ref,
    up_ref,
    source_ref,
    given,
    kept_ref,
    *refs,
):
    if fetch:
        down_ref, *refs = refs
    else:
        down_ref = source_ref
    rows_ref, meta_ref, inner_ref, table_ref, sems, down_sem = refs
    experts, _, units = gate_ref.shape
    total_rows = rows_ref.shape[0]
    quarter = kept_ref.shape[1]
    ep_rank, tp_rank = ranks_ref[0], ranks_ref[1]

    def columns_of(part):
        return pl.ds(pl.multiple_of((tp_rank ^ part) * quarter, 128), quarter)

    copies = []
    for start, parts, has_meta, piece in pieces:
        rows = pl.ds(start, piece.shape[0])
        if parts is None:
            copies.append((piece, rows_ref.at[rows, :]))
            continue
        for i, part in enumerate(parts):
            copies.append(
                (piece.at[:, pl.ds(i * quarter, quarter)], rows_ref.at[rows, columns_of(part)])
            )
        if has_meta:
            copies.append((piece.at[:, pl.ds(piece.shape[1] - 128, 128)], meta_ref.at[rows, :]))
    copies = [
        pltpu.make_async_copy(source, target, sems.at[i])
        for i, (source, target) in enumerate(copies)
    ]
    for one in copies:
        one.start()
    if fetch:
        down_copy = pltpu.make_async_copy(source_ref, down_ref, down_sem)
        down_copy.start()
    for one in copies:
        one.wait()
    meta = meta_ref[...].astype(jnp.float32)
    gates = sum(pltpu.roll(meta, 128 - i * top, 1) for i in range(1, 4))
    lane = lax.broadcasted_iota(jnp.int32, meta.shape, 1)
    for e in range(experts):
        name = (ep_rank * experts + e).astype(jnp.float32)
        mine = jnp.where((lane < top) & (meta == name), gates, 0.0)
        table_ref[:, e : e + 1] = jnp.sum(mine, axis=1, keepdims=True)
    stride = math.gcd(total_rows, ROWS)
    for e in range(experts):

        @pl.loop(0, total_rows // stride)
        def _(step):
            at = pl.ds(pl.multiple_of(step * stride, stride), stride)
            rows = rows_ref[at, :]
            gate = jnp.dot(rows, gate_ref[e], preferred_element_type=jnp.float32)
            up = jnp.dot(rows, up_ref[e], preferred_element_type=jnp.float32)
            act = gate / (1.0 + jnp.exp(-gate)) * up * table_ref[at, e : e + 1]
            inner_ref[at, e * units : (e + 1) * units] = act.astype(jnp.bfloat16)

    if fetch:
        down_copy.wait()
    last = len(given) - 1
    for part, out_ref, half in (
        (3, given[0], 0),
        (1, given[last], 1 - last),
        (2, kept_ref, 0),
        (0, kept_ref, 1),
    ):

        @pl.loop(0, total_rows // stride)
        def _(step):
            at = pl.ds(pl.multiple_of(step * stride, stride), stride)
            to = pl.ds(pl.multiple_of(half * total_rows + step * stride, stride), stride)
            weight = down_ref[:, :, columns_of(part)].reshape(experts * units, quarter)
            out_ref[to, :] = jnp.dot(
                inner_ref[at, :], weight, preferred_element_type=jnp.float32
            ).astype(jnp.bfloat16)


def run_experts(ranks, pieces, w_gate, w_up, w_down, rows, columns, top, fetch, given):
    experts, width, units = w_gate.shape
    arrays = [piece for *_, piece in pieces]
    count = sum(1 if parts is None else len(parts) + has_meta for _, parts, has_meta, _ in pieces)

    def kernel(ranks_ref, refs, *others):
        named = [(*about[:3], ref) for about, ref in zip(pieces, refs)]
        experts_kernel(top, fetch, ranks_ref, named, *others)

    need = 2 * rows * (width + 128 + experts * units) + 512 * rows
    down_shape = [pltpu.VMEM(w_down.shape, w_down.dtype)] if fetch else []
    return pl.pallas_call(
        kernel,
        out_shape=[
            [pltpu.VMEM((2 * rows // given, columns), jnp.bfloat16)] * given,
            pltpu.VMEM((2 * rows, columns), jnp.bfloat16),
        ]
        + down_shape,
        in_specs=[
            IN_SMEM,
            [ANYWHERE] * len(arrays),
            IN_VMEM,
            IN_VMEM,
            ANYWHERE if fetch else IN_VMEM,
        ],
        out_specs=[[IN_VMEM] * given, IN_VMEM] + [IN_VMEM] * len(down_shape),
        scratch_shapes=[
            pltpu.VMEM((rows, width), jnp.bfloat16),
            pltpu.VMEM((rows, 128), jnp.bfloat16),
            pltpu.VMEM((rows, experts * units), jnp.bfloat16),
            pltpu.VMEM((rows, 128), jnp.float32),
            pltpu.SemaphoreType.DMA((count,)),
            pltpu.SemaphoreType.DMA,
        ],
        compiler_params=pltpu.CompilerParams(vmem_limit_bytes=need + 6 * MIB),
        cost_estimate=pl.CostEstimate(
            flops=0,
            bytes_accessed=0,
            transcendentals=0,
        ),
        name="experts",
    )(
        ranks,
        arrays,
        in_vmem(w_gate),
        in_vmem(w_up),
        in_hbm(w_down) if fetch else in_vmem(w_down),
    )


def total_of(*terms):
    value = terms[0].astype(jnp.float32)
    for term in terms[1:]:
        value = value + term.astype(jnp.float32)
    return value.astype(jnp.bfloat16)


def local(
    cache_pages,
    queries,
    lengths,
    swap_slot,
    swap_mask,
    hidden,
    expert_ids,
    gate_weights,
    w_gate,
    w_up,
    w_down,
):
    groups = lax.axis_size("tp")
    ep_size = lax.axis_size("ep")
    ranks = jnp.stack([lax.axis_index("ep"), lax.axis_index("tp")]).astype(jnp.int32)
    mask_value = swap_mask[0]
    columns = hidden.shape[1] // groups
    top = expert_ids.shape[1]
    cache_pages = jnp.swapaxes(cache_pages, 1, 2)
    queries = jnp.swapaxes(queries, 1, 2)

    rows = hidden.shape[0]
    pairs = ep_size // 2
    late = list(range(2, pairs))
    half = len(late) // 2
    rest = len(late) - half
    levels = ep_size.bit_length() - 1
    tie = lax.optimization_barrier

    def cut(array, start, count):
        return lax.slice_in_dim(array, start * rows, (start + count) * rows, axis=0)

    def bare(array):
        return array[:, :columns]

    def page_take(page, swapped, level):
        bit = jnp.bitwise_and(jnp.right_shift(mask_value, level), 1) == 1
        return jnp.where(bit, swapped, page)

    def page_hop(page, level):
        return page_take(page, flip(page, "ep", 1 << level), level)

    def page_far(page):
        for level in range(levels - 1, 2, -1):
            page = page_hop(page, level)
        return flip(page, "ep", 4) if levels > 2 else page, page

    own, both, page = pick(
        ranks, swap_slot, expert_ids, gate_weights, hidden, cache_pages, groups
    )
    late_pieces = [flip(own, "ep", 2 * m) for m in late]
    near_2 = flip(own, "ep", 2)
    both_1 = flip(both, "ep", 1)

    (w_gate,) = load(w_gate)
    near_2, w_gate, w_up = tie((near_2, w_gate, w_up))
    far_2 = flip(bare(near_2), "tp", 2)
    near_3 = flip(near_2, "ep", 1)
    (w_up,) = load(w_up)
    far_2, near_3, w_gate, w_up, page, *late_pieces = tie(
        (far_2, near_3, w_gate, w_up, page, *late_pieces)
    )
    near_late = jnp.concatenate(late_pieces, axis=0)
    far_3 = flip(jnp.concatenate([bare(near_3), bare(near_late)], axis=0), "tp", 2)
    near_odds = flip(near_late, "ep", 1)
    wide = jnp.pad(far_2, ((0, 0), (0, near_2.shape[1] - columns)))
    core_23 = flip(jnp.concatenate([near_2, near_3, wide], axis=0), "tp", 1)
    core_1 = flip(both_1, "tp", 1)
    queries, core_1, core_23 = tie((queries, core_1, core_23))
    count = queries.shape[0]
    some, middle = count // 4, count // 2
    attended = attend_part(ranks, lengths, queries, cache_pages, groups, 0, some)
    least = page.shape[0] // 4
    upper, lower = jnp.split(page, [least], axis=0)
    swapped, upper = page_far(upper)
    far_3, near_late, near_odds, attended, swapped = tie(
        (far_3, near_late, near_odds, attended, swapped)
    )
    upper = page_take(upper, swapped, 2) if levels > 2 else upper
    page = jnp.concatenate([upper, lower], axis=0)
    core_3 = flip(far_3, "tp", 1)
    far_late, core_late = cut(far_3, 1, len(late)), cut(core_3, 1, len(late))
    far_3, core_3 = cut(far_3, 0, 1), cut(core_3, 0, 1)
    far_odds = flip(bare(near_odds), "tp", 2)

    def piece(start, part, array):
        return start * rows, (part,), part == 0, array

    pieces = [(0, None, False, hidden), (0, (), True, own)]
    pieces += [(rows, (0, 2), True, both_1), (rows, (1, 3), False, core_1)]
    pieces += [piece(2, 0, near_2), piece(3, 0, near_3), piece(2, 1, cut(core_23, 0, 2))]
    pieces += [piece(2, 2, far_2), piece(2, 3, bare(cut(core_23, 2, 1)))]
    pieces += [piece(3, 2, far_3), piece(3, 3, core_3)]
    *first, w_down = run_experts(
        ranks, pieces, w_gate, w_up, w_down, 4 * rows, columns, top, True, 1
    )
    near_both = jnp.concatenate([near_late, near_odds], axis=0)
    early = flip(near_both, "tp", 1)
    swapped = flip(page, "ep", 1)
    first, far_odds, early, swapped = tie((first, far_odds, early, swapped))
    page = page_take(page, swapped, 0)

    (given,), own = first
    sent, kept = jnp.split(total_of(own, flip(given, "tp", 1)), 2, axis=0)
    last = flip(far_odds, "tp", 1)
    over_23 = flip(cut(sent, 2, 2), "tp", 2)
    over_1 = flip(jnp.concatenate([cut(kept, 1, 1), cut(sent, 1, 1)], axis=1), "ep", 1)
    swapped = flip(page, "ep", 2)
    odds = len(late)
    pieces = [piece(0, 0, near_both), (0, (1,), False, early)]
    pieces += [piece(0, 2, far_late), piece(0, 3, core_late)]
    pieces += [piece(odds, 2, far_odds), piece(odds, 3, last)]
    second = [
        *run_experts(
            ranks, pieces, w_gate, w_up, w_down, 2 * len(late) * rows, columns, top, False, 2
        )
    ]
    second, over_23, over_1, swapped = tie((second, over_23, over_1, swapped))
    page = page_take(page, swapped, 1)
    upper, lower = jnp.split(page, [least], axis=0)
    swapped, lower = page_far(lower)
    (cross, side), own = second
    late_sent, late_kept = jnp.split(own, 2, axis=0)
    late_sent = total_of(late_sent, flip(cross, "tp", 1))
    over_3 = flip(total_of(cut(kept, 3, 1), cut(over_23, 1, 1)), "ep", 1)
    zero = flip(total_of(cut(sent, 0, 1), over_1[:, columns:]), "tp", 2)
    late_sent, side, queries = tie((late_sent, side, queries))
    side = flip(side, "tp", 1)

    over_y = flip(cut(late_sent, len(late), half), "tp", 2)
    over_x = flip(cut(late_sent, len(late) + half, rest), "ep", 1)
    over_y, over_x, over_3, side, queries = tie((over_y, over_x, over_3, side, queries))
    late_kept = total_of(late_kept, side)
    odd = total_of(
        cut(late_kept, len(late), len(late)), jnp.pad(over_y, ((0, rest * rows), (0, 0)))
    )
    odd = flip(odd, "ep", 1)
    even = total_of(cut(late_sent, 0, len(late)), jnp.pad(over_x, ((half * rows, 0), (0, 0))))
    even = flip(even, "tp", 2)
    attended = attend_part(
        ranks, lengths, queries, cache_pages, groups, some, middle - some, attended
    )
    odd, even, attended, swapped = tie((odd, even, attended, swapped))
    lower = page_take(lower, swapped, 2) if levels > 2 else lower
    page = jnp.concatenate([upper, lower], axis=0)
    even = total_of(cut(late_kept, 0, len(late)), even, odd)
    back = [flip(cut(even, i, 1), "ep", 2 * m) for i, m in enumerate(late)]
    back.append(flip(total_of(cut(kept, 2, 1), cut(over_23, 0, 1), over_3), "ep", 2))
    attended = attend_rest(
        ranks,
        lengths,
        swap_slot,
        swap_mask,
        queries,
        cache_pages,
        page,
        attended,
        groups,
        middle,
    )
    *back, attended = tie((*back, attended))
    moe_out = total_of(cut(kept, 0, 1), over_1[:, :columns], zero, *back)
    return attended, moe_out


def solution(mesh):
    in_specs = (
        P(("ep", "tp"), None, None),
        P(("ep", "tp"), None, None),
        P(),
        P(),
        P(),
        P("ep", None),
        P("ep", None),
        P("ep", None),
        P("ep", None, "tp"),
        P("ep", None, "tp"),
        P("ep", "tp", None),
    )
    out_specs = (P(("ep", "tp"), None, None), P("ep", "tp"))
    return jax.shard_map(local, mesh=mesh, in_specs=in_specs, out_specs=out_specs, check_vma=False)
```
